32 devices in a mesh: dp: 8 (over z, core), tensor: 4 (over y, x).
Axes of the slice: x: 2, y: 2, z: 4, core: 2. Of those that a mesh axis runs over, the one named last changes fastest.
Arguments:
- tokens: bfloat16 [4096, 2048], P('dp'), may hold values from -6 to 6
- cotangent: bfloat16 [4096, 2048], P('dp'), may hold values from -6 to 6
- routes: int32 [4096, 8], P('dp'), may hold values from 0 to 15, all different within a row; in each aligned block of 256 rows (0 to 255, 256 to 511, ...) at most 176 rows name the same one
- wq: bfloat16 [2048, 2048], P('dp', 'tensor'), may hold values from -0.125 to 0.125
- wk: bfloat16 [2048, 2048], P('dp', 'tensor'), may hold values from -0.125 to 0.125
- wv: bfloat16 [2048, 2048], P('dp', 'tensor'), may hold values from -0.125 to 0.125
- wo: bfloat16 [2048, 2048], P('tensor', 'dp'), may hold values from -0.5 to 0.5
- attn_gain: bfloat16 [2048], P('dp'), may hold values from 0.5 to 1.5
- q_gain: bfloat16 [2048], P('tensor'), may hold values from 0.5 to 1.5
- k_gain: bfloat16 [2048], P('tensor'), may hold values from 0.5 to 1.5
- moe_gain: bfloat16 [2048], P('dp'), may hold values from 0.5 to 1.5
- router: bfloat16 [2048, 16], P('dp'), may hold values from -0.0625 to 0.0625
- w_gate: bfloat16 [16, 2048, 1024], P(None, 'dp', 'tensor'), may hold values from -0.125 to 0.125
- w_up: bfloat16 [16, 2048, 1024], P(None, 'dp', 'tensor'), may hold values from -0.125 to 0.125
- w_down: bfloat16 [16, 1024, 2048], P(None, 'tensor', 'dp'), may hold values from -1.5 to 1.5
Outputs:
- mixed: bfloat16 [4096, 2048], P('dp')
- tokens_grad: bfloat16 [4096, 2048], P('dp')
- wq_grad: float32 [2048, 2048], P('dp', 'tensor')
- wk_grad: float32 [2048, 2048], P('dp', 'tensor')
- wv_grad: float32 [2048, 2048], P('dp', 'tensor')
- wo_grad: float32 [2048, 2048], P('tensor', 'dp')
- attn_gain_grad: float32 [2048], P('dp')
- q_gain_grad: float32 [2048], P('tensor')
- k_gain_grad: float32 [2048], P('tensor')
- moe_gain_grad: float32 [2048], P('dp')
- router_grad: float32 [2048, 16], P('dp')
- w_gate_grad: float32 [16, 2048, 1024], P(None, 'dp', 'tensor')
- w_up_grad: float32 [16, 2048, 1024], P(None, 'dp', 'tensor')
- w_down_grad: float32 [16, 1024, 2048], P(None, 'tensor', 'dp')
The draws below stay inside these ranges and needn't reach their ends.
Inputs may be any that keep to these rules, and one draw needn't show every extreme that they name: `routes`: each row names 8 different experts; within each aligned block of 256 rows no expert is named by more than 176 rows, a bound that some block reaches.
All inputs are finite; a program needn't handle non-finite values.
Results may differ from the reference program's by a relative error of at most 0.024.
Values may be sent and summed in bfloat16 or wider, within the bound.
No kernel may reach another device: no remote copies, remote signals or barrier semaphores. Data moves between devices by JAX's collectives and lax.ppermute only.
A program may use at most 320 MiB of HBM per device.

```python
import math
import jax
import jax.numpy as jnp
import numpy as np
from jax import lax

D = 2048
HEADS = 16
HEAD_DIM = 128
FF = 1024
TOPK = 8
EXPERTS = 16
MB = 2
MB_TOK = 256
MOST = 176
TOKENS = 4096


def level_of(rng, shape, cuts, smallest, top_value):
    def one(position, blocks):
        steps = jax.random.uniform(jax.random.fold_in(jax.random.fold_in(rng, 6), position), (blocks,), jnp.float32, smallest / len(cuts), top_value / len(cuts))
        return jnp.repeat(jnp.exp(steps), shape[position] // blocks).reshape((-1,) + (1,) * (len(shape) - position - 1))

    factor_of = one(*cuts[0])
    for cut in cuts[1:]:
        factor_of = factor_of * one(*cut)
    return factor_of


def routed_block(stream_key, own, number, rows, count, top, most, slope):
    ranking = jax.random.permutation(stream_key, count)
    packed, ordinary = portions_of(count, rows * top, most, slope, True), portions_of(count, rows * top, most, slope, False)
    places = jnp.arange(count)

    def named(tallies, turn):
        used = int((tallies > 0).sum())
        fixed = max(1, used // 4)
        passed = fixed + (places - fixed + turn * (used - fixed)) % max(1, count - fixed)
        return jnp.zeros((count,), jnp.int32).at[ranking[jnp.where(places < fixed, places, passed)]].set(jnp.asarray(tallies, jnp.int32))

    tallies = jnp.where(number % 4 == 0, named(packed, number // 4), named(ordinary, number - number // 4 - 1))
    mixed = jax.random.permutation(jax.random.fold_in(own, 3), count)
    donor, sink = mixed[0:count // 2 * 2:2], mixed[1:count // 2 * 2:2]
    margin = jnp.minimum(tallies[donor] - 1, most - tallies[sink]) // 2
    margin = jnp.where((donor == ranking[0]) | (sink == ranking[0]) | (tallies[sink] == 0), 0, jnp.maximum(margin, 0))
    passed = jax.random.randint(jax.random.fold_in(own, 4), (count // 2,), 0, 1 << 20) % (margin + 1)
    tallies = tallies.at[donor].add(-passed).at[sink].add(passed)
    items = jnp.searchsorted(jnp.cumsum(tallies), jnp.arange(rows * top), side="right").astype(jnp.int32)
    grid = items.reshape(top, rows).T
    grid = grid[jax.random.permutation(jax.random.fold_in(own, 1), rows)]
    turn = jax.random.randint(jax.random.fold_in(own, 2), (rows, 1), 0, top)
    return jnp.take_along_axis(grid, (jnp.arange(top)[None, :] + turn) % top, axis=1)


def portions_of(amount, total, bound, slope, full):
    loads = [(1 << 20) // math.isqrt(rank ** slope) + 1 for rank in range(1, amount + 1)]
    largest = bound if full else min(bound, max(-(-total // amount), total * loads[0] // sum(loads)))
    least = 1 if total - largest >= amount - 1 else 0
    given, spare = [largest] + [least] * (amount - 1), total - largest - least * (amount - 1)
    while spare > 0:
        candidates = [i for i in range(1, amount) if given[i] < largest] or [i for i in range(1, amount) if given[i] < bound]
        mass, remaining = sum([loads[i] for i in candidates]), spare
        for i in candidates:
            addition = min(bound - given[i], max(1, remaining * loads[i] // mass), spare)
            given[i] = given[i] + addition
            spare = spare - addition
    return np.array(given)


def gaussian(rng, shape, width, limit, shards=(), held_as=jnp.bfloat16):
    level = level_of(rng, shape, shards, -0.22, 0.18) if shards else 1.0
    drawn = jax.random.normal(rng, shape, jnp.float32) * width * level
    return jnp.minimum(jnp.maximum(drawn, -limit), limit).astype(held_as)


def setup_inputs(seed: int = 0) -> dict:
    arg_keys = jax.random.split(jax.random.key(seed), 16)
    tokens = gaussian(arg_keys[0], (TOKENS, D), 1.0, 6.0, ((0, 8),))
    cotangent = gaussian(arg_keys[1], (TOKENS, D), 1.0, 6.0, ((0, 8),))
    routes_keys = jax.random.split(jax.random.fold_in(arg_keys[2], 1), TOKENS // MB_TOK)
    routes_turns = jax.random.permutation(jax.random.fold_in(arg_keys[2], 3), TOKENS // MB_TOK)
    routes = jax.vmap(lambda own, number: routed_block(jax.random.fold_in(arg_keys[2], 2), own, number, MB_TOK, EXPERTS, TOPK, MOST, 1))(routes_keys, routes_turns).reshape((TOKENS, TOPK))
    wq = gaussian(arg_keys[3], (D, D), D ** -0.5, 0.125, ((0, 8), (1, 4)))
    wk = gaussian(arg_keys[4], (D, D), D ** -0.5, 0.125, ((0, 8), (1, 4)))
    wv = gaussian(arg_keys[5], (D, D), D ** -0.5, 0.125, ((0, 8), (1, 4)))
    wo = gaussian(arg_keys[6], (D, D), (D // 16) ** -0.5, 0.5, ((0, 4), (1, 8)))
    attn_gain = jnp.clip(1.0 + 0.1 * jax.random.normal(arg_keys[7], (D,), jnp.float32), 0.5, 1.5).astype(jnp.bfloat16)
    q_gain = jnp.clip(1.0 + 0.1 * jax.random.normal(arg_keys[8], (D,), jnp.float32), 0.5, 1.5).astype(jnp.bfloat16)
    k_gain = jnp.clip(1.0 + 0.1 * jax.random.normal(arg_keys[9], (D,), jnp.float32), 0.5, 1.5).astype(jnp.bfloat16)
    moe_gain = jnp.clip(1.0 + 0.1 * jax.random.normal(arg_keys[10], (D,), jnp.float32), 0.5, 1.5).astype(jnp.bfloat16)
    router = gaussian(arg_keys[11], (D, EXPERTS), (4 * D) ** -0.5, 0.0625, ((0, 8),))
    w_gate = gaussian(arg_keys[12], (EXPERTS, D, FF), D ** -0.5, 0.125, ((1, 8), (2, 4)))
    w_up = gaussian(arg_keys[13], (EXPERTS, D, FF), D ** -0.5, 0.125, ((1, 8), (2, 4)))
    w_down = gaussian(arg_keys[14], (EXPERTS, FF, D), (max(1, FF // 64)) ** -0.5, 1.5, ((1, 4), (2, 8)))
    return dict(tokens=tokens, cotangent=cotangent, routes=routes, wq=wq, wk=wk, wv=wv, wo=wo, attn_gain=attn_gain, q_gain=q_gain, k_gain=k_gain, moe_gain=moe_gain, router=router, w_gate=w_gate, w_up=w_up, w_down=w_down)


EPS = 1e-05
THETA = 10000.0
HIGH = lax.Precision.HIGHEST

@jax.custom_vjp
def low(v):
    return lax.optimization_barrier(v.astype(jnp.bfloat16)).astype(jnp.float32)

@jax.custom_vjp
def low_back(v):
    return v

def low_keep(v):
    return (low(v), None)

def low_pass(kept, grad):
    return (grad,)

def back_keep(v):
    return (v, None)

def back_low(kept, grad):
    return (low(grad),)
low.defvjp(low_keep, low_pass)
low_back.defvjp(back_keep, back_low)

def norm_scale(value, gain):
    return value * lax.rsqrt(lax.optimization_barrier(jnp.mean(value * value, axis=-1, keepdims=True)) + EPS) * gain

def rope_tables(length, head_dim):
    half = head_dim // 2
    freq = THETA ** (-(jnp.arange(half).astype(jnp.float32) * 2.0 / head_dim))
    angle = jnp.arange(length).astype(jnp.float32)[:, None] * freq[None, :]
    cosine = jnp.concatenate([jnp.cos(angle), jnp.cos(angle)], -1)
    sine = jnp.concatenate([jnp.sin(angle), jnp.sin(angle)], -1)
    return (cosine, sine)

def rotate(value, cosine, sine):
    half = value.shape[-1] // 2
    turned = jnp.concatenate([-value[..., half:], value[..., :half]], -1)
    return value * cosine[:, None, :] + turned * sine[:, None, :]

def dispatch(route_block, experts, most):
    count = route_block.shape[0] * route_block.shape[1]
    flat = route_block.reshape(count).astype(jnp.int32)
    onehot = (flat[:, None] == jnp.arange(experts).astype(jnp.int32)[None, :]).astype(jnp.int32)
    before = jnp.cumsum(onehot, axis=0) - onehot
    slot = lax.optimization_barrier(jnp.sum(before * onehot, axis=1))
    dest = (flat * most + slot).astype(jnp.int32)
    owner = jnp.zeros((experts * most,), jnp.int32).at[dest].set((jnp.arange(count) // route_block.shape[1]).astype(jnp.int32))
    filled = jnp.zeros((experts * most,), jnp.int32).at[dest].set(1)
    return (dest, owner, filled)

def layer(routes, xf, wq, wk, wv, wo, attn_gain, q_gain, k_gain, moe_gain, router, w_gate, w_up, w_down):
    seq = MB * MB_TOK
    total = xf.shape[0]
    nseq = total // seq
    a = low(norm_scale(xf, attn_gain))
    q = low_back(jnp.dot(a, wq, precision=HIGH))
    k = low_back(jnp.dot(a, wk, precision=HIGH))
    v = low_back(jnp.dot(a, wv, precision=HIGH))
    qn = norm_scale(q, q_gain).reshape(nseq, seq, HEADS, HEAD_DIM)
    kn = norm_scale(k, k_gain).reshape(nseq, seq, HEADS, HEAD_DIM)
    cosine, sine = rope_tables(seq, HEAD_DIM)
    qr = low(rotate(qn, cosine, sine))
    kr = low(rotate(kn, cosine, sine))
    vb = low(v).reshape(nseq, seq, HEADS, HEAD_DIM)
    scale = HEAD_DIM ** (-0.5)
    causal = jnp.arange(seq)[:, None] >= jnp.arange(seq)[None, :]

    def attend(pieces):
        queries, keys, values = pieces
        scores = low_back(scale * jnp.einsum('qhd,khd->hqk', queries, keys, precision=HIGH))
        scores = jnp.where(causal[None], scores, -1e+30)
        probs_att = jax.nn.softmax(scores, axis=-1)
        return jnp.einsum('hqk,khd->qhd', low(probs_att), values, precision=HIGH)
    heads_out = lax.map(jax.checkpoint(attend), (qr, kr, vb))
    joined = low(low_back(heads_out.reshape(total, D)))
    attn = low_back(jnp.dot(joined, wo, precision=HIGH))
    resid = xf + attn
    m = low(norm_scale(resid, moe_gain))
    probs = jax.nn.softmax(jnp.dot(m, router, precision=HIGH), axis=-1)
    gates = jnp.take_along_axis(probs, routes, axis=1)
    nblock = total // MB_TOK

    def expert_block(pieces):
        m_block, gate_block, route_block = pieces
        dest, owner, filled = dispatch(route_block, EXPERTS, MOST)
        slots = jnp.where(filled[:, None] > 0, m_block[owner], 0.0).reshape(EXPERTS, MOST, D)
        gate_act = low_back(jnp.einsum('ecd,edf->ecf', slots, w_gate, precision=HIGH))
        up_act = low_back(jnp.einsum('ecd,edf->ecf', slots, w_up, precision=HIGH))
        hidden = low(jax.nn.silu(gate_act) * up_act)
        expert_out = low_back(jnp.einsum('ecf,efd->ecd', hidden, w_down, precision=HIGH))
        picked = expert_out.reshape(EXPERTS * MOST, D)[dest].reshape(MB_TOK, TOPK, D)
        return lax.optimization_barrier(jnp.sum(gate_block[:, :, None] * picked, axis=1))
    moe = lax.map(jax.checkpoint(expert_block), (m.reshape(nblock, MB_TOK, D), gates.reshape(nblock, MB_TOK, TOPK), routes.reshape(nblock, MB_TOK, TOPK)))
    return resid + moe.reshape(total, D)

def reference(tokens, cotangent, routes, wq, wk, wv, wo, attn_gain, q_gain, k_gain, moe_gain, router, w_gate, w_up, w_down):
    floats = [item.astype(jnp.float32) for item in (tokens, wq, wk, wv, wo, attn_gain, q_gain, k_gain, moe_gain, router, w_gate, w_up, w_down)]
    mixed, pullback = jax.vjp(lambda *items: layer(routes, *items), *floats)
    grads = pullback(cotangent.astype(jnp.float32))
    return (mixed.astype(jnp.bfloat16), grads[0].astype(jnp.bfloat16), grads[1], grads[2], grads[3], grads[4], grads[5], grads[6], grads[7], grads[8], grads[9], grads[10], grads[11], grads[12])
```

```python
import jax
import jax.numpy as jnp
from jax import lax
from jax.sharding import Mesh
from jax.sharding import PartitionSpec as P

HEAD_DIM = 128
EXPERTS = 16

EPS = 1e-05
THETA = 10000.0
HIGH = lax.Precision.HIGHEST
f32 = jnp.float32
bf16 = jnp.bfloat16


def swap(value, axis, mask):
    if mask == 0:
        return value
    n = lax.axis_size(axis)
    return lax.ppermute(value, axis, [(i, i ^ mask) for i in range(n)])


def tensor_sum(value):
    n = lax.axis_size("tensor")
    parts = [value] + [swap(value, "tensor", k) for k in range(1, n)]
    while len(parts) > 1:
        parts = [parts[i] + parts[i + 1] for i in range(0, len(parts), 2)]
    return parts[0]


def rope_tables(length, head_dim):
    half = head_dim // 2
    freq = THETA ** (-(jnp.arange(half).astype(f32) * 2.0 / head_dim))
    angle = jnp.arange(length).astype(f32)[:, None] * freq[None, :]
    cosine = jnp.concatenate([jnp.cos(angle), jnp.cos(angle)], -1)
    sine = jnp.concatenate([jnp.sin(angle), jnp.sin(angle)], -1)
    return (cosine, sine)


def rotate(value, cosine, sine):
    half = value.shape[-1] // 2
    turned = jnp.concatenate([-value[..., half:], value[..., :half]], -1)
    return value * cosine[:, None, :] + turned * sine[:, None, :]


def unrotate(grad, cosine, sine):
    half = grad.shape[-1] // 2
    scaled = grad * sine[:, None, :]
    back_turn = jnp.concatenate([scaled[..., half:], -scaled[..., :half]], -1)
    return grad * cosine[:, None, :] + back_turn


def columns(value, index, size):
    return lax.dynamic_slice_in_dim(value, index * size, size, 1)


def spread_z(value):
    return jnp.stack([swap(value, "z", k) for k in range(lax.axis_size("z"))])


def gather_quarters(value):
    me, n = lax.axis_index("tensor"), lax.axis_size("tensor")
    rows, width = value.shape
    half = rows // 2
    if n != 4:
        out = jnp.zeros((rows, n * width), value.dtype)
        for k in range(n):
            part = swap(value, "tensor", k)
            out = lax.dynamic_update_slice(out, part, (0, (me ^ k) * width))
        return out
    near = swap(value, "tensor", 1)
    far = swap(value, "tensor", 2)
    cross = jnp.concatenate([swap(near[:half], "tensor", 2), swap(far[half:], "tensor", 1)], 0)
    out = jnp.zeros((rows, 4 * width), value.dtype)
    for k, part in enumerate((value, near, far, cross)):
        out = lax.dynamic_update_slice(out, part, (0, (me ^ k) * width))
    return out


def scatter_quarters(value):
    me, n = lax.axis_index("tensor"), lax.axis_size("tensor")
    rows, width = value.shape[0], value.shape[1] // n
    half = rows // 2
    if n != 4:
        got = [swap(columns(value, me ^ k, width), "tensor", k).astype(f32) for k in range(n)]
        return sum(got[1:], got[0])
    outs = []
    for part, first, second in ((value[:half], 1, 2), (value[half:], 2, 1)):
        pick = lambda k: columns(part, me ^ k, width)
        sent = jnp.stack([pick(first), pick(first ^ second)])
        got = swap(sent, "tensor", first).astype(f32)
        mine = pick(0).astype(f32) + got[0]
        other = (pick(second).astype(f32) + got[1]).astype(bf16)
        outs.append(mine + swap(other, "tensor", second).astype(f32))
    return jnp.concatenate(outs, 0)


def shards(
    tokens,
    cotangent,
    routes,
    wq,
    wk,
    wv,
    wo,
    attn_gain,
    q_gain,
    k_gain,
    moe_gain,
    router,
    w_gate,
    w_up,
    w_down,
):
    nz = lax.axis_size("z")
    me_t = lax.axis_index("tensor")
    me_z = lax.axis_index("z")
    me_c = lax.axis_index("core")
    dp = ("z", "core")
    seq, width = tokens.shape
    quarter = width // lax.axis_size("tensor")
    local = wq.shape[1]
    local_heads = local // HEAD_DIM
    slice_d = wq.shape[0]
    own_e = EXPERTS // nz
    hid = w_gate.shape[2]

    small = jnp.concatenate([attn_gain[:, None], moe_gain[:, None], router], 1)
    pad = -small.shape[1] % 128
    small = jnp.pad(small, ((0, 0), (0, pad)))
    packed = lax.all_gather(jnp.concatenate([wq, wk, wv, small], 1), dp, axis=0, tiled=True)
    wqkv_full = packed[:, : 3 * local]
    a_gain = packed[:, 3 * local].astype(f32)
    m_gain = packed[:, 3 * local + 1].astype(f32)
    router_full = packed[:, 3 * local + 2 : 3 * local + 2 + EXPERTS]
    wo_full = lax.all_gather(wo, dp, axis=1, tiled=True)

    stacked = jnp.stack([w_gate, w_up, w_down.transpose(0, 1, 2)])

    def experts_of(z):
        return lax.dynamic_slice_in_dim(stacked, z * own_e, own_e, 1)

    parts_w = jnp.stack([swap(experts_of(me_z ^ k), "z", k) for k in range(nz)])
    both_w = (parts_w, swap(parts_w, "core", 1))
    gate_full = jnp.zeros((width, own_e, hid), bf16)
    up_full = jnp.zeros((width, own_e, hid), bf16)
    down_full = jnp.zeros((own_e, hid, width), bf16)
    for c in range(2):
        for k in range(nz):
            at = ((me_z ^ k) * 2 + (me_c ^ c)) * slice_d
            piece = both_w[c][k]
            gate_full = lax.dynamic_update_slice(
                gate_full, piece[0].transpose(1, 0, 2), (at, 0, 0)
            )
            up_full = lax.dynamic_update_slice(up_full, piece[1].transpose(1, 0, 2), (at, 0, 0))
            down_full = lax.dynamic_update_slice(down_full, piece[2], (0, 0, at))
    gate_full = gate_full.reshape(width, own_e * hid)
    up_full = up_full.reshape(width, own_e * hid)
    down_full = down_full.reshape(own_e * hid, width)

    cot_all = gather_quarters(
        spread_z(columns(cotangent, me_t, quarter)).reshape(nz * seq, quarter)
    )
    mask = jnp.sum(
        (routes[:, :, None] == jnp.arange(EXPERTS)[None, None, :]).astype(bf16), 1
    )
    mask_all = spread_z(mask.T).transpose(0, 2, 1).reshape(nz * seq, EXPERTS).astype(f32)

    xf = tokens.astype(f32)
    rate_x = lax.rsqrt(jnp.mean(xf * xf, -1, keepdims=True) + EPS)
    gain_q = q_gain.astype(f32)
    gain_k = k_gain.astype(f32)
    a_low = (xf * rate_x * a_gain).astype(bf16)
    qkv = jnp.dot(a_low, wqkv_full, preferred_element_type=f32)
    query, keyed, valued = qkv[:, :local], qkv[:, local : 2 * local], qkv[:, 2 * local :]
    sums = tensor_sum(jnp.stack([jnp.sum(query * query, -1), jnp.sum(keyed * keyed, -1)]))
    rate_q = lax.rsqrt(sums[0] / width + EPS)[:, None]
    rate_k = lax.rsqrt(sums[1] / width + EPS)[:, None]
    cosine, sine = rope_tables(seq, HEAD_DIM)
    heads = (seq, local_heads, HEAD_DIM)
    q_rot = rotate((query * rate_q * gain_q).reshape(heads), cosine, sine).astype(bf16)
    k_rot = rotate((keyed * rate_k * gain_k).reshape(heads), cosine, sine).astype(bf16)
    v_low = valued.reshape(heads).astype(bf16)
    scale = HEAD_DIM ** (-0.5)
    scores = scale * jnp.einsum("qhd,khd->hqk", q_rot, k_rot, preferred_element_type=f32)
    causal = jnp.arange(seq)[:, None] >= jnp.arange(seq)[None, :]
    scores = jnp.where(causal[None], scores, -1e30)
    peak = jnp.max(scores, -1, keepdims=True)
    expd = jnp.exp(scores - peak)
    weights = expd / jnp.sum(expd, -1, keepdims=True)
    weights_low = weights.astype(bf16)
    outputs = jnp.einsum("hqk,khd->qhd", weights_low, v_low, preferred_element_type=f32)
    joined = outputs.reshape(seq, local).astype(bf16)
    attn = jnp.dot(joined, wo_full, preferred_element_type=f32)

    x_own = columns(xf, me_t, quarter)
    resid = x_own + scatter_quarters(attn.astype(bf16))
    rate_r = lax.rsqrt(tensor_sum(jnp.sum(resid * resid, -1)) / width + EPS)[:, None]
    gain_own = lax.dynamic_slice_in_dim(m_gain, me_t * quarter, quarter, 0)
    m_own = (resid * rate_r * gain_own).astype(bf16)

    m_all = gather_quarters(spread_z(m_own).reshape(nz * seq, quarter))
    logits = jnp.dot(m_all, router_full, preferred_element_type=f32)
    probs_all = jax.nn.softmax(logits, axis=-1)
    gates_all = lax.dynamic_slice_in_dim(probs_all * mask_all, me_z * own_e, own_e, 1)
    tall = (nz * seq, own_e, hid)
    wide = (nz * seq, own_e * hid)
    gate_b = jnp.broadcast_to(gates_all[:, :, None], tall).reshape(wide)
    gate_act = jnp.dot(m_all, gate_full, preferred_element_type=f32)
    up_act = jnp.dot(m_all, up_full, preferred_element_type=f32)
    dhid_raw = jnp.einsum("td,fd->tf", cot_all, down_full, preferred_element_type=f32)
    sigma = jax.nn.sigmoid(gate_act)
    silu_gate = gate_act * sigma
    hidden = silu_gate * up_act
    hidden_low = (gate_b * hidden).astype(bf16)
    dgate_part = jnp.sum((hidden * dhid_raw).reshape(tall), -1)
    dhid = gate_b * dhid_raw
    dgate_act = (dhid * up_act * sigma * (1.0 + gate_act * (1.0 - sigma))).astype(bf16)
    dup_act = (dhid * silu_gate).astype(bf16)
    dm_part = (
        jnp.einsum("tf,df->td", dgate_act, gate_full, preferred_element_type=f32)
        + jnp.einsum("tf,df->td", dup_act, up_full, preferred_element_type=f32)
    ).astype(bf16)
    moe_part = jnp.dot(hidden_low, down_full, preferred_element_type=f32).astype(bf16)

    def to_owner(part):
        sums = scatter_quarters(part).astype(bf16).reshape(nz, seq, quarter)
        got = [swap(sums[k], "z", k).astype(f32) for k in range(nz)]
        return sum(got[1:], got[0])

    dm_own = to_owner(dm_part)
    moe_own = to_owner(moe_part)
    mixed = gather_quarters((resid + moe_own).astype(bf16))

    dg = dgate_part.reshape(nz, seq, own_e).transpose(0, 2, 1)
    dgate = jnp.zeros((EXPERTS, seq), f32)
    for k in range(nz):
        dgate = lax.dynamic_update_slice(dgate, swap(dg[k], "z", k), ((me_z ^ k) * own_e, 0))
    dgate = tensor_sum(dgate).T
    probs = probs_all[:seq]
    dprobs = dgate * mask.astype(f32)
    dlogits = probs * (dprobs - jnp.sum(probs * dprobs, -1, keepdims=True))
    router_own = lax.dynamic_slice_in_dim(router_full, me_t * quarter, quarter, 0)
    router_part = jnp.dot(m_own.astype(f32).T, dlogits, precision=HIGH)
    dm_own = dm_own + jnp.dot(dlogits, router_own.astype(f32).T, precision=HIGH)

    gate_grad = jnp.einsum("td,tf->df", m_all, dgate_act, preferred_element_type=f32)
    up_grad = jnp.einsum("td,tf->df", m_all, dup_act, preferred_element_type=f32)
    down_grad = jnp.einsum("tf,td->fd", hidden_low, cot_all, preferred_element_type=f32)
    cut = (nz, 2, slice_d, own_e, hid)
    grads = jnp.stack(
        [
            gate_grad.reshape(cut).transpose(1, 0, 3, 2, 4),
            up_grad.reshape(cut).transpose(1, 0, 3, 2, 4),
            down_grad.reshape(own_e, hid, nz, 2, slice_d).transpose(3, 2, 0, 1, 4),
        ],
        2,
    )
    keep = lax.dynamic_index_in_dim(grads, me_c, 0, keepdims=False)
    give = lax.dynamic_index_in_dim(grads, me_c ^ 1, 0, keepdims=False).astype(bf16)
    summed = (keep + swap(give, "core", 1).astype(f32)).astype(bf16)
    expert_grads = jnp.zeros((3, EXPERTS, slice_d, hid), f32)
    for k in range(nz):
        sent = lax.dynamic_index_in_dim(summed, me_z ^ k, 0, keepdims=False)
        expert_grads = lax.dynamic_update_slice(
            expert_grads, swap(sent, "z", k).astype(f32), (0, (me_z ^ k) * own_e, 0, 0)
        )

    normed = resid * rate_r
    moe_gain_part = jnp.sum(dm_own * normed, 0)
    pulled = dm_own * gain_own
    inner_r = tensor_sum(jnp.sum(pulled * normed, -1))[:, None] / width
    cot_own = columns(cotangent, me_t, quarter).astype(f32)
    dresid = cot_own + rate_r * (pulled - normed * inner_r)
    dresid_low = gather_quarters(dresid.astype(bf16))

    wo_grad = jnp.einsum("sa,sd->ad", joined, dresid_low, preferred_element_type=f32)
    dout = (
        jnp.einsum("sd,ad->sa", dresid_low, wo_full, preferred_element_type=f32)
        .astype(bf16)
        .reshape(heads)
    )
    dweights = jnp.einsum("qhd,khd->hqk", dout, v_low, preferred_element_type=f32)
    dv = jnp.einsum("hqk,qhd->khd", weights_low, dout, preferred_element_type=f32)
    inner = jnp.sum(weights * dweights, -1, keepdims=True)
    dscores = (weights * (dweights - inner)).astype(bf16)
    dq_rot = scale * jnp.einsum("hqk,khd->qhd", dscores, k_rot, preferred_element_type=f32)
    dk_rot = scale * jnp.einsum("hqk,qhd->khd", dscores, q_rot, preferred_element_type=f32)
    dq_norm = unrotate(dq_rot, cosine, sine).reshape(seq, local)
    dk_norm = unrotate(dk_rot, cosine, sine).reshape(seq, local)
    inners = tensor_sum(
        jnp.stack(
            [jnp.sum(dq_norm * gain_q * query, -1), jnp.sum(dk_norm * gain_k * keyed, -1)]
        )
    )
    dq_low = (rate_q * gain_q * dq_norm - query * rate_q**3 * inners[0][:, None] / width).astype(
        bf16
    )
    dk_low = (rate_k * gain_k * dk_norm - keyed * rate_k**3 * inners[1][:, None] / width).astype(
        bf16
    )
    dv_low = dv.reshape(seq, local).astype(bf16)
    q_gain_part = jnp.sum(dq_norm * query * rate_q, 0)
    k_gain_part = jnp.sum(dk_norm * keyed * rate_k, 0)
    dqkv = jnp.concatenate([dq_low, dk_low, dv_low], 1)
    wqkv_grad = jnp.einsum("sd,sa->da", a_low, dqkv, preferred_element_type=f32).astype(bf16)
    da_part = jnp.einsum("sa,da->sd", dqkv, wqkv_full, preferred_element_type=f32)
    da_own = scatter_quarters(da_part.astype(bf16))
    norm_x = x_own * rate_x
    attn_gain_part = jnp.sum(da_own * norm_x, 0)
    pulled_x = da_own * lax.dynamic_slice_in_dim(a_gain, me_t * quarter, quarter, 0)
    inner_x = tensor_sum(jnp.sum(pulled_x * norm_x, -1))[:, None] / width
    tokens_grad = gather_quarters(
        (dresid + rate_x * (pulled_x - norm_x * inner_x)).astype(bf16)
    )

    wqkv_own = lax.psum_scatter(wqkv_grad, dp, scatter_dimension=0, tiled=True).astype(f32)
    wo_own = lax.psum_scatter(wo_grad.astype(bf16), dp, scatter_dimension=1, tiled=True).astype(f32)
    q_gain_grad, k_gain_grad = lax.psum((q_gain_part, k_gain_part), dp)
    smalls = jnp.concatenate([attn_gain_part[None], moe_gain_part[None], router_part.T], 0)
    smalls = lax.all_gather(smalls, "tensor", axis=1, tiled=True)
    smalls = lax.psum_scatter(smalls, dp, scatter_dimension=1, tiled=True)
    return (
        mixed,
        tokens_grad,
        wqkv_own[:, :local],
        wqkv_own[:, local : 2 * local],
        wqkv_own[:, 2 * local :],
        wo_own,
        smalls[0],
        q_gain_grad,
        k_gain_grad,
        smalls[1],
        smalls[2:].T,
        expert_grads[0],
        expert_grads[1],
        expert_grads[2],
    )


def solution(mesh):
    fine = Mesh(
        mesh.devices.reshape(mesh.shape["dp"] // 2, 2, mesh.shape["tensor"]),
        ("z", "core", "tensor"),
    )
    dp = ("z", "core")
    in_specs = (
        P(dp, None),
        P(dp, None),
        P(dp, None),
        P(dp, "tensor"),
        P(dp, "tensor"),
        P(dp, "tensor"),
        P("tensor", dp),
        P(dp),
        P("tensor"),
        P("tensor"),
        P(dp),
        P(dp, None),
        P(None, dp, "tensor"),
        P(None, dp, "tensor"),
        P(None, "tensor", dp),
    )
    out_specs = (
        P(dp, None),
        P(dp, None),
        P(dp, "tensor"),
        P(dp, "tensor"),
        P(dp, "tensor"),
        P("tensor", dp),
        P(dp),
        P("tensor"),
        P("tensor"),
        P(dp),
        P(dp, None),
        P(None, dp, "tensor"),
        P(None, dp, "tensor"),
        P(None, "tensor", dp),
    )
    return jax.shard_map(shards, mesh=fine, in_specs=in_specs, out_specs=out_specs, check_vma=False)
```

```python
import functools

import jax
import jax.numpy as jnp
from jax import lax
from jax.experimental import pallas as pl
from jax.experimental.pallas import tpu as pltpu
from jax.sharding import Mesh
from jax.sharding import PartitionSpec as P

HEAD_DIM = 128
EXPERTS = 16
LANES = 128
FIRST = 2

EPS = 1e-05
THETA = 10000.0
HIGH = lax.Precision.HIGHEST
f32 = jnp.float32
bf16 = jnp.bfloat16
MIB = 1 << 20


def after(value, *earlier):
    return lax.optimization_barrier((value, *earlier))[0]


def fence(*values):
    return lax.optimization_barrier(values)


def swap(value, axis, mask):
    if mask == 0:
        return value
    n = lax.axis_size(axis)
    return lax.ppermute(value, axis, [(i, i ^ mask) for i in range(n)])


def bits_of(axis):
    n = lax.axis_size(axis)
    return [1 << b for b in range(n.bit_length() - 1)]


def butterfly_sum(value, axes):
    for axis in axes:
        for bit in bits_of(axis):
            value = value + swap(value, axis, bit)
    return value


def tensor_sum(value):
    return butterfly_sum(value, ("tensor",))


def rope_tables(length, head_dim):
    half = head_dim // 2
    freq = THETA ** (-(jnp.arange(half).astype(f32) * 2.0 / head_dim))
    angle = jnp.arange(length).astype(f32)[:, None] * freq[None, :]
    cosine = jnp.concatenate([jnp.cos(angle), jnp.cos(angle)], -1)
    sine = jnp.concatenate([jnp.sin(angle), jnp.sin(angle)], -1)
    return (cosine, sine)


def rotate(value, cosine, sine):
    half = value.shape[-1] // 2
    turned = jnp.concatenate([-value[..., half:], value[..., :half]], -1)
    return value * cosine[:, None, :] + turned * sine[:, None, :]


def unrotate(grad, cosine, sine):
    half = grad.shape[-1] // 2
    scaled = grad * sine[:, None, :]
    back_turn = jnp.concatenate([scaled[..., half:], -scaled[..., :half]], -1)
    return grad * cosine[:, None, :] + back_turn


def columns(value, index, size):
    return lax.dynamic_slice_in_dim(value, index * size, size, 1)


def spread_z(value):
    parts = {0: value}
    for bit in reversed(bits_of("z")):
        parts.update({k ^ bit: swap(v, "z", bit) for k, v in parts.items()})
    return [parts[k] for k in range(len(parts))]


def spread_tensor_near(value):
    n = lax.axis_size("tensor")
    return [swap(value, "tensor", k) for k in ((1, 2) if n == 4 else range(1, n))]


def spread_tensor_far(value, near):
    if lax.axis_size("tensor") != 4:
        return jnp.stack([value, *near])
    half = value.shape[0] // 2
    cross = [swap(near[0][:half], "tensor", 2), swap(near[1][half:], "tensor", 1)]
    return jnp.stack([value, *near, jnp.concatenate(cross, 0)])


def spread_tensor(value):
    return spread_tensor_far(value, spread_tensor_near(value))


def gather_tensor(value):
    me, n = lax.axis_index("tensor"), lax.axis_size("tensor")
    rows, width = value.shape
    out = jnp.zeros((rows, n * width), value.dtype)
    parts = spread_tensor(value)
    for k in range(n):
        part = parts[k]
        out = lax.dynamic_update_slice(out, part, (0, (me ^ k) * width))
    return out


def order_of(n, odd):
    if n != 4:
        return tuple(range(n))
    return (0, 1, 2, 3) if odd else (0, 2, 1, 3)


def scatter_first(block, odd):
    n = block.shape[0]
    if n != 4:
        return jnp.stack([swap(block[k], "tensor", k) for k in range(1, n)])
    return swap(block[2:], "tensor", 2 if odd else 1)


def scatter_second(block, got, odd):
    got = got.astype(f32)
    mine = block[0].astype(f32)
    if block.shape[0] != 4:
        return mine + jnp.sum(got, 0), None
    other = (block[1].astype(f32) + got[1]).astype(bf16)
    return mine + got[0], swap(other, "tensor", 1 if odd else 2)


def scatter_third(mine, got):
    return mine if got is None else mine + got.astype(f32)


def scatter_z_near(parts):
    return swap(jnp.stack([parts[k].astype(bf16) for k in sorted(parts)]), "z", 1)


def scatter_z_far(parts, got):
    parts = {k: parts[k] + got[i].astype(f32) for i, k in enumerate(sorted(parts))}
    for bit in bits_of("z")[1:]:
        away = sorted(k for k in parts if k & bit)
        got = swap(jnp.stack([parts[k].astype(bf16) for k in away]), "z", bit)
        parts = {k ^ bit: parts[k ^ bit] + got[i].astype(f32) for i, k in enumerate(away)}
    return parts[0]


def scatter_columns(value):
    me, n = lax.axis_index("tensor"), lax.axis_size("tensor")
    rows, width = value.shape[0], value.shape[1] // n
    half = rows // 2
    outs = []
    for odd in (0, 1):
        part = value[odd * half : (odd + 1) * half]
        block = jnp.stack([columns(part, me ^ k, width) for k in order_of(n, odd)])
        outs.append(scatter_third(*scatter_second(block, scatter_first(block, odd), odd)))
    return jnp.concatenate(outs, 0)


def dot_nn(a, b):
    return lax.dot_general(a, b, (((1,), (0,)), ((), ())), preferred_element_type=f32)


def dot_nt(a, b):
    return lax.dot_general(a, b, (((1,), (1,)), ((), ())), preferred_element_type=f32)


def dot_tn(a, b):
    return lax.dot_general(a, b, (((0,), (0,)), ((), ())), preferred_element_type=f32)


def load_weights(nz, slice_d, me_z, me_c, pairs, sems, along_last):
    copies = []
    for w, (parts, whole) in enumerate(pairs):
        for c in range(2):
            for k in range(nz):
                j = c * nz + k
                at = pl.ds(pl.multiple_of((me_c ^ c) * slice_d, slice_d), slice_d)
                target = (
                    whole.at[me_z ^ k, :, :, at] if along_last[w] else whole.at[me_z ^ k, :, at, :]
                )
                copies.append(pltpu.make_async_copy(parts[c].at[k], target, sems.at[w, j]))
    for copy in copies:
        copy.start()
    for copy in copies:
        copy.wait()


def own_gate(gates, lane, me_z, own_e, e):
    return jnp.sum(jnp.where(lane == FIRST + me_z * own_e + e, gates, 0.0), -1, keepdims=True)


def forward_kernel(nz, n, own_e, hid, slice_d, idx, *refs):
    m_ref, mask_ref, router_ref = refs[:3]
    act_ref, up_ref, hid_ref, probs_ref, w_gate, w_up, sems = refs[7:]
    me_z, me_c, me_t = idx[0], idx[1], idx[2]

    @pl.when(pl.program_id(0) == 0)
    def _():
        pairs = ((refs[3:5], w_gate), (refs[5:7], w_up))
        load_weights(nz, slice_d, me_z, me_c, pairs, sems, (False, False))

    rows = m_ref.shape[1]
    lane = lax.broadcasted_iota(jnp.int32, (rows, LANES), 1)
    logits = jnp.zeros((rows, LANES), f32)
    for k in range(n):
        logits += dot_nn(m_ref[k], router_ref[me_t ^ k])
    named = (lane >= FIRST) & (lane < FIRST + EXPERTS)
    logits = jnp.where(named, logits, -1e30)
    expd = jnp.where(named, jnp.exp(logits - jnp.max(logits, -1, keepdims=True)), 0.0)
    probs = expd / jnp.sum(expd, -1, keepdims=True)
    probs_ref[...] = probs
    gates = probs * mask_ref[...]
    for e in range(own_e):
        gate = own_gate(gates, lane, me_z, own_e, e)
        act = jnp.zeros((rows, hid), f32)
        up = jnp.zeros((rows, hid), f32)
        for k in range(n):
            act += dot_nn(m_ref[k], w_gate[me_t ^ k, e])
            up += dot_nn(m_ref[k], w_up[me_t ^ k, e])
        at = pl.ds(e * hid, hid)
        act_ref[:, at] = act
        up_ref[:, at] = up
        hid_ref[:, at] = (gate * (act * jax.nn.sigmoid(act) * up)).astype(bf16)


def forward_call(idx, m_all, mask_all, router_q, gate_parts, up_parts, nz):
    n, tokens, quarter = m_all.shape
    seq = tokens // nz
    own_e, slice_d, hid = up_parts[0].shape[1:]
    wide = own_e * hid
    here = lambda i, idx: (i, 0)
    return pl.pallas_call(
        functools.partial(forward_kernel, nz, n, own_e, hid, slice_d),
        grid_spec=pltpu.PrefetchScalarGridSpec(
            num_scalar_prefetch=1,
            grid=(nz,),
            in_specs=[
                pl.BlockSpec((n, seq, quarter), lambda i, idx: (0, i, 0)),
                pl.BlockSpec((seq, LANES), here),
                pl.BlockSpec((n, quarter, LANES), lambda i, idx: (0, 0, 0)),
            ]
            + [pl.BlockSpec(memory_space=pl.ANY)] * 4,
            out_specs=[
                pl.BlockSpec((seq, wide), here),
                pl.BlockSpec((seq, wide), here),
                pl.BlockSpec((seq, wide), here),
                pl.BlockSpec((seq, LANES), here),
            ],
            scratch_shapes=[
                pltpu.VMEM((n, own_e, quarter, hid), bf16),
                pltpu.VMEM((n, own_e, quarter, hid), bf16),
                pltpu.SemaphoreType.DMA((2, 2 * nz)),
            ],
        ),
        out_shape=[
            jax.ShapeDtypeStruct((tokens, wide), f32),
            jax.ShapeDtypeStruct((tokens, wide), f32),
            jax.ShapeDtypeStruct((tokens, wide), bf16),
            jax.ShapeDtypeStruct((tokens, LANES), f32),
        ],
        compiler_params=pltpu.CompilerParams(vmem_limit_bytes=52 * MIB),
        cost_estimate=pl.CostEstimate(
            flops=4 * tokens * n * quarter * wide, bytes_accessed=40 * MIB, transcendentals=0
        ),
    )(idx, m_all, mask_all, router_q, *gate_parts, *up_parts)


def backward_kernel(nz, n, own_e, hid, slice_d, quarter, idx, *refs):
    g_ref, act_ref, up_ref, probs_ref, mask_ref = refs[:5]
    dx_ref, dg_ref, du_ref, w_gate, w_up, w_down, sems = refs[11:]
    i = pl.program_id(0)
    me_z, me_c, me_t = idx[0], idx[1], idx[2]

    @pl.when(i == 0)
    def _():
        pairs = ((refs[5:7], w_gate), (refs[7:9], w_up), (refs[9:11], w_down))
        load_weights(nz, slice_d, me_z, me_c, pairs, sems, (False, False, True))

    rows = act_ref.shape[0]
    lane = lax.broadcasted_iota(jnp.int32, (rows, LANES), 1)
    gates = probs_ref[...] * mask_ref[...]
    dgate = jnp.zeros((rows, LANES), f32)
    for e in range(own_e):
        gate = own_gate(gates, lane, me_z, own_e, e)
        at = pl.ds(e * hid, hid)
        back = jnp.zeros((rows, hid), f32)
        for q in range(n):
            back += dot_nt(g_ref[q, 0], w_down[q, e])
        act = act_ref[:, at]
        up = up_ref[:, at]
        sigma = jax.nn.sigmoid(act)
        silu = act * sigma
        dgate = jnp.where(lane == me_z * own_e + e, jnp.sum(silu * up * back, -1, keepdims=True), dgate)
        back = gate * back
        dg_ref[:, at] = (back * up * sigma * (1.0 + act * (1.0 - sigma))).astype(bf16)
        du_ref[:, at] = (back * silu).astype(bf16)
    dgate = jnp.transpose(dgate)[:EXPERTS].astype(bf16)
    even, odd = order_of(n, 0), order_of(n, 1)
    for j in range(n):
        q = me_t ^ jnp.where(i % 2 == 0, even[j], odd[j])
        total = jnp.zeros((rows, quarter), f32)
        for e in range(own_e):
            at = pl.ds(e * hid, hid)
            total += dot_nt(dg_ref[:, at], w_gate[q, e])
            total += dot_nt(du_ref[:, at], w_up[q, e])
        dx_ref[0, j, pl.ds(0, rows), :] = total.astype(bf16)
        for h in range(rows // quarter):
            dx_ref[0, j, pl.ds(rows + h * EXPERTS, EXPERTS), :] = dgate[
                :, h * quarter : (h + 1) * quarter
            ]


def backward_call(idx, first, g_all, act, up, probs, mask_all, weights):
    n, nz, seq, quarter = g_all.shape
    own_e, slice_d, hid = weights[0].shape[1:]
    blocks = nz // 2
    wide = own_e * hid
    tall = seq + EXPERTS * (seq // quarter)
    some = lambda i, idx: (2 * i + first, 0)
    here = lambda i, idx: (i, 0)
    hbm = pl.BlockSpec(memory_space=pl.ANY)
    return pl.pallas_call(
        functools.partial(backward_kernel, nz, n, own_e, hid, slice_d, quarter),
        grid_spec=pltpu.PrefetchScalarGridSpec(
            num_scalar_prefetch=1,
            grid=(blocks,),
            in_specs=[
                pl.BlockSpec((n, 1, seq, quarter), lambda i, idx: (0, 2 * i + first, 0, 0)),
                pl.BlockSpec((seq, wide), some),
                pl.BlockSpec((seq, wide), some),
                pl.BlockSpec((seq, LANES), some),
                pl.BlockSpec((seq, LANES), some),
            ]
            + [hbm] * 6,
            out_specs=[
                pl.BlockSpec((1, n, tall, quarter), lambda i, idx: (i, 0, 0, 0)),
                pl.BlockSpec((seq, wide), here),
                pl.BlockSpec((seq, wide), here),
            ],
            scratch_shapes=[
                pltpu.VMEM((n, own_e, quarter, hid), bf16),
                pltpu.VMEM((n, own_e, quarter, hid), bf16),
                pltpu.VMEM((n, own_e, hid, quarter), bf16),
                pltpu.SemaphoreType.DMA((3, 2 * nz)),
            ],
        ),
        out_shape=[
            jax.ShapeDtypeStruct((blocks, n, tall, quarter), bf16),
            jax.ShapeDtypeStruct((blocks * seq, wide), bf16),
            jax.ShapeDtypeStruct((blocks * seq, wide), bf16),
        ],
        compiler_params=pltpu.CompilerParams(vmem_limit_bytes=56 * MIB),
        cost_estimate=pl.CostEstimate(
            flops=6 * blocks * seq * n * quarter * wide,
            bytes_accessed=40 * MIB,
            transcendentals=0,
        ),
    )(idx, g_all, act, up, probs, mask_all, *weights)


def output_kernel(nz, n, own_e, hid, slice_d, quarter, idx, *refs):
    hid_ref, near, far, y_ref, w_down, sems = refs

    @pl.when(pl.program_id(0) == 0)
    def _():
        load_weights(nz, slice_d, idx[0], idx[1], (((near, far), w_down),), sems, (True,))

    for q in range(n):
        total = jnp.zeros((hid_ref.shape[0], quarter), f32)
        for e in range(own_e):
            total += dot_nn(hid_ref[:, pl.ds(e * hid, hid)], w_down[q, e])
        y_ref[q, 0] = total.astype(bf16)


def output_call(idx, hidden, parts, n, nz):
    tokens, wide = hidden.shape
    seq = tokens // nz
    own_e, hid, slice_d = parts[0].shape[1:]
    quarter = 2 * slice_d
    return pl.pallas_call(
        functools.partial(output_kernel, nz, n, own_e, hid, slice_d, quarter),
        grid_spec=pltpu.PrefetchScalarGridSpec(
            num_scalar_prefetch=1,
            grid=(nz,),
            in_specs=[pl.BlockSpec((seq, wide), lambda i, idx: (i, 0))]
            + [pl.BlockSpec(memory_space=pl.ANY)] * 2,
            out_specs=pl.BlockSpec((n, 1, seq, quarter), lambda i, idx: (0, i, 0, 0)),
            scratch_shapes=[
                pltpu.VMEM((n, own_e, hid, quarter), bf16),
                pltpu.SemaphoreType.DMA((1, 2 * nz)),
            ],
        ),
        out_shape=jax.ShapeDtypeStruct((n, nz, seq, quarter), bf16),
        compiler_params=pltpu.CompilerParams(vmem_limit_bytes=48 * MIB),
        cost_estimate=pl.CostEstimate(
            flops=2 * tokens * n * quarter * wide, bytes_accessed=16 * MIB, transcendentals=0
        ),
    )(idx, hidden, *parts)


def down_grad_kernel(nz, own_e, hid, seq, slice_d, idx, g_ref, hid_ref, keep_ref, give_ref):
    for out_ref, c in ((keep_ref, idx[1]), (give_ref, 1 - idx[1])):
        cols = pl.ds(pl.multiple_of(c * slice_d, slice_d), slice_d)
        for e in range(own_e):
            total = jnp.zeros((hid, slice_d), f32)
            for blk in range(nz):
                left = hid_ref[pl.ds(blk * seq, seq), pl.ds(e * hid, hid)]
                total += dot_tn(left, g_ref[0, blk, :, cols])
            out_ref[0, e] = total.astype(bf16)


def down_grad_call(idx, g_all, hidden, own_e):
    n, nz, seq, quarter = g_all.shape
    tokens, wide = hidden.shape
    hid, slice_d = wide // own_e, quarter // 2
    out = pl.BlockSpec((1, own_e, hid, slice_d), lambda q, idx: (q ^ idx[0], 0, 0, 0))
    return pl.pallas_call(
        functools.partial(down_grad_kernel, nz, own_e, hid, seq, slice_d),
        grid_spec=pltpu.PrefetchScalarGridSpec(
            num_scalar_prefetch=1,
            grid=(n,),
            in_specs=[
                pl.BlockSpec((1, nz, seq, quarter), lambda q, idx: (q, 0, 0, 0)),
                pl.BlockSpec((tokens, wide), lambda q, idx: (0, 0)),
            ],
            out_specs=[out, out],
        ),
        out_shape=[jax.ShapeDtypeStruct((nz, own_e, hid, slice_d), bf16)] * 2,
        compiler_params=pltpu.CompilerParams(vmem_limit_bytes=48 * MIB),
        cost_estimate=pl.CostEstimate(
            flops=2 * tokens * n * quarter * wide, bytes_accessed=16 * MIB, transcendentals=0
        ),
    )(idx, g_all, hidden)


def up_grad_kernel(nz, own_e, hid, seq, slice_d, idx, m_ref, *refs):
    rights, (keep_ref, give_ref) = refs[:4], refs[4:]
    for out_ref, c in ((keep_ref, idx[1]), (give_ref, 1 - idx[1])):
        cols = pl.ds(pl.multiple_of(c * slice_d, slice_d), slice_d)
        for w in range(2):
            for e in range(own_e):
                total = jnp.zeros((slice_d, hid), f32)
                for blk in range(nz):
                    right = rights[2 * w + blk % 2][
                        pl.ds(blk // 2 * seq, seq), pl.ds(e * hid, hid)
                    ]
                    total += dot_tn(m_ref[0, pl.ds(blk * seq, seq), cols], right)
                out_ref[0, w, e] = total.astype(bf16)


def up_grad_call(idx, m_all, early, late, own_e, nz):
    n, tokens, quarter = m_all.shape
    seq = tokens // nz
    wide = early[0].shape[1]
    hid, slice_d = wide // own_e, quarter // 2
    full = pl.BlockSpec(early[0].shape, lambda k, idx: (0, 0))
    out = pl.BlockSpec(
        (1, 2, own_e, slice_d, hid), lambda k, idx: (k ^ idx[2] ^ idx[0], 0, 0, 0, 0)
    )
    return pl.pallas_call(
        functools.partial(up_grad_kernel, nz, own_e, hid, seq, slice_d),
        grid_spec=pltpu.PrefetchScalarGridSpec(
            num_scalar_prefetch=1,
            grid=(n,),
            in_specs=[pl.BlockSpec((1, tokens, quarter), lambda k, idx: (k, 0, 0))] + [full] * 4,
            out_specs=[out, out],
        ),
        out_shape=[jax.ShapeDtypeStruct((nz, 2, own_e, slice_d, hid), bf16)] * 2,
        compiler_params=pltpu.CompilerParams(vmem_limit_bytes=48 * MIB),
        cost_estimate=pl.CostEstimate(
            flops=4 * tokens * n * quarter * wide, bytes_accessed=24 * MIB, transcendentals=0
        ),
    )(idx, m_all, early[0], late[0], early[1], late[1])


def place_kernel(nz, idx, *refs):
    ups, downs, outs = refs[:nz], refs[nz : 2 * nz], refs[2 * nz :]
    for i in range(nz):

        @pl.when(pl.program_id(0) == i)
        def _(i=i):
            outs[0][...] = ups[i][0].astype(f32)
            outs[1][...] = ups[i][1].astype(f32)
            outs[2][...] = downs[i][...].astype(f32)


def place_call(idx, ups, downs):
    nz = len(ups)
    flat = list(ups) + list(downs)
    fixed = lambda rank: lambda k, idx: (0,) * rank
    shapes = [ups[0].shape[1:], ups[0].shape[1:], downs[0].shape]
    return pl.pallas_call(
        functools.partial(place_kernel, nz),
        grid_spec=pltpu.PrefetchScalarGridSpec(
            num_scalar_prefetch=1,
            grid=(nz,),
            in_specs=[pl.BlockSpec(part.shape, fixed(part.ndim)) for part in flat],
            out_specs=[
                pl.BlockSpec(shape, lambda k, idx: (k ^ idx[0], 0, 0)) for shape in shapes
            ],
        ),
        out_shape=[jax.ShapeDtypeStruct((EXPERTS,) + shape[1:], f32) for shape in shapes],
        compiler_params=pltpu.CompilerParams(vmem_limit_bytes=48 * MIB),
        cost_estimate=pl.CostEstimate(flops=0, bytes_accessed=20 * MIB, transcendentals=0),
    )(idx, *flat)


def shards(
    tokens,
    cotangent,
    routes,
    wq,
    wk,
    wv,
    wo,
    attn_gain,
    q_gain,
    k_gain,
    moe_gain,
    router,
    w_gate,
    w_up,
    w_down,
):
    nz = lax.axis_size("z")
    me_t = lax.axis_index("tensor")
    me_z = lax.axis_index("z")
    me_c = lax.axis_index("core")
    dp = ("z", "core")
    seq, width = tokens.shape
    quarter = width // lax.axis_size("tensor")
    local = wq.shape[1]
    local_heads = local // HEAD_DIM
    slice_d = wq.shape[0]
    own_e = EXPERTS // nz
    hid = w_gate.shape[2]

    idx = jnp.stack([me_z, me_c, me_t]).astype(jnp.int32)

    small = jnp.concatenate([attn_gain[:, None], moe_gain[:, None], router], 1)
    small = jnp.pad(small, ((0, 0), (0, LANES - small.shape[1])))
    packed = lax.all_gather(jnp.concatenate([wq, wk, wv, small], 1), dp, axis=0, tiled=True)
    mask = jnp.sum(
        (routes[:, :, None] == jnp.arange(EXPERTS)[None, None, :]).astype(bf16), 1
    )
    packed, *mask_parts = fence(packed, *spread_z(mask.T))
    mask_all = jnp.stack(mask_parts).transpose(0, 2, 1)
    mask_all = jnp.pad(
        mask_all.reshape(nz * seq, EXPERTS).astype(f32),
        ((0, 0), (FIRST, LANES - EXPERTS - FIRST)),
    )
    wqkv_full = packed[:, : 3 * local]
    small_full = packed[:, 3 * local :]
    a_gain = small_full[:, 0].astype(f32)
    m_gain = small_full[:, 1].astype(f32)
    router_full = small_full[:, FIRST : FIRST + EXPERTS]
    wo_full = lax.all_gather(after(wo, packed), dp, axis=1, tiled=True)

    def fetch(weight):
        pick = lambda k: lax.dynamic_slice_in_dim(weight, (me_z ^ k) * own_e, own_e, 0)
        return [swap(pick(k), "z", k) for k in range(nz)]

    def both_cores(parts):
        parts = jnp.stack(parts)
        return [parts, swap(parts, "core", 1)]

    cot_parts = spread_z(after(columns(cotangent, me_t, quarter), packed))

    xf = tokens.astype(f32)
    rate_x = lax.rsqrt(jnp.mean(xf * xf, -1, keepdims=True) + EPS)
    gain_q = q_gain.astype(f32)
    gain_k = k_gain.astype(f32)
    a_low = (xf * rate_x * a_gain).astype(bf16)
    qkv = jnp.dot(a_low, wqkv_full, preferred_element_type=f32)
    query, keyed, valued = qkv[:, :local], qkv[:, local : 2 * local], qkv[:, 2 * local :]
    sums = tensor_sum(jnp.stack([jnp.sum(query * query, -1), jnp.sum(keyed * keyed, -1)]))
    rate_q = lax.rsqrt(sums[0] / width + EPS)[:, None]
    rate_k = lax.rsqrt(sums[1] / width + EPS)[:, None]
    cosine, sine = rope_tables(seq, HEAD_DIM)
    heads = (seq, local_heads, HEAD_DIM)
    q_rot = rotate((query * rate_q * gain_q).reshape(heads), cosine, sine).astype(bf16)
    k_rot = rotate((keyed * rate_k * gain_k).reshape(heads), cosine, sine).astype(bf16)
    v_low = valued.reshape(heads).astype(bf16)
    scale = HEAD_DIM ** (-0.5)
    scores = scale * jnp.einsum("qhd,khd->hqk", q_rot, k_rot, preferred_element_type=f32)
    causal = jnp.arange(seq)[:, None] >= jnp.arange(seq)[None, :]
    scores = jnp.where(causal[None], scores, -1e30)
    peak = jnp.max(scores, -1, keepdims=True)
    expd = jnp.exp(scores - peak)
    weights = expd / jnp.sum(expd, -1, keepdims=True)
    weights_low = weights.astype(bf16)
    outputs = jnp.einsum("hqk,khd->qhd", weights_low, v_low, preferred_element_type=f32)
    joined = outputs.reshape(seq, local).astype(bf16)
    wo_full = after(wo_full, joined)
    attn = jnp.dot(joined, wo_full, preferred_element_type=f32).astype(bf16)
    attn, *cot_parts = fence(attn, *cot_parts)
    cot_all = lax.all_gather(jnp.stack(cot_parts), "tensor", axis=0, tiled=False)
    gate_parts = fetch(after(w_gate, attn))

    x_own = columns(xf, me_t, quarter)
    resid = x_own + scatter_columns(attn)
    rate_r = lax.rsqrt(tensor_sum(jnp.sum(resid * resid, -1)) / width + EPS)[:, None]
    gain_own = lax.dynamic_slice_in_dim(m_gain, me_t * quarter, quarter, 0)
    m_own = (resid * rate_r * gain_own).astype(bf16)

    m_own, *gate_parts = fence(m_own, *gate_parts)
    m_parts = fence(*spread_z(m_own))
    up_parts = fetch(after(w_up, m_parts[0]))
    gate_parts = both_cores(gate_parts)
    m_flat = jnp.concatenate(m_parts, 0)
    m_near = spread_tensor_near(m_flat)
    held = fence(*m_near, *up_parts)
    m_near, up_parts = held[: len(m_near)], held[len(m_near) :]
    up_parts = both_cores(up_parts)
    down_parts = fetch(after(w_down, up_parts[0]))
    m_all = spread_tensor_far(m_flat, m_near)
    m_all, down_parts[2] = fence(m_all, down_parts[2])
    router_q = small_full.reshape(-1, quarter, LANES)
    act, up, hidden, probs_all = forward_call(
        idx, m_all, mask_all, router_q, gate_parts, up_parts, nz
    )
    hidden, *down_parts = fence(hidden, *down_parts)
    down_parts = both_cores(down_parts)
    down_keep, down_give = down_grad_call(idx, cot_all, hidden, own_e)

    def to_owners(keep, got):
        summed = (keep.astype(f32) + got.astype(f32)).astype(bf16)
        return [swap(summed[k], "z", k) for k in range(nz)]

    down_own = to_owners(down_keep, swap(down_give, "core", 1))
    half_call = lambda first, probs: backward_call(
        idx, first, cot_all, act, up, probs, mask_all, gate_parts + up_parts + down_parts
    )
    odds, evens = range(1, nz, 2), range(0, nz, 2)
    late = half_call(1, after(probs_all, down_give))
    first = {k: scatter_first(late[0][k // 2], k // 2 % 2) for k in odds}
    early = half_call(0, after(probs_all, late[1]))
    held = fence(*early, *(first[k] for k in odds), *down_own[:3])
    early, got = held[:3], dict(zip(odds, held[3:]))
    down_own[:3] = held[3 + nz // 2 :]
    second = {k: scatter_second(late[0][k // 2], got[k], k // 2 % 2) for k in odds}
    first = {k: scatter_first(early[0][k // 2], k // 2 % 2) for k in evens}
    up_keep, up_give = up_grad_call(idx, m_all, early[1:3], late[1:3], own_e, nz)
    held = fence(up_keep, up_give, *(first[k] for k in evens), *down_own[3:])
    (up_keep, up_give), got = held[:2], dict(zip(evens, held[2:]))
    down_own[3:] = held[2 + nz // 2 :]
    near = scatter_z_near({k: scatter_third(*second[k]) for k in odds})
    second = {k: scatter_second(early[0][k // 2], got[k], k // 2 % 2) for k in evens}
    up_got = swap(up_give, "core", 1)
    moe_part = output_call(idx, after(hidden, up_give), down_parts, width // quarter, nz)
    moe_part, near, up_got = fence(moe_part, near, up_got)
    dm_own = scatter_z_far({k: scatter_third(*second[k]) for k in evens}, near)
    dgate = jnp.concatenate(
        [dm_own[seq + h * EXPERTS :][:EXPERTS] for h in range(seq // quarter)], 1
    )
    dm_own = dm_own[:seq]
    up_own = to_owners(after(up_keep, dm_own), up_got)
    moe_sum = lax.psum_scatter(moe_part, "tensor", scatter_dimension=0, tiled=False)

    dgate = dgate.T
    probs = probs_all[:seq, FIRST : FIRST + EXPERTS]
    dprobs = dgate * mask.astype(f32)
    dlogits = probs * (dprobs - jnp.sum(probs * dprobs, -1, keepdims=True))
    router_own = lax.dynamic_slice_in_dim(router_full, me_t * quarter, quarter, 0)
    router_part = jnp.dot(m_own.astype(f32).T, dlogits, precision=HIGH)
    dm_own = dm_own + jnp.dot(dlogits, router_own.astype(f32).T, precision=HIGH)

    normed = resid * rate_r
    moe_gain_part = jnp.sum(dm_own * normed, 0)
    pulled = dm_own * gain_own
    inner_r = tensor_sum(jnp.sum(pulled * normed, -1))[:, None] / width
    cot_own = columns(cotangent, me_t, quarter).astype(f32)
    dresid = cot_own + rate_r * (pulled - normed * inner_r)
    dresid_low = gather_tensor(dresid.astype(bf16))

    wo_grad = jnp.einsum("sa,sd->ad", joined, dresid_low, preferred_element_type=f32)
    dout = (
        jnp.einsum("sd,ad->sa", dresid_low, wo_full, preferred_element_type=f32)
        .astype(bf16)
        .reshape(heads)
    )
    dweights = jnp.einsum("qhd,khd->hqk", dout, v_low, preferred_element_type=f32)
    dv = jnp.einsum("hqk,qhd->khd", weights_low, dout, preferred_element_type=f32)
    inner = jnp.sum(weights * dweights, -1, keepdims=True)
    dscores = (weights * (dweights - inner)).astype(bf16)
    dq_rot = scale * jnp.einsum("hqk,khd->qhd", dscores, k_rot, preferred_element_type=f32)
    dk_rot = scale * jnp.einsum("hqk,qhd->khd", dscores, q_rot, preferred_element_type=f32)
    dq_norm = unrotate(dq_rot, cosine, sine).reshape(seq, local)
    dk_norm = unrotate(dk_rot, cosine, sine).reshape(seq, local)
    inners = tensor_sum(
        jnp.stack(
            [jnp.sum(dq_norm * gain_q * query, -1), jnp.sum(dk_norm * gain_k * keyed, -1)]
        )
    )
    dq_low = (rate_q * gain_q * dq_norm - query * rate_q**3 * inners[0][:, None] / width).astype(
        bf16
    )
    dk_low = (rate_k * gain_k * dk_norm - keyed * rate_k**3 * inners[1][:, None] / width).astype(
        bf16
    )
    dv_low = dv.reshape(seq, local).astype(bf16)
    q_gain_part = jnp.sum(dq_norm * query * rate_q, 0)
    k_gain_part = jnp.sum(dk_norm * keyed * rate_k, 0)
    dqkv = jnp.concatenate([dq_low, dk_low, dv_low], 1)
    dqkv, *up_own = fence(dqkv, *up_own)
    moe_sum = after(moe_sum, dqkv)
    moe_near = scatter_z_near({k: moe_sum[k] for k in odds})
    moe_own = scatter_z_far({k: moe_sum[k].astype(f32) for k in evens}, moe_near)
    mixed = gather_tensor((resid + moe_own).astype(bf16))
    expert_grads = place_call(idx, up_own, down_own)
    wqkv_grad = jnp.einsum("sd,sa->da", a_low, dqkv, preferred_element_type=f32).astype(bf16)
    da_part = jnp.einsum("sa,da->sd", dqkv, wqkv_full, preferred_element_type=f32)
    da_own = scatter_columns(da_part.astype(bf16))
    norm_x = x_own * rate_x
    attn_gain_part = jnp.sum(da_own * norm_x, 0)
    pulled_x = da_own * lax.dynamic_slice_in_dim(a_gain, me_t * quarter, quarter, 0)
    inner_x = tensor_sum(jnp.sum(pulled_x * norm_x, -1))[:, None] / width
    tokens_grad = gather_tensor(
        (dresid + rate_x * (pulled_x - norm_x * inner_x)).astype(bf16)
    )

    wqkv_own = lax.psum_scatter(wqkv_grad, dp, scatter_dimension=0, tiled=True).astype(f32)
    wo_own = lax.psum_scatter(wo_grad.astype(bf16), dp, scatter_dimension=1, tiled=True).astype(f32)
    smalls = jnp.concatenate(
        [
            q_gain_part[None],
            k_gain_part[None],
            attn_gain_part[None],
            moe_gain_part[None],
            router_part.T,
        ],
        0,
    )
    smalls = butterfly_sum(smalls, ("core", "z"))
    half = lax.dynamic_slice_in_dim(smalls[2:], me_c * slice_d, slice_d, 1)
    half = tensor_sum(jnp.where(me_t == me_z, half, 0.0))
    return (
        mixed,
        tokens_grad,
        wqkv_own[:, :local],
        wqkv_own[:, local : 2 * local],
        wqkv_own[:, 2 * local :],
        wo_own,
        half[0],
        smalls[0],
        smalls[1],
        half[1],
        half[2:].T,
        expert_grads[0],
        expert_grads[1],
        expert_grads[2],
    )


def solution(mesh):
    fine = Mesh(
        mesh.devices.reshape(mesh.shape["dp"] // 2, 2, mesh.shape["tensor"]),
        ("z", "core", "tensor"),
    )
    dp = ("z", "core")
    in_specs = (
        P(dp, None),
        P(dp, None),
        P(dp, None),
        P(dp, "tensor"),
        P(dp, "tensor"),
        P(dp, "tensor"),
        P("tensor", dp),
        P(dp),
        P("tensor"),
        P("tensor"),
        P(dp),
        P(dp, None),
        P(None, dp, "tensor"),
        P(None, dp, "tensor"),
        P(None, "tensor", dp),
    )
    out_specs = (
        P(dp, None),
        P(dp, None),
        P(dp, "tensor"),
        P(dp, "tensor"),
        P(dp, "tensor"),
        P("tensor", dp),
        P(dp),
        P("tensor"),
        P("tensor"),
        P(dp),
        P(dp, None),
        P(None, dp, "tensor"),
        P(None, dp, "tensor"),
        P(None, "tensor", dp),
    )
    return jax.shard_map(shards, mesh=fine, in_specs=in_specs, out_specs=out_specs, check_vma=False)
```

```python
import functools

import jax
import jax.numpy as jnp
from jax import lax
from jax.experimental import pallas as pl
from jax.experimental.pallas import tpu as pltpu
from jax.sharding import Mesh
from jax.sharding import PartitionSpec as P

HEAD_DIM = 128
EXPERTS = 16
LANES = 128
FIRST = 2

EPS = 1e-05
THETA = 10000.0
HIGH = lax.Precision.HIGHEST
f32 = jnp.float32
bf16 = jnp.bfloat16
MIB = 1 << 20


def after(value, *earlier):
    return lax.optimization_barrier((value, *earlier))[0]


def fence(*values):
    return list(lax.optimization_barrier(values))


def swap(value, axis, mask):
    if mask == 0:
        return value
    n = lax.axis_size(axis)
    return lax.ppermute(value, axis, [(i, i ^ mask) for i in range(n)])


def bits_of(axis):
    n = lax.axis_size(axis)
    return [1 << b for b in range(n.bit_length() - 1)]


def butterfly_sum(value, axes):
    for axis in axes:
        for bit in bits_of(axis):
            value = value + swap(value, axis, bit)
    return value


def tensor_sum(value):
    return butterfly_sum(value, ("tensor",))


def rope_tables(length, head_dim):
    half = head_dim // 2
    freq = THETA ** (-(jnp.arange(half).astype(f32) * 2.0 / head_dim))
    angle = jnp.arange(length).astype(f32)[:, None] * freq[None, :]
    cosine = jnp.concatenate([jnp.cos(angle), jnp.cos(angle)], -1)
    sine = jnp.concatenate([jnp.sin(angle), jnp.sin(angle)], -1)
    return (cosine, sine)


def rotate(value, cosine, sine):
    half = value.shape[-1] // 2
    turned = jnp.concatenate([-value[..., half:], value[..., :half]], -1)
    return value * cosine[:, None, :] + turned * sine[:, None, :]


def unrotate(grad, cosine, sine):
    half = grad.shape[-1] // 2
    scaled = grad * sine[:, None, :]
    back_turn = jnp.concatenate([scaled[..., half:], -scaled[..., :half]], -1)
    return grad * cosine[:, None, :] + back_turn


def columns(value, index, size):
    return lax.dynamic_slice_in_dim(value, index * size, size, 1)


def spread_z(value):
    parts = {0: value}
    for bit in reversed(bits_of("z")):
        parts.update({k ^ bit: swap(v, "z", bit) for k, v in parts.items()})
    return [parts[k] for k in range(len(parts))]


def spread_tensor_near(value):
    n = lax.axis_size("tensor")
    return [swap(value, "tensor", k) for k in ((1, 2) if n == 4 else range(1, n))]


def spread_tensor_cross(near):
    if lax.axis_size("tensor") != 4:
        return []
    half = near[0].shape[0] // 2
    return [swap(near[0][:half], "tensor", 2), swap(near[1][half:], "tensor", 1)]


def place_of(n, half, k, row):
    if n != 4 or k < 3:
        return (k, row)
    return (3, row) if row < half else (4, row - half)


def spread_tensor_far(value, near):
    if lax.axis_size("tensor") != 4:
        return jnp.stack([value, *near])
    half = value.shape[0] // 2
    cross = [swap(near[0][:half], "tensor", 2), swap(near[1][half:], "tensor", 1)]
    return jnp.stack([value, *near, jnp.concatenate(cross, 0)])


def spread_tensor(value):
    return spread_tensor_far(value, spread_tensor_near(value))


def gather_tensor(value):
    me, n = lax.axis_index("tensor"), lax.axis_size("tensor")
    rows, width = value.shape
    out = jnp.zeros((rows, n * width), value.dtype)
    parts = spread_tensor(value)
    for k in range(n):
        part = parts[k]
        out = lax.dynamic_update_slice(out, part, (0, (me ^ k) * width))
    return out


def order_of(n, odd):
    if n != 4:
        return tuple(range(n))
    return (0, 1, 2, 3) if odd else (0, 2, 1, 3)


def scatter_first(block, odd):
    n = block.shape[0]
    if n != 4:
        return jnp.stack([swap(block[k], "tensor", k) for k in range(1, n)])
    return swap(block[2:], "tensor", 2 if odd else 1)


def scatter_second(block, got, odd):
    got = got.astype(f32)
    mine = block[0].astype(f32)
    if block.shape[0] != 4:
        return mine + jnp.sum(got, 0), None
    other = (block[1].astype(f32) + got[1]).astype(bf16)
    return mine + got[0], swap(other, "tensor", 1 if odd else 2)


def scatter_third(mine, got):
    return mine if got is None else mine + got.astype(f32)


def scatter_z_near(parts):
    return swap(jnp.stack([parts[k].astype(bf16) for k in sorted(parts)]), "z", 1)


def scatter_z_far(parts, got):
    parts = {k: parts[k] + got[i].astype(f32) for i, k in enumerate(sorted(parts))}
    for bit in bits_of("z")[1:]:
        away = sorted(k for k in parts if k & bit)
        got = swap(jnp.stack([parts[k].astype(bf16) for k in away]), "z", bit)
        parts = {k ^ bit: parts[k ^ bit] + got[i].astype(f32) for i, k in enumerate(away)}
    return parts[0]


def columns_blocks(value):
    me, n = lax.axis_index("tensor"), lax.axis_size("tensor")
    rows, width = value.shape[0], value.shape[1] // n
    half = rows // 2
    return [
        jnp.stack(
            [
                columns(value[odd * half : (odd + 1) * half], me ^ k, width)
                for k in order_of(n, odd)
            ]
        )
        for odd in (0, 1)
    ]


def dot_nn(a, b):
    return lax.dot_general(a, b, (((1,), (0,)), ((), ())), preferred_element_type=f32)


def dot_nt(a, b):
    return lax.dot_general(a, b, (((1,), (1,)), ((), ())), preferred_element_type=f32)


def dot_tn(a, b):
    return lax.dot_general(a, b, (((0,), (0,)), ((), ())), preferred_element_type=f32)


def weight_copies(nz, slice_d, own_e, idx, parts, whole, sems, down):
    copies = []
    for c in range(2):
        for k in range(nz):
            half = pl.multiple_of((idx[1] ^ c) * slice_d, slice_d)
            at = pl.multiple_of((idx[0] ^ k ^ idx[2]) * 2 * slice_d, slice_d) + half
            if down:
                copies.append((parts[c].at[k], whole.at[:, :, pl.ds(at, slice_d)]))
            else:
                hid = whole.shape[1] // own_e
                for e in range(own_e):
                    target = whole.at[pl.ds(at, slice_d), pl.ds(e * hid, hid)]
                    copies.append((parts[c].at[k, e], target))
    return [pltpu.make_async_copy(*pair, sems.at[j]) for j, pair in enumerate(copies)]


def start(copies):
    for copy in copies:
        copy.start()


def finish(copies):
    for copy in copies:
        copy.wait()


def own_gate(gates, lane, me_z, own_e, e):
    return jnp.sum(jnp.where(lane == FIRST + me_z * own_e + e, gates, 0.0), -1, keepdims=True)


def forward_kernel(nz, n, own_e, hid, slice_d, seq, quarter, places, idx, *refs):
    mask_ref, router_ref = refs[:2]
    gate_parts, up_parts, m_refs = refs[2:4], refs[4:6], refs[6:-11]
    act_ref, up_ref, hid_ref, probs_ref, m_out, w_gate, w_up, m_full, *sems = refs[-11:]
    gate_sems, up_sems, m_sems = sems
    me_z, me_t = idx[0], idx[2]
    step = pl.program_id(0)
    first = step == 0
    m_copies = [
        [
            pltpu.make_async_copy(
                m_refs[j].at[pl.ds(row, seq), :],
                m_full.at[pl.ds(i * seq, seq), pl.ds(k * quarter, quarter)],
                m_sems.at[i, k],
            )
            for k, (j, row) in enumerate(places[i])
        ]
        for i in range(nz)
    ]
    gate_copies = weight_copies(nz, slice_d, own_e, idx, gate_parts, w_gate, gate_sems, False)
    up_copies = weight_copies(nz, slice_d, own_e, idx, up_parts, w_up, up_sems, False)

    @pl.when(first)
    def _():
        start(m_copies[0] + gate_copies + up_copies)
        for copies in m_copies[1:]:
            start(copies)

    for i in range(nz):

        @pl.when(step == i)
        def _(i=i):
            finish(m_copies[i])

    rows = seq
    m_block = m_full[pl.ds(pl.multiple_of(step * seq, seq), seq), :]
    m_out[...] = m_block
    lane = lax.broadcasted_iota(jnp.int32, (rows, LANES), 1)
    logits = jnp.zeros((rows, LANES), f32)
    for k in range(n):
        logits += dot_nn(m_block[:, k * quarter : (k + 1) * quarter], router_ref[me_t ^ k])
    named = (lane >= FIRST) & (lane < FIRST + EXPERTS)
    logits = jnp.where(named, logits, -1e30)
    expd = jnp.where(named, jnp.exp(logits - jnp.max(logits, -1, keepdims=True)), 0.0)
    probs = expd / jnp.sum(expd, -1, keepdims=True)
    probs_ref[...] = probs
    gates = probs * mask_ref[...]

    @pl.when(first)
    def _():
        finish(gate_copies)

    for e in range(own_e):
        at = pl.ds(e * hid, hid)
        act_ref[:, at] = dot_nn(m_block, w_gate[:, at])

    @pl.when(first)
    def _():
        finish(up_copies)

    for e in range(own_e):
        at = pl.ds(e * hid, hid)
        up = dot_nn(m_block, w_up[:, at])
        up_ref[:, at] = up
        act = act_ref[:, at]
        gate = own_gate(gates, lane, me_z, own_e, e)
        hid_ref[:, at] = (gate * (act * jax.nn.sigmoid(act) * up)).astype(bf16)


def forward_call(idx, pieces, places, mask_all, router_q, gate_parts, up_parts, nz):
    n, quarter = router_q.shape[:2]
    tokens = mask_all.shape[0]
    seq = tokens // nz
    own_e, slice_d, hid = up_parts[0].shape[1:]
    wide = own_e * hid
    here = lambda i, idx: (i, 0)
    return pl.pallas_call(
        functools.partial(forward_kernel, nz, n, own_e, hid, slice_d, seq, quarter, places),
        grid_spec=pltpu.PrefetchScalarGridSpec(
            num_scalar_prefetch=1,
            grid=(nz,),
            in_specs=[
                pl.BlockSpec((seq, LANES), here),
                pl.BlockSpec((n, quarter, LANES), lambda i, idx: (0, 0, 0)),
            ]
            + [pl.BlockSpec(memory_space=pl.ANY)] * (4 + len(pieces)),
            out_specs=[
                pl.BlockSpec((seq, wide), here),
                pl.BlockSpec((seq, wide), here),
                pl.BlockSpec((seq, wide), here),
                pl.BlockSpec((seq, LANES), here),
                pl.BlockSpec((seq, n * quarter), here),
            ],
            scratch_shapes=[
                pltpu.VMEM((n * quarter, wide), bf16),
                pltpu.VMEM((n * quarter, wide), bf16),
                pltpu.VMEM((tokens, n * quarter), bf16),
                pltpu.SemaphoreType.DMA((2 * nz * own_e,)),
                pltpu.SemaphoreType.DMA((2 * nz * own_e,)),
                pltpu.SemaphoreType.DMA((nz, n)),
            ],
        ),
        out_shape=[
            jax.ShapeDtypeStruct((tokens, wide), f32),
            jax.ShapeDtypeStruct((tokens, wide), f32),
            jax.ShapeDtypeStruct((tokens, wide), bf16),
            jax.ShapeDtypeStruct((tokens, LANES), f32),
            jax.ShapeDtypeStruct((tokens, n * quarter), bf16),
        ],
        compiler_params=pltpu.CompilerParams(vmem_limit_bytes=56 * MIB),
        cost_estimate=pl.CostEstimate(
            flops=4 * tokens * n * quarter * wide, bytes_accessed=40 * MIB, transcendentals=0
        ),
    )(idx, mask_all, router_q, *gate_parts, *up_parts, *pieces)


def backward_kernel(nz, n, own_e, hid, slice_d, quarter, idx, *refs):
    g_ref, act_ref, up_ref, probs_ref, mask_ref = refs[:5]
    dx_ref, dg_ref, du_ref, w_gate, w_up, w_down, gate_sems, up_sems, down_sems = refs[11:]
    i = pl.program_id(0)
    me_z = idx[0]
    gate_copies = weight_copies(nz, slice_d, own_e, idx, refs[5:7], w_gate, gate_sems, False)
    up_copies = weight_copies(nz, slice_d, own_e, idx, refs[7:9], w_up, up_sems, False)
    down_copies = weight_copies(nz, slice_d, own_e, idx, refs[9:11], w_down, down_sems, True)

    @pl.when(i == 0)
    def _():
        start(down_copies + gate_copies + up_copies)
        finish(down_copies)

    rows = act_ref.shape[0]
    lane = lax.broadcasted_iota(jnp.int32, (rows, LANES), 1)
    gates = probs_ref[...] * mask_ref[...]
    dgate = jnp.zeros((rows, LANES), f32)
    g_block = jnp.concatenate([g_ref[q, 0] for q in range(n)], 1)
    for e in range(own_e):
        gate = own_gate(gates, lane, me_z, own_e, e)
        at = pl.ds(e * hid, hid)
        back = dot_nt(g_block, w_down[e])
        act = act_ref[:, at]
        up = up_ref[:, at]
        sigma = jax.nn.sigmoid(act)
        silu = act * sigma
        dgate = jnp.where(
            lane == me_z * own_e + e, jnp.sum(silu * up * back, -1, keepdims=True), dgate
        )
        back = gate * back
        dg_ref[:, at] = (back * up * sigma * (1.0 + act * (1.0 - sigma))).astype(bf16)
        du_ref[:, at] = (back * silu).astype(bf16)
    dgate = jnp.transpose(dgate)[:EXPERTS].astype(bf16)

    @pl.when(i == 0)
    def _():
        finish(gate_copies + up_copies)

    even, odd = order_of(n, 0), order_of(n, 1)
    for j in range(n):
        k = jnp.where(i % 2 == 0, even[j], odd[j])
        at = pl.ds(pl.multiple_of(k * quarter, quarter), quarter)
        total = dot_nt(dg_ref[...], w_gate[at, :]) + dot_nt(du_ref[...], w_up[at, :])
        dx_ref[0, j, pl.ds(0, rows), :] = total.astype(bf16)
        for h in range(rows // quarter):
            dx_ref[0, j, pl.ds(rows + h * EXPERTS, EXPERTS), :] = dgate[
                :, h * quarter : (h + 1) * quarter
            ]


def backward_call(idx, first, g_all, act, up, probs, mask_all, weights):
    n, nz, seq, quarter = g_all.shape
    own_e, slice_d, hid = weights[0].shape[1:]
    blocks = nz // 2
    wide = own_e * hid
    tall = seq + EXPERTS * (seq // quarter)
    some = lambda i, idx: (2 * i + first, 0)
    here = lambda i, idx: (i, 0)
    hbm = pl.BlockSpec(memory_space=pl.ANY)
    return pl.pallas_call(
        functools.partial(backward_kernel, nz, n, own_e, hid, slice_d, quarter),
        grid_spec=pltpu.PrefetchScalarGridSpec(
            num_scalar_prefetch=1,
            grid=(blocks,),
            in_specs=[
                pl.BlockSpec((n, 1, seq, quarter), lambda i, idx: (0, 2 * i + first, 0, 0)),
                pl.BlockSpec((seq, wide), some),
                pl.BlockSpec((seq, wide), some),
                pl.BlockSpec((seq, LANES), some),
                pl.BlockSpec((seq, LANES), some),
            ]
            + [hbm] * 6,
            out_specs=[
                pl.BlockSpec((1, n, tall, quarter), lambda i, idx: (i, 0, 0, 0)),
                pl.BlockSpec((seq, wide), here),
                pl.BlockSpec((seq, wide), here),
            ],
            scratch_shapes=[
                pltpu.VMEM((n * quarter, wide), bf16),
                pltpu.VMEM((n * quarter, wide), bf16),
                pltpu.VMEM((own_e, hid, n * quarter), bf16),
                pltpu.SemaphoreType.DMA((2 * nz * own_e,)),
                pltpu.SemaphoreType.DMA((2 * nz * own_e,)),
                pltpu.SemaphoreType.DMA((2 * nz,)),
            ],
        ),
        out_shape=[
            jax.ShapeDtypeStruct((blocks, n, tall, quarter), bf16),
            jax.ShapeDtypeStruct((blocks * seq, wide), bf16),
            jax.ShapeDtypeStruct((blocks * seq, wide), bf16),
        ],
        compiler_params=pltpu.CompilerParams(vmem_limit_bytes=56 * MIB),
        cost_estimate=pl.CostEstimate(
            flops=6 * blocks * seq * n * quarter * wide,
            bytes_accessed=40 * MIB,
            transcendentals=0,
        ),
    )(idx, g_all, act, up, probs, mask_all, *weights)


def output_kernel(nz, own_e, hid, slice_d, quarter, idx, hid_ref, near, far, y_ref, w_down, sems):
    i, j = pl.program_id(0), pl.program_id(1)

    @pl.when((i == 0) & (j == 0))
    def _():
        copies = weight_copies(nz, slice_d, own_e, idx, (near, far), w_down, sems, True)
        start(copies)
        finish(copies)

    at = pl.ds(pl.multiple_of(j * quarter, quarter), quarter)
    part = w_down[:, :, at].reshape(own_e * hid, quarter)
    y_ref[0, 0] = dot_nn(hid_ref[...], part).astype(bf16)


def output_call(idx, hidden, parts, n, nz):
    tokens, wide = hidden.shape
    seq = tokens // nz
    own_e, hid, slice_d = parts[0].shape[1:]
    quarter = 2 * slice_d
    return pl.pallas_call(
        functools.partial(output_kernel, nz, own_e, hid, slice_d, quarter),
        grid_spec=pltpu.PrefetchScalarGridSpec(
            num_scalar_prefetch=1,
            grid=(nz, n),
            in_specs=[pl.BlockSpec((seq, wide), lambda i, j, idx: (i, 0))]
            + [pl.BlockSpec(memory_space=pl.ANY)] * 2,
            out_specs=pl.BlockSpec(
                (1, 1, seq, quarter), lambda i, j, idx: (j ^ idx[2], i ^ idx[0], 0, 0)
            ),
            scratch_shapes=[
                pltpu.VMEM((own_e, hid, n * quarter), bf16),
                pltpu.SemaphoreType.DMA((2 * nz,)),
            ],
        ),
        out_shape=jax.ShapeDtypeStruct((n, nz, seq, quarter), bf16),
        compiler_params=pltpu.CompilerParams(vmem_limit_bytes=48 * MIB),
        cost_estimate=pl.CostEstimate(
            flops=2 * tokens * n * quarter * wide, bytes_accessed=16 * MIB, transcendentals=0
        ),
    )(idx, hidden, *parts)


def down_grad_kernel(nz, n, own_e, hid, seq, slice_d, idx, hid_ref, *refs):
    g_refs, (keep_ref, give_ref, g_out, g_full, sems) = refs[:-5], refs[-5:]
    step = pl.program_id(0)
    copies = []
    for k in range(n):
        copies.append([])
        for i in range(nz):
            j, row = place_of(n, nz * seq // 2, k, i * seq)
            copies[k].append(
                pltpu.make_async_copy(
                    g_refs[j].at[pl.ds(row, seq), :],
                    g_full.at[k, pl.ds(i * seq, seq), :],
                    sems.at[k, i],
                )
            )

    @pl.when(step == 0)
    def _():
        for some in copies:
            start(some)

    for k in range(n):

        @pl.when(step == k)
        def _(k=k):
            finish(copies[k])

    g_block = g_full[step]
    g_out[0] = g_block
    total = dot_tn(g_block, hid_ref[...])
    halves = (total[:slice_d], total[slice_d:])
    for e in range(own_e):
        parts = [jnp.transpose(half[:, e * hid : (e + 1) * hid]).astype(bf16) for half in halves]
        keep_ref[0, e] = jnp.where(idx[1] == 0, parts[0], parts[1])
        give_ref[0, e] = jnp.where(idx[1] == 0, parts[1], parts[0])


def down_grad_call(idx, pieces, hidden, own_e, nz, n):
    tokens, wide = hidden.shape
    quarter, seq = pieces[0].shape[1], tokens // nz
    hid, slice_d = wide // own_e, quarter // 2
    out = pl.BlockSpec((1, own_e, hid, slice_d), lambda k, idx: (k ^ idx[2] ^ idx[0], 0, 0, 0))
    return pl.pallas_call(
        functools.partial(down_grad_kernel, nz, n, own_e, hid, seq, slice_d),
        grid_spec=pltpu.PrefetchScalarGridSpec(
            num_scalar_prefetch=1,
            grid=(n,),
            in_specs=[pl.BlockSpec((tokens, wide), lambda k, idx: (0, 0))]
            + [pl.BlockSpec(memory_space=pl.ANY)] * len(pieces),
            out_specs=[out, out, pl.BlockSpec((1, tokens, quarter), lambda k, idx: (k, 0, 0))],
            scratch_shapes=[
                pltpu.VMEM((n, tokens, quarter), bf16),
                pltpu.SemaphoreType.DMA((n, nz)),
            ],
        ),
        out_shape=[jax.ShapeDtypeStruct((nz, own_e, hid, slice_d), bf16)] * 2
        + [jax.ShapeDtypeStruct((n, tokens, quarter), bf16)],
        compiler_params=pltpu.CompilerParams(vmem_limit_bytes=48 * MIB),
        cost_estimate=pl.CostEstimate(
            flops=2 * tokens * n * quarter * wide, bytes_accessed=24 * MIB, transcendentals=0
        ),
    )(idx, hidden, *pieces)


def up_grad_kernel(nz, own_e, hid, seq, slice_d, idx, m_ref, *refs):
    rights, (keep_ref, give_ref) = refs[:4], refs[4:]
    lefts = [
        jnp.concatenate([m_ref[pl.ds(blk * seq, seq), :] for blk in range(odd, nz, 2)], 0)
        for odd in (0, 1)
    ]
    for w in range(2):
        for e in range(own_e):
            at = pl.ds(e * hid, hid)
            total = dot_tn(lefts[0], rights[2 * w][:, at]) + dot_tn(
                lefts[1], rights[2 * w + 1][:, at]
            )
            parts = (total[:slice_d].astype(bf16), total[slice_d:].astype(bf16))
            keep_ref[0, w, e] = jnp.where(idx[1] == 0, parts[0], parts[1])
            give_ref[0, w, e] = jnp.where(idx[1] == 0, parts[1], parts[0])


def up_grad_call(idx, m_all, early, late, own_e, nz, n):
    tokens, quarter = m_all.shape[0], m_all.shape[1] // n
    seq = tokens // nz
    wide = early[0].shape[1]
    hid, slice_d = wide // own_e, quarter // 2
    full = pl.BlockSpec(early[0].shape, lambda k, idx: (0, 0))
    out = pl.BlockSpec(
        (1, 2, own_e, slice_d, hid), lambda k, idx: (k ^ idx[2] ^ idx[0], 0, 0, 0, 0)
    )
    return pl.pallas_call(
        functools.partial(up_grad_kernel, nz, own_e, hid, seq, slice_d),
        grid_spec=pltpu.PrefetchScalarGridSpec(
            num_scalar_prefetch=1,
            grid=(n,),
            in_specs=[pl.BlockSpec((tokens, quarter), lambda k, idx: (0, k))] + [full] * 4,
            out_specs=[out, out],
        ),
        out_shape=[jax.ShapeDtypeStruct((nz, 2, own_e, slice_d, hid), bf16)] * 2,
        compiler_params=pltpu.CompilerParams(vmem_limit_bytes=48 * MIB),
        cost_estimate=pl.CostEstimate(
            flops=4 * tokens * n * quarter * wide, bytes_accessed=24 * MIB, transcendentals=0
        ),
    )(idx, m_all, early[0], late[0], early[1], late[1])


def place_kernel(nz, idx, *refs):
    ups, downs, outs = refs[:nz], refs[nz : 2 * nz], refs[2 * nz :]
    for i in range(nz):

        @pl.when(pl.program_id(0) == i)
        def _(i=i):
            outs[0][...] = ups[i][0].astype(f32)
            outs[1][...] = ups[i][1].astype(f32)
            outs[2][...] = downs[i][...].astype(f32)


def place_call(idx, ups, downs):
    nz = len(ups)
    flat = list(ups) + list(downs)
    fixed = lambda rank: lambda k, idx: (0,) * rank
    shapes = [ups[0].shape[1:], ups[0].shape[1:], downs[0].shape]
    return pl.pallas_call(
        functools.partial(place_kernel, nz),
        grid_spec=pltpu.PrefetchScalarGridSpec(
            num_scalar_prefetch=1,
            grid=(nz,),
            in_specs=[pl.BlockSpec(part.shape, fixed(part.ndim)) for part in flat],
            out_specs=[
                pl.BlockSpec(shape, lambda k, idx: (k ^ idx[0], 0, 0)) for shape in shapes
            ],
        ),
        out_shape=[jax.ShapeDtypeStruct((EXPERTS,) + shape[1:], f32) for shape in shapes],
        compiler_params=pltpu.CompilerParams(vmem_limit_bytes=48 * MIB),
        cost_estimate=pl.CostEstimate(flops=0, bytes_accessed=20 * MIB, transcendentals=0),
    )(idx, *flat)


def shards(
    tokens,
    cotangent,
    routes,
    wq,
    wk,
    wv,
    wo,
    attn_gain,
    q_gain,
    k_gain,
    moe_gain,
    router,
    w_gate,
    w_up,
    w_down,
):
    nz = lax.axis_size("z")
    me_t = lax.axis_index("tensor")
    me_z = lax.axis_index("z")
    me_c = lax.axis_index("core")
    dp = ("z", "core")
    seq, width = tokens.shape
    quarter = width // lax.axis_size("tensor")
    local = wq.shape[1]
    local_heads = local // HEAD_DIM
    slice_d = wq.shape[0]
    own_e = EXPERTS // nz
    hid = w_gate.shape[2]

    idx = jnp.stack([me_z, me_c, me_t]).astype(jnp.int32)

    small = jnp.concatenate([attn_gain[:, None], moe_gain[:, None], router], 1)
    small = jnp.pad(small, ((0, 0), (0, LANES - small.shape[1])))
    packed = lax.all_gather(jnp.concatenate([wq, wk, wv, small], 1), dp, axis=0, tiled=True)
    mask = jnp.sum(
        (routes[:, :, None] == jnp.arange(EXPERTS)[None, None, :]).astype(bf16), 1
    )
    n = width // quarter
    packed, *mask_parts = fence(packed, *spread_z(mask.T))
    mask_all = jnp.stack(mask_parts).transpose(0, 2, 1)
    mask_all = jnp.pad(
        mask_all.reshape(nz * seq, EXPERTS).astype(f32),
        ((0, 0), (FIRST, LANES - EXPERTS - FIRST)),
    )
    wqkv_full = packed[:, : 3 * local]
    small_full = packed[:, 3 * local :]
    a_gain = small_full[:, 0].astype(f32)
    m_gain = small_full[:, 1].astype(f32)
    router_full = small_full[:, FIRST : FIRST + EXPERTS]
    wo_full = lax.all_gather(after(wo, packed), dp, axis=1, tiled=True)

    def fetch(weight, ks):
        pick = lambda k: lax.dynamic_slice_in_dim(weight, (me_z ^ k) * own_e, own_e, 0)
        return [swap(pick(k), "z", k) for k in ks]

    def both_cores(parts):
        parts = jnp.stack(parts)
        return [parts, swap(parts, "core", 1)]

    most, last = range(nz - 1), range(nz - 1, nz)
    cot_parts = spread_z(after(columns(cotangent, me_t, quarter), packed))

    xf = tokens.astype(f32)
    rate_x = lax.rsqrt(jnp.mean(xf * xf, -1, keepdims=True) + EPS)
    gain_q = q_gain.astype(f32)
    gain_k = k_gain.astype(f32)
    a_low = (xf * rate_x * a_gain).astype(bf16)
    qkv = jnp.dot(a_low, wqkv_full, preferred_element_type=f32)
    query, keyed, valued = qkv[:, :local], qkv[:, local : 2 * local], qkv[:, 2 * local :]
    sums = tensor_sum(jnp.stack([jnp.sum(query * query, -1), jnp.sum(keyed * keyed, -1)]))
    rate_q = lax.rsqrt(sums[0] / width + EPS)[:, None]
    rate_k = lax.rsqrt(sums[1] / width + EPS)[:, None]
    cosine, sine = rope_tables(seq, HEAD_DIM)
    heads = (seq, local_heads, HEAD_DIM)
    q_rot = rotate((query * rate_q * gain_q).reshape(heads), cosine, sine).astype(bf16)
    k_rot = rotate((keyed * rate_k * gain_k).reshape(heads), cosine, sine).astype(bf16)
    v_low = valued.reshape(heads).astype(bf16)
    scale = HEAD_DIM ** (-0.5)
    scores = scale * jnp.einsum("qhd,khd->hqk", q_rot, k_rot, preferred_element_type=f32)
    causal = jnp.arange(seq)[:, None] >= jnp.arange(seq)[None, :]
    scores = jnp.where(causal[None], scores, -1e30)
    peak = jnp.max(scores, -1, keepdims=True)
    expd = jnp.exp(scores - peak)
    weights = expd / jnp.sum(expd, -1, keepdims=True)
    weights_low = weights.astype(bf16)
    outputs = jnp.einsum("hqk,khd->qhd", weights_low, v_low, preferred_element_type=f32)
    joined = outputs.reshape(seq, local).astype(bf16)
    wo_full = after(wo_full, joined)
    attn = jnp.dot(joined, wo_full, preferred_element_type=f32).astype(bf16)
    attn, *cot_parts[:-1] = fence(attn, *cot_parts[:-1])
    gate_parts = fetch(after(w_gate, attn), most)

    x_own = columns(xf, me_t, quarter)
    blocks = columns_blocks(attn)
    got = [scatter_first(block, odd) for odd, block in enumerate(blocks)]
    resid = x_own + jnp.concatenate(
        [scatter_third(*scatter_second(b, g, odd)) for odd, (b, g) in enumerate(zip(blocks, got))],
        0,
    )
    rate_r = lax.rsqrt(tensor_sum(jnp.sum(resid * resid, -1)) / width + EPS)[:, None]
    gain_own = lax.dynamic_slice_in_dim(m_gain, me_t * quarter, quarter, 0)
    m_own = (resid * rate_r * gain_own).astype(bf16)

    held = fence(m_own, *gate_parts, *cot_parts)
    m_own, gate_parts, cot_parts = held[0], held[1:nz], held[nz:]
    cot_flat = jnp.concatenate(cot_parts, 0)
    cot_near = spread_tensor_near(cot_flat)
    held = fence(*spread_z(m_own), *cot_near)
    m_parts, cot_near = held[:nz], held[nz:]
    gate_parts += fetch(after(w_gate, m_parts[0]), last)
    up_parts = fetch(after(w_up, m_parts[0]), most)
    m_flat = jnp.concatenate(m_parts, 0)
    m_near = spread_tensor_near(m_flat)
    held = fence(gate_parts[-1], *up_parts, *m_near)
    gate_parts[-1], up_parts, m_near = held[0], held[1:nz], held[nz:]
    gate_parts = both_cores(gate_parts)
    up_parts += fetch(after(w_up, m_near[0]), last)
    up_parts[-1], *pieces = fence(up_parts[-1], m_flat, *m_near, *spread_tensor_cross(m_near))
    up_parts = both_cores(up_parts)
    down_parts = fetch(after(w_down, up_parts[0]), range(nz))
    cot_cross = spread_tensor_cross([after(x, pieces[-1]) for x in cot_near])
    places = [
        [place_of(n, nz * seq // 2, k, i * seq) for k in range(n)] for i in range(nz)
    ]
    router_q = small_full.reshape(-1, quarter, LANES)
    act, up, hidden, probs_all, m_all = forward_call(
        idx, pieces, places, mask_all, router_q, gate_parts, up_parts, nz
    )
    hidden, *held = fence(hidden, *down_parts, *cot_cross)
    down_parts, cot_cross = held[:nz], held[nz:]
    down_parts = both_cores(down_parts)
    down_keep, down_give, cot_all = down_grad_call(
        idx, [cot_flat, *cot_near, *cot_cross], hidden, own_e, nz, n
    )
    cot_all = cot_all.reshape(n, nz, seq, quarter)

    def to_owners(keep, got):
        summed = (keep.astype(f32) + got.astype(f32)).astype(bf16)
        return [swap(summed[k], "z", k) for k in range(nz)]

    down_got = swap(down_give, "core", 1)
    down_own = to_owners(down_keep, down_got)
    half_call = lambda first, probs: backward_call(
        idx, first, cot_all, act, up, probs, mask_all, gate_parts + up_parts + down_parts
    )
    odds, evens = range(1, nz, 2), range(0, nz, 2)
    late = half_call(1, after(probs_all, down_own[0]))
    first = {k: scatter_first(late[0][k // 2], k // 2 % 2) for k in odds}
    held = fence(late[1], *down_own[:-1])
    down_own[:-1] = held[1:]
    early = half_call(0, after(probs_all, *held))
    held = fence(*early, *(first[k] for k in odds), down_own[-1])
    early, got, down_own[-1] = held[:3], dict(zip(odds, held[3:-1])), held[-1]
    second = {k: scatter_second(late[0][k // 2], got[k], k // 2 % 2) for k in odds}
    first = {k: scatter_first(early[0][k // 2], k // 2 % 2) for k in evens}
    up_keep, up_give = up_grad_call(idx, m_all, early[1:3], late[1:3], own_e, nz, n)
    few = [second[k] for k in odds if second[k][1] is not None]
    held = fence(
        up_keep, up_give, *(first[k] for k in evens), *(x[1] for x in few)
    )
    (up_keep, up_give), got = held[:2], dict(zip(evens, held[2:]))
    if few:
        second = {k: (second[k][0], x) for k, x in zip(odds, held[2 + nz // 2 :])}
    near = scatter_z_near({k: scatter_third(*second[k]) for k in odds})
    second = {k: scatter_second(early[0][k // 2], got[k], k // 2 % 2) for k in evens}
    up_got = swap(up_give, "core", 1)
    moe_part = output_call(idx, after(hidden, up_give), down_parts, n, nz)
    few = [second[k][1] for k in evens if second[k][1] is not None]
    near, moe_part, *few = fence(near, moe_part, *few)
    if few:
        second = {k: (second[k][0], x) for k, x in zip(evens, few)}
    dm_own = scatter_z_far({k: scatter_third(*second[k]) for k in evens}, near)
    dgate = jnp.concatenate(
        [dm_own[seq + h * EXPERTS :][:EXPERTS] for h in range(seq // quarter)], 1
    )
    dm_own, up_got = fence(dm_own[:seq], up_got)
    summed = (up_keep.astype(f32) + up_got.astype(f32)).astype(bf16)
    up_own = [swap(summed[k], "z", k) for k in range(nz - 1)] + [None]
    up_last = summed[nz - 1]
    moe_sum = lax.psum_scatter(moe_part, "tensor", scatter_dimension=0, tiled=False)

    dgate = dgate.T
    probs = probs_all[:seq, FIRST : FIRST + EXPERTS]
    dprobs = dgate * mask.astype(f32)
    dlogits = probs * (dprobs - jnp.sum(probs * dprobs, -1, keepdims=True))
    router_own = lax.dynamic_slice_in_dim(router_full, me_t * quarter, quarter, 0)
    router_part = jnp.dot(m_own.astype(f32).T, dlogits, precision=HIGH)
    dm_own = dm_own + jnp.dot(dlogits, router_own.astype(f32).T, precision=HIGH)

    normed = resid * rate_r
    moe_gain_part = jnp.sum(dm_own * normed, 0)
    pulled = dm_own * gain_own
    inner_r = tensor_sum(jnp.sum(pulled * normed, -1))[:, None] / width
    cot_own = columns(cotangent, me_t, quarter).astype(f32)
    dresid = cot_own + rate_r * (pulled - normed * inner_r)
    dresid_low = gather_tensor(dresid.astype(bf16))
    dresid_low, *up_own[:-1] = fence(dresid_low, *up_own[:-1])
    up_own[-1] = swap(after(up_last, dresid_low), "z", nz - 1)
    moe_sum = after(moe_sum, dresid_low)
    moe_own = lax.psum_scatter(moe_sum, "z", scatter_dimension=0, tiled=False)

    wo_grad = jnp.einsum("sd,sa->da", dresid_low, joined, preferred_element_type=f32)
    dout = (
        jnp.einsum("sd,ad->sa", dresid_low, wo_full, preferred_element_type=f32)
        .astype(bf16)
        .reshape(heads)
    )
    dweights = jnp.einsum("qhd,khd->hqk", dout, v_low, preferred_element_type=f32)
    dv = jnp.einsum("hqk,qhd->khd", weights_low, dout, preferred_element_type=f32)
    inner = jnp.sum(weights * dweights, -1, keepdims=True)
    dscores = (weights * (dweights - inner)).astype(bf16)
    dscores, up_own[-1] = fence(dscores, up_own[-1])
    dq_rot = scale * jnp.einsum("hqk,khd->qhd", dscores, k_rot, preferred_element_type=f32)
    dk_rot = scale * jnp.einsum("hqk,qhd->khd", dscores, q_rot, preferred_element_type=f32)
    dq_norm = unrotate(dq_rot, cosine, sine).reshape(seq, local)
    dk_norm = unrotate(dk_rot, cosine, sine).reshape(seq, local)
    inners = tensor_sum(
        jnp.stack(
            [jnp.sum(dq_norm * gain_q * query, -1), jnp.sum(dk_norm * gain_k * keyed, -1)]
        )
    )
    dq_low = (rate_q * gain_q * dq_norm - query * rate_q**3 * inners[0][:, None] / width).astype(
        bf16
    )
    dk_low = (rate_k * gain_k * dk_norm - keyed * rate_k**3 * inners[1][:, None] / width).astype(
        bf16
    )
    dv_low = dv.reshape(seq, local).astype(bf16)
    q_gain_part = jnp.sum(dq_norm * query * rate_q, 0)
    k_gain_part = jnp.sum(dk_norm * keyed * rate_k, 0)
    dqkv = jnp.concatenate([dq_low, dk_low, dv_low], 1)
    smalls = jnp.concatenate(
        [q_gain_part[None], k_gain_part[None], moe_gain_part[None], router_part.T], 0
    )
    dqkv, smalls = fence(dqkv, butterfly_sum(smalls, ("core", "z")))
    half = lax.dynamic_slice_in_dim(smalls[2:], me_c * slice_d, slice_d, 1)
    half = tensor_sum(jnp.where(me_t == me_z, half, 0.0))
    mixed = gather_tensor((after(resid, dqkv) + moe_own.astype(f32)).astype(bf16))
    wqkv_grad = jnp.einsum("sd,sa->da", a_low, dqkv, preferred_element_type=f32).astype(bf16)
    da_part = jnp.einsum("sa,da->sd", dqkv, wqkv_full, preferred_element_type=f32)
    blocks = columns_blocks(da_part.astype(bf16))
    got = [scatter_first(b, odd) for odd, b in enumerate(blocks)]
    expert_grads = place_call(idx, up_own, down_own)
    da_own = jnp.concatenate(
        [scatter_third(*scatter_second(b, g, odd)) for odd, (b, g) in enumerate(zip(blocks, got))],
        0,
    )
    da_own, mixed = fence(da_own, mixed)
    norm_x = x_own * rate_x
    pulled_x = da_own * lax.dynamic_slice_in_dim(a_gain, me_t * quarter, quarter, 0)
    inner_x = tensor_sum(jnp.sum(pulled_x * norm_x, -1))[:, None] / width
    tokens_grad = gather_tensor(
        (dresid + rate_x * (pulled_x - norm_x * inner_x)).astype(bf16)
    )

    both_grads = jnp.concatenate([wqkv_grad, wo_grad.astype(bf16)], 1)
    both_own = lax.psum_scatter(both_grads, dp, scatter_dimension=0, tiled=True)
    tokens_grad, both_own = fence(tokens_grad, both_own)
    both_own = both_own.astype(f32)
    wqkv_own, wo_own = both_own[:, : 3 * local], both_own[:, 3 * local :].T
    attn_gain_grad = jnp.sum(jnp.concatenate([wq, wk, wv], 1).astype(f32) * wqkv_own, -1)
    attn_gain_grad = tensor_sum(attn_gain_grad) / attn_gain.astype(f32)
    return (
        mixed,
        tokens_grad,
        wqkv_own[:, :local],
        wqkv_own[:, local : 2 * local],
        wqkv_own[:, 2 * local : 3 * local],
        wo_own,
        attn_gain_grad,
        smalls[0],
        smalls[1],
        half[0],
        half[1:].T,
        expert_grads[0],
        expert_grads[1],
        expert_grads[2],
    )


def solution(mesh):
    fine = Mesh(
        mesh.devices.reshape(mesh.shape["dp"] // 2, 2, mesh.shape["tensor"]),
        ("z", "core", "tensor"),
    )
    dp = ("z", "core")
    in_specs = (
        P(dp, None),
        P(dp, None),
        P(dp, None),
        P(dp, "tensor"),
        P(dp, "tensor"),
        P(dp, "tensor"),
        P("tensor", dp),
        P(dp),
        P("tensor"),
        P("tensor"),
        P(dp),
        P(dp, None),
        P(None, dp, "tensor"),
        P(None, dp, "tensor"),
        P(None, "tensor", dp),
    )
    out_specs = (
        P(dp, None),
        P(dp, None),
        P(dp, "tensor"),
        P(dp, "tensor"),
        P(dp, "tensor"),
        P("tensor", dp),
        P(dp),
        P("tensor"),
        P("tensor"),
        P(dp),
        P(dp, None),
        P(None, dp, "tensor"),
        P(None, dp, "tensor"),
        P(None, "tensor", dp),
    )
    return jax.shard_map(shards, mesh=fine, in_specs=in_specs, out_specs=out_specs, check_vma=False)
```

```python
import functools

import jax
import jax.numpy as jnp
from jax import lax
from jax.experimental import pallas as pl
from jax.experimental.pallas import tpu as pltpu
from jax.sharding import Mesh
from jax.sharding import PartitionSpec as P

HEAD_DIM = 128
EXPERTS = 16
LANES = 128
FIRST = 2

EPS = 1e-05
THETA = 10000.0
HIGH = lax.Precision.HIGHEST
f32 = jnp.float32
bf16 = jnp.bfloat16
MIB = 1 << 20


def after(value, *earlier):
    return lax.optimization_barrier((value, *earlier))[0]


def fence(*values):
    return list(lax.optimization_barrier(values))


def swap(value, axis, mask):
    if mask == 0:
        return value
    n = lax.axis_size(axis)
    return lax.ppermute(value, axis, [(i, i ^ mask) for i in range(n)])


def bits_of(axis):
    n = lax.axis_size(axis)
    return [1 << b for b in range(n.bit_length() - 1)]


def butterfly_sum(value, axes):
    for axis in axes:
        for bit in bits_of(axis):
            value = value + swap(value, axis, bit)
    return value


def tensor_sum(value):
    return butterfly_sum(value, ("tensor",))


def rope_tables(length, head_dim):
    half = head_dim // 2
    freq = THETA ** (-(jnp.arange(half).astype(f32) * 2.0 / head_dim))
    angle = jnp.arange(length).astype(f32)[:, None] * freq[None, :]
    cosine = jnp.concatenate([jnp.cos(angle), jnp.cos(angle)], -1)
    sine = jnp.concatenate([jnp.sin(angle), jnp.sin(angle)], -1)
    return (cosine, sine)


def rotate(value, cosine, sine):
    half = value.shape[-1] // 2
    turned = jnp.concatenate([-value[..., half:], value[..., :half]], -1)
    return value * cosine[:, None, :] + turned * sine[:, None, :]


def unrotate(grad, cosine, sine):
    half = grad.shape[-1] // 2
    scaled = grad * sine[:, None, :]
    back_turn = jnp.concatenate([scaled[..., half:], -scaled[..., :half]], -1)
    return grad * cosine[:, None, :] + back_turn


def columns(value, index, size):
    return lax.dynamic_slice_in_dim(value, index * size, size, 1)


def spread_z(value):
    parts = {0: value}
    for bit in reversed(bits_of("z")):
        parts.update({k ^ bit: swap(v, "z", bit) for k, v in parts.items()})
    return [parts[k] for k in range(len(parts))]


def spread_tensor_near(value):
    n = lax.axis_size("tensor")
    return [swap(value, "tensor", k) for k in ((1, 2) if n == 4 else range(1, n))]


def spread_tensor_cross(near):
    if lax.axis_size("tensor") != 4:
        return []
    half = near[0].shape[0] // 2
    return [swap(near[0][:half], "tensor", 2), swap(near[1][half:], "tensor", 1)]


def place_of(n, half, k, row):
    if n != 4 or k < 3:
        return (k, row)
    return (3, row) if row < half else (4, row - half)


def spread_tensor_far(value, near):
    if lax.axis_size("tensor") != 4:
        return jnp.stack([value, *near])
    half = value.shape[0] // 2
    cross = [swap(near[0][:half], "tensor", 2), swap(near[1][half:], "tensor", 1)]
    return jnp.stack([value, *near, jnp.concatenate(cross, 0)])


def spread_tensor(value):
    return spread_tensor_far(value, spread_tensor_near(value))


def gather_tensor(value):
    me, n = lax.axis_index("tensor"), lax.axis_size("tensor")
    rows, width = value.shape
    out = jnp.zeros((rows, n * width), value.dtype)
    parts = spread_tensor(value)
    for k in range(n):
        part = parts[k]
        out = lax.dynamic_update_slice(out, part, (0, (me ^ k) * width))
    return out


def order_of(n, odd):
    if n != 4:
        return tuple(range(n))
    return (0, 1, 2, 3) if odd else (0, 2, 1, 3)


def scatter_first(block, odd):
    n = block.shape[0]
    if n != 4:
        return jnp.stack([swap(block[k], "tensor", k) for k in range(1, n)])
    return swap(block[2:], "tensor", 2 if odd else 1)


def scatter_second(block, got, odd):
    got = got.astype(f32)
    mine = block[0].astype(f32)
    if block.shape[0] != 4:
        return mine + jnp.sum(got, 0), None
    other = (block[1].astype(f32) + got[1]).astype(bf16)
    return mine + got[0], swap(other, "tensor", 1 if odd else 2)


def scatter_third(mine, got):
    return mine if got is None else mine + got.astype(f32)


def scatter_z_near(parts):
    return swap(jnp.stack([parts[k].astype(bf16) for k in sorted(parts)]), "z", 1)


def scatter_z_far(parts, got):
    parts = {k: parts[k] + got[i].astype(f32) for i, k in enumerate(sorted(parts))}
    for bit in bits_of("z")[1:]:
        away = sorted(k for k in parts if k & bit)
        got = swap(jnp.stack([parts[k].astype(bf16) for k in away]), "z", bit)
        parts = {k ^ bit: parts[k ^ bit] + got[i].astype(f32) for i, k in enumerate(away)}
    return parts[0]


def columns_blocks(value):
    me, n = lax.axis_index("tensor"), lax.axis_size("tensor")
    rows, width = value.shape[0], value.shape[1] // n
    half = rows // 2
    return [
        jnp.stack(
            [
                columns(value[odd * half : (odd + 1) * half], me ^ k, width)
                for k in order_of(n, odd)
            ]
        )
        for odd in (0, 1)
    ]


def dot_nn(a, b):
    return lax.dot_general(a, b, (((1,), (0,)), ((), ())), preferred_element_type=f32)


def dot_nt(a, b):
    return lax.dot_general(a, b, (((1,), (1,)), ((), ())), preferred_element_type=f32)


def dot_tn(a, b):
    return lax.dot_general(a, b, (((0,), (0,)), ((), ())), preferred_element_type=f32)


def weight_copies(nz, slice_d, own_e, idx, parts, whole, sems, down):
    copies = []
    for c in range(2):
        for k in range(nz):
            half = pl.multiple_of((idx[1] ^ c) * slice_d, slice_d)
            at = pl.multiple_of((idx[0] ^ k ^ idx[2]) * 2 * slice_d, slice_d) + half
            if down:
                copies.append((parts[c].at[k], whole.at[:, :, pl.ds(at, slice_d)]))
            else:
                hid = whole.shape[1] // own_e
                for e in range(own_e):
                    target = whole.at[pl.ds(at, slice_d), pl.ds(e * hid, hid)]
                    copies.append((parts[c].at[k, e], target))
    return [pltpu.make_async_copy(*pair, sems.at[j]) for j, pair in enumerate(copies)]


def start(copies):
    for copy in copies:
        copy.start()


def finish(copies):
    for copy in copies:
        copy.wait()


def own_gate(gates, lane, me_z, own_e, e):
    return jnp.sum(jnp.where(lane == FIRST + me_z * own_e + e, gates, 0.0), -1, keepdims=True)


def forward_kernel(nz, n, own_e, hid, slice_d, seq, quarter, places, idx, *refs):
    mask_ref, router_ref = refs[:2]
    gate_parts, up_parts, m_refs = refs[2:4], refs[4:6], refs[6:-11]
    act_ref, up_ref, hid_ref, probs_ref, m_out, w_gate, w_up, m_full, *sems = refs[-11:]
    gate_sems, up_sems, m_sems = sems
    me_z, me_t = idx[0], idx[2]
    step = pl.program_id(0)
    first = step == 0
    m_copies = [
        [
            pltpu.make_async_copy(
                m_refs[j].at[pl.ds(row, seq), :],
                m_full.at[pl.ds(i * seq, seq), pl.ds(k * quarter, quarter)],
                m_sems.at[i, k],
            )
            for k, (j, row) in enumerate(places[i])
        ]
        for i in range(nz)
    ]
    gate_copies = weight_copies(nz, slice_d, own_e, idx, gate_parts, w_gate, gate_sems, False)
    up_copies = weight_copies(nz, slice_d, own_e, idx, up_parts, w_up, up_sems, False)

    @pl.when(first)
    def _():
        start(m_copies[0] + gate_copies + up_copies)
        for copies in m_copies[1:]:
            start(copies)

    for i in range(nz):

        @pl.when(step == i)
        def _(i=i):
            finish(m_copies[i])

    rows = seq
    m_block = m_full[pl.ds(pl.multiple_of(step * seq, seq), seq), :]
    m_out[...] = m_block
    lane = lax.broadcasted_iota(jnp.int32, (rows, LANES), 1)
    logits = jnp.zeros((rows, LANES), f32)
    for k in range(n):
        logits += dot_nn(m_block[:, k * quarter : (k + 1) * quarter], router_ref[me_t ^ k])
    named = (lane >= FIRST) & (lane < FIRST + EXPERTS)
    logits = jnp.where(named, logits, -1e30)
    expd = jnp.where(named, jnp.exp(logits - jnp.max(logits, -1, keepdims=True)), 0.0)
    probs = expd / jnp.sum(expd, -1, keepdims=True)
    probs_ref[...] = probs
    gates = probs * mask_ref[...]

    @pl.when(first)
    def _():
        finish(gate_copies)

    for e in range(own_e):
        at = pl.ds(e * hid, hid)
        act_ref[:, at] = dot_nn(m_block, w_gate[:, at])

    @pl.when(first)
    def _():
        finish(up_copies)

    for e in range(own_e):
        at = pl.ds(e * hid, hid)
        up = dot_nn(m_block, w_up[:, at])
        up_ref[:, at] = up
        act = act_ref[:, at]
        gate = own_gate(gates, lane, me_z, own_e, e)
        hid_ref[:, at] = (gate * (act * jax.nn.sigmoid(act) * up)).astype(bf16)


def forward_call(idx, pieces, places, mask_all, router_q, gate_parts, up_parts, nz):
    n, quarter = router_q.shape[:2]
    tokens = mask_all.shape[0]
    seq = tokens // nz
    own_e, slice_d, hid = up_parts[0].shape[1:]
    wide = own_e * hid
    here = lambda i, idx: (i, 0)
    return pl.pallas_call(
        functools.partial(forward_kernel, nz, n, own_e, hid, slice_d, seq, quarter, places),
        grid_spec=pltpu.PrefetchScalarGridSpec(
            num_scalar_prefetch=1,
            grid=(nz,),
            in_specs=[
                pl.BlockSpec((seq, LANES), here),
                pl.BlockSpec((n, quarter, LANES), lambda i, idx: (0, 0, 0)),
            ]
            + [pl.BlockSpec(memory_space=pl.ANY)] * (4 + len(pieces)),
            out_specs=[
                pl.BlockSpec((seq, wide), here),
                pl.BlockSpec((seq, wide), here),
                pl.BlockSpec((seq, wide), here),
                pl.BlockSpec((seq, LANES), here),
                pl.BlockSpec((seq, n * quarter), here),
            ],
            scratch_shapes=[
                pltpu.VMEM((n * quarter, wide), bf16),
                pltpu.VMEM((n * quarter, wide), bf16),
                pltpu.VMEM((tokens, n * quarter), bf16),
                pltpu.SemaphoreType.DMA((2 * nz * own_e,)),
                pltpu.SemaphoreType.DMA((2 * nz * own_e,)),
                pltpu.SemaphoreType.DMA((nz, n)),
            ],
        ),
        out_shape=[
            jax.ShapeDtypeStruct((tokens, wide), f32),
            jax.ShapeDtypeStruct((tokens, wide), f32),
            jax.ShapeDtypeStruct((tokens, wide), bf16),
            jax.ShapeDtypeStruct((tokens, LANES), f32),
            jax.ShapeDtypeStruct((tokens, n * quarter), bf16),
        ],
        compiler_params=pltpu.CompilerParams(vmem_limit_bytes=56 * MIB),
        cost_estimate=pl.CostEstimate(
            flops=4 * tokens * n * quarter * wide, bytes_accessed=40 * MIB, transcendentals=0
        ),
    )(idx, mask_all, router_q, *gate_parts, *up_parts, *pieces)


def backward_kernel(nz, n, own_e, hid, slice_d, quarter, idx, *refs):
    g_ref, act_ref, up_ref, probs_ref, mask_ref = refs[:5]
    dx_ref, dg_ref, du_ref, w_gate, w_up, w_down, gate_sems, up_sems, down_sems = refs[11:]
    i = pl.program_id(0)
    me_z = idx[0]
    gate_copies = weight_copies(nz, slice_d, own_e, idx, refs[5:7], w_gate, gate_sems, False)
    up_copies = weight_copies(nz, slice_d, own_e, idx, refs[7:9], w_up, up_sems, False)
    down_copies = weight_copies(nz, slice_d, own_e, idx, refs[9:11], w_down, down_sems, True)

    @pl.when(i == 0)
    def _():
        start(down_copies + gate_copies + up_copies)
        finish(down_copies)

    rows = act_ref.shape[0]
    lane = lax.broadcasted_iota(jnp.int32, (rows, LANES), 1)
    gates = probs_ref[...] * mask_ref[...]
    dgate = jnp.zeros((rows, LANES), f32)
    g_block = jnp.concatenate([g_ref[q, 0] for q in range(n)], 1)
    for e in range(own_e):
        gate = own_gate(gates, lane, me_z, own_e, e)
        at = pl.ds(e * hid, hid)
        back = dot_nt(g_block, w_down[e])
        act = act_ref[:, at]
        up = up_ref[:, at]
        sigma = jax.nn.sigmoid(act)
        silu = act * sigma
        dgate = jnp.where(
            lane == me_z * own_e + e, jnp.sum(silu * up * back, -1, keepdims=True), dgate
        )
        back = gate * back
        dg_ref[:, at] = (back * up * sigma * (1.0 + act * (1.0 - sigma))).astype(bf16)
        du_ref[:, at] = (back * silu).astype(bf16)
    dgate = jnp.transpose(dgate)[:EXPERTS].astype(bf16)

    @pl.when(i == 0)
    def _():
        finish(gate_copies + up_copies)

    even, odd = order_of(n, 0), order_of(n, 1)
    for j in range(n):
        k = jnp.where(i % 2 == 0, even[j], odd[j])
        at = pl.ds(pl.multiple_of(k * quarter, quarter), quarter)
        total = dot_nt(dg_ref[...], w_gate[at, :]) + dot_nt(du_ref[...], w_up[at, :])
        dx_ref[0, j, pl.ds(0, rows), :] = total.astype(bf16)
        for h in range(rows // quarter):
            dx_ref[0, j, pl.ds(rows + h * EXPERTS, EXPERTS), :] = dgate[
                :, h * quarter : (h + 1) * quarter
            ]


def backward_call(idx, first, g_all, act, up, probs, mask_all, weights):
    n, nz, seq, quarter = g_all.shape
    own_e, slice_d, hid = weights[0].shape[1:]
    blocks = nz // 2
    wide = own_e * hid
    tall = seq + EXPERTS * (seq // quarter)
    some = lambda i, idx: (2 * i + first, 0)
    here = lambda i, idx: (i, 0)
    hbm = pl.BlockSpec(memory_space=pl.ANY)
    return pl.pallas_call(
        functools.partial(backward_kernel, nz, n, own_e, hid, slice_d, quarter),
        grid_spec=pltpu.PrefetchScalarGridSpec(
            num_scalar_prefetch=1,
            grid=(blocks,),
            in_specs=[
                pl.BlockSpec((n, 1, seq, quarter), lambda i, idx: (0, 2 * i + first, 0, 0)),
                pl.BlockSpec((seq, wide), some),
                pl.BlockSpec((seq, wide), some),
                pl.BlockSpec((seq, LANES), some),
                pl.BlockSpec((seq, LANES), some),
            ]
            + [hbm] * 6,
            out_specs=[
                pl.BlockSpec((1, n, tall, quarter), lambda i, idx: (i, 0, 0, 0)),
                pl.BlockSpec((seq, wide), here),
                pl.BlockSpec((seq, wide), here),
            ],
            scratch_shapes=[
                pltpu.VMEM((n * quarter, wide), bf16),
                pltpu.VMEM((n * quarter, wide), bf16),
                pltpu.VMEM((own_e, hid, n * quarter), bf16),
                pltpu.SemaphoreType.DMA((2 * nz * own_e,)),
                pltpu.SemaphoreType.DMA((2 * nz * own_e,)),
                pltpu.SemaphoreType.DMA((2 * nz,)),
            ],
        ),
        out_shape=[
            jax.ShapeDtypeStruct((blocks, n, tall, quarter), bf16),
            jax.ShapeDtypeStruct((blocks * seq, wide), bf16),
            jax.ShapeDtypeStruct((blocks * seq, wide), bf16),
        ],
        compiler_params=pltpu.CompilerParams(vmem_limit_bytes=56 * MIB),
        cost_estimate=pl.CostEstimate(
            flops=6 * blocks * seq * n * quarter * wide,
            bytes_accessed=40 * MIB,
            transcendentals=0,
        ),
    )(idx, g_all, act, up, probs, mask_all, *weights)


def output_kernel(nz, own_e, hid, slice_d, quarter, idx, hid_ref, near, far, y_ref, w_down, sems):
    i, j = pl.program_id(0), pl.program_id(1)

    @pl.when((i == 0) & (j == 0))
    def _():
        copies = weight_copies(nz, slice_d, own_e, idx, (near, far), w_down, sems, True)
        start(copies)
        finish(copies)

    at = pl.ds(pl.multiple_of(j * quarter, quarter), quarter)
    part = w_down[:, :, at].reshape(own_e * hid, quarter)
    y_ref[0, 0] = dot_nn(hid_ref[...], part).astype(bf16)


def output_call(idx, hidden, parts, n, nz):
    tokens, wide = hidden.shape
    seq = tokens // nz
    own_e, hid, slice_d = parts[0].shape[1:]
    quarter = 2 * slice_d
    return pl.pallas_call(
        functools.partial(output_kernel, nz, own_e, hid, slice_d, quarter),
        grid_spec=pltpu.PrefetchScalarGridSpec(
            num_scalar_prefetch=1,
            grid=(nz, n),
            in_specs=[pl.BlockSpec((seq, wide), lambda i, j, idx: (i, 0))]
            + [pl.BlockSpec(memory_space=pl.ANY)] * 2,
            out_specs=pl.BlockSpec(
                (1, 1, seq, quarter), lambda i, j, idx: (j ^ idx[2], i ^ idx[0], 0, 0)
            ),
            scratch_shapes=[
                pltpu.VMEM((own_e, hid, n * quarter), bf16),
                pltpu.SemaphoreType.DMA((2 * nz,)),
            ],
        ),
        out_shape=jax.ShapeDtypeStruct((n, nz, seq, quarter), bf16),
        compiler_params=pltpu.CompilerParams(vmem_limit_bytes=48 * MIB),
        cost_estimate=pl.CostEstimate(
            flops=2 * tokens * n * quarter * wide, bytes_accessed=16 * MIB, transcendentals=0
        ),
    )(idx, hidden, *parts)


def down_grad_kernel(nz, n, own_e, hid, seq, slice_d, idx, hid_ref, *refs):
    g_refs, (keep_ref, give_ref, g_out, g_full, sems) = refs[:-5], refs[-5:]
    step = pl.program_id(0)
    copies = []
    for k in range(n):
        copies.append([])
        for i in range(nz):
            j, row = place_of(n, nz * seq // 2, k, i * seq)
            copies[k].append(
                pltpu.make_async_copy(
                    g_refs[j].at[pl.ds(row, seq), :],
                    g_full.at[k, pl.ds(i * seq, seq), :],
                    sems.at[k, i],
                )
            )

    @pl.when(step == 0)
    def _():
        for some in copies:
            start(some)

    for k in range(n):

        @pl.when(step == k)
        def _(k=k):
            finish(copies[k])

    g_block = g_full[step]
    g_out[0] = g_block
    total = dot_tn(g_block, hid_ref[...])
    halves = (total[:slice_d], total[slice_d:])
    for e in range(own_e):
        parts = [jnp.transpose(half[:, e * hid : (e + 1) * hid]).astype(bf16) for half in halves]
        keep_ref[0, e] = jnp.where(idx[1] == 0, parts[0], parts[1])
        give_ref[0, e] = jnp.where(idx[1] == 0, parts[1], parts[0])


def down_grad_call(idx, pieces, hidden, own_e, nz, n):
    tokens, wide = hidden.shape
    quarter, seq = pieces[0].shape[1], tokens // nz
    hid, slice_d = wide // own_e, quarter // 2
    out = pl.BlockSpec((1, own_e, hid, slice_d), lambda k, idx: (k ^ idx[2] ^ idx[0], 0, 0, 0))
    return pl.pallas_call(
        functools.partial(down_grad_kernel, nz, n, own_e, hid, seq, slice_d),
        grid_spec=pltpu.PrefetchScalarGridSpec(
            num_scalar_prefetch=1,
            grid=(n,),
            in_specs=[pl.BlockSpec((tokens, wide), lambda k, idx: (0, 0))]
            + [pl.BlockSpec(memory_space=pl.ANY)] * len(pieces),
            out_specs=[out, out, pl.BlockSpec((1, tokens, quarter), lambda k, idx: (k, 0, 0))],
            scratch_shapes=[
                pltpu.VMEM((n, tokens, quarter), bf16),
                pltpu.SemaphoreType.DMA((n, nz)),
            ],
        ),
        out_shape=[jax.ShapeDtypeStruct((nz, own_e, hid, slice_d), bf16)] * 2
        + [jax.ShapeDtypeStruct((n, tokens, quarter), bf16)],
        compiler_params=pltpu.CompilerParams(vmem_limit_bytes=48 * MIB),
        cost_estimate=pl.CostEstimate(
            flops=2 * tokens * n * quarter * wide, bytes_accessed=24 * MIB, transcendentals=0
        ),
    )(idx, hidden, *pieces)


def up_grad_kernel(nz, own_e, hid, seq, slice_d, idx, m_ref, *refs):
    rights, (keep_ref, give_ref) = refs[:4], refs[4:]
    lefts = [
        jnp.concatenate([m_ref[pl.ds(blk * seq, seq), :] for blk in range(odd, nz, 2)], 0)
        for odd in (0, 1)
    ]
    for w in range(2):
        for e in range(own_e):
            at = pl.ds(e * hid, hid)
            total = dot_tn(lefts[0], rights[2 * w][:, at]) + dot_tn(
                lefts[1], rights[2 * w + 1][:, at]
            )
            parts = (total[:slice_d].astype(bf16), total[slice_d:].astype(bf16))
            keep_ref[0, w, e] = jnp.where(idx[1] == 0, parts[0], parts[1])
            give_ref[0, w, e] = jnp.where(idx[1] == 0, parts[1], parts[0])


def up_grad_call(idx, m_all, early, late, own_e, nz, n):
    tokens, quarter = m_all.shape[0], m_all.shape[1] // n
    seq = tokens // nz
    wide = early[0].shape[1]
    hid, slice_d = wide // own_e, quarter // 2
    full = pl.BlockSpec(early[0].shape, lambda k, idx: (0, 0))
    out = pl.BlockSpec(
        (1, 2, own_e, slice_d, hid), lambda k, idx: (k ^ idx[2] ^ idx[0], 0, 0, 0, 0)
    )
    return pl.pallas_call(
        functools.partial(up_grad_kernel, nz, own_e, hid, seq, slice_d),
        grid_spec=pltpu.PrefetchScalarGridSpec(
            num_scalar_prefetch=1,
            grid=(n,),
            in_specs=[pl.BlockSpec((tokens, quarter), lambda k, idx: (0, k))] + [full] * 4,
            out_specs=[out, out],
        ),
        out_shape=[jax.ShapeDtypeStruct((nz, 2, own_e, slice_d, hid), bf16)] * 2,
        compiler_params=pltpu.CompilerParams(vmem_limit_bytes=48 * MIB),
        cost_estimate=pl.CostEstimate(
            flops=4 * tokens * n * quarter * wide, bytes_accessed=24 * MIB, transcendentals=0
        ),
    )(idx, m_all, early[0], late[0], early[1], late[1])


def place_kernel(nz, idx, *refs):
    ups, downs, outs = refs[:nz], refs[nz : 2 * nz], refs[2 * nz :]
    for i in range(nz):

        @pl.when(pl.program_id(0) == i)
        def _(i=i):
            outs[0][...] = ups[i][0].astype(f32)
            outs[1][...] = ups[i][1].astype(f32)
            outs[2][...] = downs[i][...].astype(f32)


def place_call(idx, ups, downs):
    nz = len(ups)
    flat = list(ups) + list(downs)
    fixed = lambda rank: lambda k, idx: (0,) * rank
    shapes = [ups[0].shape[1:], ups[0].shape[1:], downs[0].shape]
    return pl.pallas_call(
        functools.partial(place_kernel, nz),
        grid_spec=pltpu.PrefetchScalarGridSpec(
            num_scalar_prefetch=1,
            grid=(nz,),
            in_specs=[pl.BlockSpec(part.shape, fixed(part.ndim)) for part in flat],
            out_specs=[
                pl.BlockSpec(shape, lambda k, idx: (k ^ idx[0], 0, 0)) for shape in shapes
            ],
        ),
        out_shape=[jax.ShapeDtypeStruct((EXPERTS,) + shape[1:], f32) for shape in shapes],
        compiler_params=pltpu.CompilerParams(vmem_limit_bytes=48 * MIB),
        cost_estimate=pl.CostEstimate(flops=0, bytes_accessed=20 * MIB, transcendentals=0),
    )(idx, *flat)


def shards(
    tokens,
    cotangent,
    routes,
    wq,
    wk,
    wv,
    wo,
    attn_gain,
    q_gain,
    k_gain,
    moe_gain,
    router,
    w_gate,
    w_up,
    w_down,
):
    nz = lax.axis_size("z")
    me_t = lax.axis_index("tensor")
    me_z = lax.axis_index("z")
    me_c = lax.axis_index("core")
    dp = ("z", "core")
    seq, width = tokens.shape
    quarter = width // lax.axis_size("tensor")
    local = wq.shape[1]
    local_heads = local // HEAD_DIM
    slice_d = wq.shape[0]
    own_e = EXPERTS // nz
    hid = w_gate.shape[2]

    idx = jnp.stack([me_z, me_c, me_t]).astype(jnp.int32)

    small = jnp.concatenate([attn_gain[:, None], moe_gain[:, None], router], 1)
    small = jnp.pad(small, ((0, 0), (0, LANES - small.shape[1])))
    packed = lax.all_gather(jnp.concatenate([wq, wk, wv, small], 1), dp, axis=0, tiled=True)
    mask = jnp.sum(
        (routes[:, :, None] == jnp.arange(EXPERTS)[None, None, :]).astype(bf16), 1
    )
    n = width // quarter
    packed, *mask_parts = fence(packed, *spread_z(mask.T))
    mask_all = jnp.stack(mask_parts).transpose(0, 2, 1)
    mask_all = jnp.pad(
        mask_all.reshape(nz * seq, EXPERTS).astype(f32),
        ((0, 0), (FIRST, LANES - EXPERTS - FIRST)),
    )
    wqkv_full = packed[:, : 3 * local]
    small_full = packed[:, 3 * local :]
    a_gain = small_full[:, 0].astype(f32)
    m_gain = small_full[:, 1].astype(f32)
    router_full = small_full[:, FIRST : FIRST + EXPERTS]
    wo_full = lax.all_gather(after(wo, packed), dp, axis=1, tiled=True)

    def fetch(weight, ks):
        pick = lambda k: lax.dynamic_slice_in_dim(weight, (me_z ^ k) * own_e, own_e, 0)
        return [swap(pick(k), "z", k) for k in ks]

    def both_cores(parts):
        parts = jnp.stack(parts)
        return [parts, swap(parts, "core", 1)]

    most, last = range(nz - 1), range(nz - 1, nz)
    cot_parts = spread_z(after(columns(cotangent, me_t, quarter), packed))

    xf = tokens.astype(f32)
    rate_x = lax.rsqrt(jnp.mean(xf * xf, -1, keepdims=True) + EPS)
    gain_q = q_gain.astype(f32)
    gain_k = k_gain.astype(f32)
    a_low = (xf * rate_x * a_gain).astype(bf16)
    qkv = jnp.dot(a_low, wqkv_full, preferred_element_type=f32)
    query, keyed, valued = qkv[:, :local], qkv[:, local : 2 * local], qkv[:, 2 * local :]
    sums = tensor_sum(jnp.stack([jnp.sum(query * query, -1), jnp.sum(keyed * keyed, -1)]))
    rate_q = lax.rsqrt(sums[0] / width + EPS)[:, None]
    rate_k = lax.rsqrt(sums[1] / width + EPS)[:, None]
    cosine, sine = rope_tables(seq, HEAD_DIM)
    heads = (seq, local_heads, HEAD_DIM)
    q_rot = rotate((query * rate_q * gain_q).reshape(heads), cosine, sine).astype(bf16)
    k_rot = rotate((keyed * rate_k * gain_k).reshape(heads), cosine, sine).astype(bf16)
    v_low = valued.reshape(heads).astype(bf16)
    scale = HEAD_DIM ** (-0.5)
    scores = scale * jnp.einsum("qhd,khd->hqk", q_rot, k_rot, preferred_element_type=f32)
    causal = jnp.arange(seq)[:, None] >= jnp.arange(seq)[None, :]
    scores = jnp.where(causal[None], scores, -1e30)
    peak = jnp.max(scores, -1, keepdims=True)
    expd = jnp.exp(scores - peak)
    weights = expd / jnp.sum(expd, -1, keepdims=True)
    weights_low = weights.astype(bf16)
    outputs = jnp.einsum("hqk,khd->qhd", weights_low, v_low, preferred_element_type=f32)
    joined = outputs.reshape(seq, local).astype(bf16)
    wo_full = after(wo_full, joined)
    attn = jnp.dot(joined, wo_full, preferred_element_type=f32).astype(bf16)
    attn, *cot_parts[:-1] = fence(attn, *cot_parts[:-1])
    gate_parts = fetch(after(w_gate, attn), most)

    x_own = columns(xf, me_t, quarter)
    blocks = columns_blocks(attn)
    got = [scatter_first(block, odd) for odd, block in enumerate(blocks)]
    resid = x_own + jnp.concatenate(
        [scatter_third(*scatter_second(b, g, odd)) for odd, (b, g) in enumerate(zip(blocks, got))],
        0,
    )
    rate_r = lax.rsqrt(tensor_sum(jnp.sum(resid * resid, -1)) / width + EPS)[:, None]
    gain_own = lax.dynamic_slice_in_dim(m_gain, me_t * quarter, quarter, 0)
    m_own = (resid * rate_r * gain_own).astype(bf16)

    held = fence(m_own, *gate_parts, *cot_parts)
    m_own, gate_parts, cot_parts = held[0], held[1:nz], held[nz:]
    cot_flat = jnp.concatenate(cot_parts, 0)
    cot_near = spread_tensor_near(cot_flat)
    held = fence(*spread_z(m_own), *cot_near)
    m_parts, cot_near = held[:nz], held[nz:]
    gate_parts += fetch(after(w_gate, m_parts[0]), last)
    up_parts = fetch(after(w_up, m_parts[0]), most)
    m_flat = jnp.concatenate(m_parts, 0)
    m_near = spread_tensor_near(m_flat)
    held = fence(gate_parts[-1], *up_parts, *m_near)
    gate_parts[-1], up_parts, m_near = held[0], held[1:nz], held[nz:]
    gate_parts = both_cores(gate_parts)
    up_parts += fetch(after(w_up, m_near[0]), last)
    held = fence(m_flat, *m_near, *spread_tensor_cross(m_near), up_parts[-1])
    up_parts[-1], pieces = held[-1], held[:-1]
    up_parts = both_cores(up_parts)
    down_parts = fetch(after(w_down, up_parts[0]), range(nz))
    cot_cross = spread_tensor_cross([after(x, pieces[-1]) for x in cot_near])
    places = [
        [place_of(n, nz * seq // 2, k, i * seq) for k in range(n)] for i in range(nz)
    ]
    router_q = small_full.reshape(-1, quarter, LANES)
    act, up, hidden, probs_all, m_all = forward_call(
        idx, pieces, places, mask_all, router_q, gate_parts, up_parts, nz
    )
    hidden, *cot_cross = fence(hidden, *cot_cross)
    down_keep, down_give, cot_all = down_grad_call(
        idx, [cot_flat, *cot_near, *cot_cross], hidden, own_e, nz, n
    )
    cot_all = cot_all.reshape(n, nz, seq, quarter)

    def to_owners(keep, got):
        summed = (keep.astype(f32) + got.astype(f32)).astype(bf16)
        return [swap(summed[k], "z", k) for k in range(nz)]

    down_give, *down_parts = fence(down_give, *down_parts)
    down_parts = both_cores(down_parts)
    down_got = swap(down_give, "core", 1)
    half_call = lambda first, probs: backward_call(
        idx, first, cot_all, act, up, probs, mask_all, gate_parts + up_parts + down_parts
    )
    odds, evens = range(1, nz, 2), range(0, nz, 2)
    late = half_call(1, after(probs_all, down_give))
    first = {k: scatter_first(late[0][k // 2], k // 2 % 2) for k in odds}
    down_own = to_owners(after(down_keep, late[1]), down_got)
    early = half_call(0, after(probs_all, late[1], down_own[0]))
    held = fence(*early, *down_own[:-1], *(first[k] for k in odds))
    early, down_own[:-1] = held[:3], held[3 : 2 + nz]
    got = dict(zip(odds, held[2 + nz :]))
    second = {k: scatter_second(late[0][k // 2], got[k], k // 2 % 2) for k in odds}
    first = {k: scatter_first(early[0][k // 2], k // 2 % 2) for k in evens}
    up_keep, up_give = up_grad_call(idx, m_all, early[1:3], late[1:3], own_e, nz, n)
    few = [second[k] for k in odds if second[k][1] is not None]
    held = fence(
        up_keep,
        up_give,
        down_own[-1],
        *(first[k] for k in evens),
        *(x[1] for x in few),
    )
    (up_keep, up_give, down_own[-1]), got = held[:3], dict(zip(evens, held[3:]))
    if few:
        second = {k: (second[k][0], x) for k, x in zip(odds, held[3 + nz // 2 :])}
    near = scatter_z_near({k: scatter_third(*second[k]) for k in odds})
    second = {k: scatter_second(early[0][k // 2], got[k], k // 2 % 2) for k in evens}
    up_got = swap(up_give, "core", 1)
    moe_part = output_call(idx, after(hidden, up_give), down_parts, n, nz)
    few = [second[k][1] for k in evens if second[k][1] is not None]
    near, moe_part, *few = fence(near, moe_part, *few)
    if few:
        second = {k: (second[k][0], x) for k, x in zip(evens, few)}
    dm_own = scatter_z_far({k: scatter_third(*second[k]) for k in evens}, near)
    dgate = jnp.concatenate(
        [dm_own[seq + h * EXPERTS :][:EXPERTS] for h in range(seq // quarter)], 1
    )
    dm_own, up_got = fence(dm_own[:seq], up_got)
    summed = (up_keep.astype(f32) + up_got.astype(f32)).astype(bf16)
    up_own = [swap(summed[k], "z", k) for k in range(nz - 1)] + [None]
    up_last = summed[nz - 1]
    moe_sum = lax.psum_scatter(moe_part, "tensor", scatter_dimension=0, tiled=False)

    dgate = dgate.T
    probs = probs_all[:seq, FIRST : FIRST + EXPERTS]
    dprobs = dgate * mask.astype(f32)
    dlogits = probs * (dprobs - jnp.sum(probs * dprobs, -1, keepdims=True))
    router_own = lax.dynamic_slice_in_dim(router_full, me_t * quarter, quarter, 0)
    router_part = jnp.dot(m_own.astype(f32).T, dlogits, precision=HIGH)
    dm_own = dm_own + jnp.dot(dlogits, router_own.astype(f32).T, precision=HIGH)

    normed = resid * rate_r
    moe_gain_part = jnp.sum(dm_own * normed, 0)
    pulled = dm_own * gain_own
    inner_r = tensor_sum(jnp.sum(pulled * normed, -1))[:, None] / width
    cot_own = columns(cotangent, me_t, quarter).astype(f32)
    dresid = cot_own + rate_r * (pulled - normed * inner_r)
    dresid_low = gather_tensor(dresid.astype(bf16))
    dresid_low, *up_own[:-1] = fence(dresid_low, *up_own[:-1])
    up_own[-1] = swap(after(up_last, dresid_low), "z", nz - 1)
    moe_sum = after(moe_sum, dresid_low)
    moe_parts = {
        k: lax.dynamic_index_in_dim(moe_sum, me_z ^ k, 0, keepdims=False) for k in range(nz)
    }
    moe_near = scatter_z_near({k: moe_parts[k] for k in range(1, nz, 2)})

    wo_grad = jnp.einsum("sa,sd->ad", joined, dresid_low, preferred_element_type=f32)
    wo_own = lax.psum_scatter(wo_grad.astype(bf16), dp, scatter_dimension=1, tiled=True)
    dout = (
        jnp.einsum("sd,ad->sa", dresid_low, wo_full, preferred_element_type=f32)
        .astype(bf16)
        .reshape(heads)
    )
    dweights = jnp.einsum("qhd,khd->hqk", dout, v_low, preferred_element_type=f32)
    dv = jnp.einsum("hqk,qhd->khd", weights_low, dout, preferred_element_type=f32)
    inner = jnp.sum(weights * dweights, -1, keepdims=True)
    dscores = (weights * (dweights - inner)).astype(bf16)
    dscores, up_own[-1], moe_near = fence(dscores, up_own[-1], moe_near)
    dq_rot = scale * jnp.einsum("hqk,khd->qhd", dscores, k_rot, preferred_element_type=f32)
    dk_rot = scale * jnp.einsum("hqk,qhd->khd", dscores, q_rot, preferred_element_type=f32)
    dq_norm = unrotate(dq_rot, cosine, sine).reshape(seq, local)
    dk_norm = unrotate(dk_rot, cosine, sine).reshape(seq, local)
    inners = tensor_sum(
        jnp.stack(
            [jnp.sum(dq_norm * gain_q * query, -1), jnp.sum(dk_norm * gain_k * keyed, -1)]
        )
    )
    dq_low = (rate_q * gain_q * dq_norm - query * rate_q**3 * inners[0][:, None] / width).astype(
        bf16
    )
    dk_low = (rate_k * gain_k * dk_norm - keyed * rate_k**3 * inners[1][:, None] / width).astype(
        bf16
    )
    dv_low = dv.reshape(seq, local).astype(bf16)
    q_gain_part = jnp.sum(dq_norm * query * rate_q, 0)
    k_gain_part = jnp.sum(dk_norm * keyed * rate_k, 0)
    dqkv = jnp.concatenate([dq_low, dk_low, dv_low], 1)
    smalls = jnp.concatenate(
        [q_gain_part[None], k_gain_part[None], moe_gain_part[None], router_part.T], 0
    )
    moe_own = scatter_z_far({k: moe_parts[k].astype(f32) for k in range(0, nz, 2)}, moe_near)
    dqkv, moe_own, smalls = fence(dqkv, moe_own, butterfly_sum(smalls, ("core", "z")))
    half = lax.dynamic_slice_in_dim(smalls[2:], me_c * slice_d, slice_d, 1)
    half = tensor_sum(jnp.where(me_t == me_z, half, 0.0))
    mixed = gather_tensor((resid + moe_own).astype(bf16))
    wqkv_grad = jnp.einsum("sd,sa->da", a_low, dqkv, preferred_element_type=f32).astype(bf16)
    da_part = jnp.einsum("sa,da->sd", dqkv, wqkv_full, preferred_element_type=f32)
    blocks = columns_blocks(da_part.astype(bf16))
    got = [scatter_first(b, odd) for odd, b in enumerate(blocks)]
    expert_grads = place_call(idx, up_own, down_own)
    da_own = jnp.concatenate(
        [scatter_third(*scatter_second(b, g, odd)) for odd, (b, g) in enumerate(zip(blocks, got))],
        0,
    )
    da_own, mixed = fence(da_own, mixed)
    norm_x = x_own * rate_x
    pulled_x = da_own * lax.dynamic_slice_in_dim(a_gain, me_t * quarter, quarter, 0)
    inner_x = tensor_sum(jnp.sum(pulled_x * norm_x, -1))[:, None] / width
    tokens_grad = gather_tensor(
        (dresid + rate_x * (pulled_x - norm_x * inner_x)).astype(bf16)
    )

    wqkv_grad, wo_own = fence(wqkv_grad, wo_own)
    wqkv_own = lax.psum_scatter(wqkv_grad, dp, scatter_dimension=0, tiled=True)
    tokens_grad, wqkv_own = fence(tokens_grad, wqkv_own)
    wqkv_own, wo_own = wqkv_own.astype(f32), wo_own.astype(f32)
    attn_gain_grad = jnp.sum(jnp.concatenate([wq, wk, wv], 1).astype(f32) * wqkv_own, -1)
    attn_gain_grad = tensor_sum(attn_gain_grad) / attn_gain.astype(f32)
    return (
        mixed,
        tokens_grad,
        wqkv_own[:, :local],
        wqkv_own[:, local : 2 * local],
        wqkv_own[:, 2 * local : 3 * local],
        wo_own,
        attn_gain_grad,
        smalls[0],
        smalls[1],
        half[0],
        half[1:].T,
        expert_grads[0],
        expert_grads[1],
        expert_grads[2],
    )


def solution(mesh):
    fine = Mesh(
        mesh.devices.reshape(mesh.shape["dp"] // 2, 2, mesh.shape["tensor"]),
        ("z", "core", "tensor"),
    )
    dp = ("z", "core")
    in_specs = (
        P(dp, None),
        P(dp, None),
        P(dp, None),
        P(dp, "tensor"),
        P(dp, "tensor"),
        P(dp, "tensor"),
        P("tensor", dp),
        P(dp),
        P("tensor"),
        P("tensor"),
        P(dp),
        P(dp, None),
        P(None, dp, "tensor"),
        P(None, dp, "tensor"),
        P(None, "tensor", dp),
    )
    out_specs = (
        P(dp, None),
        P(dp, None),
        P(dp, "tensor"),
        P(dp, "tensor"),
        P(dp, "tensor"),
        P("tensor", dp),
        P(dp),
        P("tensor"),
        P("tensor"),
        P(dp),
        P(dp, None),
        P(None, dp, "tensor"),
        P(None, dp, "tensor"),
        P(None, "tensor", dp),
    )
    return jax.shard_map(shards, mesh=fine, in_specs=in_specs, out_specs=out_specs, check_vma=False)
```

```python
import functools

import jax
import jax.numpy as jnp
from jax import lax
from jax.experimental import pallas as pl
from jax.experimental.pallas import tpu as pltpu
from jax.sharding import Mesh
from jax.sharding import PartitionSpec as P

HEAD_DIM = 128
EXPERTS = 16
LANES = 128
FIRST = 2

EPS = 1e-05
THETA = 10000.0
HIGH = lax.Precision.HIGHEST
f32 = jnp.float32
bf16 = jnp.bfloat16
MIB = 1 << 20


def after(value, *earlier):
    return lax.optimization_barrier((value, *earlier))[0]


def fence(*values):
    return list(lax.optimization_barrier(values))


def swap(value, axis, mask):
    if mask == 0:
        return value
    n = lax.axis_size(axis)
    return lax.ppermute(value, axis, [(i, i ^ mask) for i in range(n)])


def bits_of(axis):
    n = lax.axis_size(axis)
    return [1 << b for b in range(n.bit_length() - 1)]


def butterfly_sum(value, axes):
    for axis in axes:
        for bit in bits_of(axis):
            value = value + swap(value, axis, bit)
    return value


def tensor_sum(value):
    return butterfly_sum(value, ("tensor",))


def rope_tables(length, head_dim):
    half = head_dim // 2
    freq = THETA ** (-(jnp.arange(half).astype(f32) * 2.0 / head_dim))
    angle = jnp.arange(length).astype(f32)[:, None] * freq[None, :]
    cosine = jnp.concatenate([jnp.cos(angle), jnp.cos(angle)], -1)
    sine = jnp.concatenate([jnp.sin(angle), jnp.sin(angle)], -1)
    return (cosine, sine)


def rotate(value, cosine, sine):
    half = value.shape[-1] // 2
    turned = jnp.concatenate([-value[..., half:], value[..., :half]], -1)
    return value * cosine[:, None, :] + turned * sine[:, None, :]


def unrotate(grad, cosine, sine):
    half = grad.shape[-1] // 2
    scaled = grad * sine[:, None, :]
    back_turn = jnp.concatenate([scaled[..., half:], -scaled[..., :half]], -1)
    return grad * cosine[:, None, :] + back_turn


def columns(value, index, size):
    return lax.dynamic_slice_in_dim(value, index * size, size, 1)


def spread_z(value):
    parts = {0: value}
    for bit in reversed(bits_of("z")):
        parts.update({k ^ bit: swap(v, "z", bit) for k, v in parts.items()})
    return [parts[k] for k in range(len(parts))]


def spread_tensor_near(value):
    n = lax.axis_size("tensor")
    return [swap(value, "tensor", k) for k in ((1, 2) if n == 4 else range(1, n))]


def spread_tensor_cross(near):
    if lax.axis_size("tensor") != 4:
        return []
    half = near[0].shape[0] // 2
    return [swap(near[0][:half], "tensor", 2), swap(near[1][half:], "tensor", 1)]


def place_of(n, half, k, row):
    if n != 4 or k < 3:
        return (k, row)
    return (3, row) if row < half else (4, row - half)


def spread_tensor_far(value, near):
    if lax.axis_size("tensor") != 4:
        return jnp.stack([value, *near])
    half = value.shape[0] // 2
    cross = [swap(near[0][:half], "tensor", 2), swap(near[1][half:], "tensor", 1)]
    return jnp.stack([value, *near, jnp.concatenate(cross, 0)])


def spread_tensor(value):
    return spread_tensor_far(value, spread_tensor_near(value))


def gather_tensor(value):
    me, n = lax.axis_index("tensor"), lax.axis_size("tensor")
    rows, width = value.shape
    out = jnp.zeros((rows, n * width), value.dtype)
    parts = spread_tensor(value)
    for k in range(n):
        part = parts[k]
        out = lax.dynamic_update_slice(out, part, (0, (me ^ k) * width))
    return out


def order_of(n, odd):
    if n != 4:
        return tuple(range(n))
    return (0, 1, 2, 3) if odd else (0, 2, 1, 3)


def scatter_first(block, odd):
    n = block.shape[0]
    if n != 4:
        return jnp.stack([swap(block[k], "tensor", k) for k in range(1, n)])
    return swap(block[2:], "tensor", 2 if odd else 1)


def scatter_second(block, got, odd):
    got = got.astype(f32)
    mine = block[0].astype(f32)
    if block.shape[0] != 4:
        return mine + jnp.sum(got, 0), None
    other = (block[1].astype(f32) + got[1]).astype(bf16)
    return mine + got[0], swap(other, "tensor", 1 if odd else 2)


def scatter_third(mine, got):
    return mine if got is None else mine + got.astype(f32)


def scatter_z_near(parts):
    return swap(jnp.stack([parts[k].astype(bf16) for k in sorted(parts)]), "z", 1)


def scatter_z_far(parts, got):
    parts = {k: parts[k] + got[i].astype(f32) for i, k in enumerate(sorted(parts))}
    for bit in bits_of("z")[1:]:
        away = sorted(k for k in parts if k & bit)
        got = swap(jnp.stack([parts[k].astype(bf16) for k in away]), "z", bit)
        parts = {k ^ bit: parts[k ^ bit] + got[i].astype(f32) for i, k in enumerate(away)}
    return parts[0]


def columns_blocks(value):
    me, n = lax.axis_index("tensor"), lax.axis_size("tensor")
    rows, width = value.shape[0], value.shape[1] // n
    half = rows // 2
    return [
        jnp.stack(
            [
                columns(value[odd * half : (odd + 1) * half], me ^ k, width)
                for k in order_of(n, odd)
            ]
        )
        for odd in (0, 1)
    ]


def dot_nn(a, b):
    return lax.dot_general(a, b, (((1,), (0,)), ((), ())), preferred_element_type=f32)


def dot_nt(a, b):
    return lax.dot_general(a, b, (((1,), (1,)), ((), ())), preferred_element_type=f32)


def dot_tn(a, b):
    return lax.dot_general(a, b, (((0,), (0,)), ((), ())), preferred_element_type=f32)


def weight_copies(nz, slice_d, own_e, idx, parts, whole, sems, down):
    copies = []
    for c in range(2):
        for k in range(nz):
            half = pl.multiple_of((idx[1] ^ c) * slice_d, slice_d)
            at = pl.multiple_of((idx[0] ^ k ^ idx[2]) * 2 * slice_d, slice_d) + half
            if down:
                copies.append((parts[c].at[k], whole.at[:, :, pl.ds(at, slice_d)]))
            else:
                hid = whole.shape[1] // own_e
                for e in range(own_e):
                    target = whole.at[pl.ds(at, slice_d), pl.ds(e * hid, hid)]
                    copies.append((parts[c].at[k, e], target))
    return [pltpu.make_async_copy(*pair, sems.at[j]) for j, pair in enumerate(copies)]


def start(copies):
    for copy in copies:
        copy.start()


def finish(copies):
    for copy in copies:
        copy.wait()


def own_gate(gates, lane, me_z, own_e, e):
    return jnp.sum(jnp.where(lane == FIRST + me_z * own_e + e, gates, 0.0), -1, keepdims=True)


def forward_kernel(nz, n, own_e, hid, slice_d, seq, quarter, places, idx, *refs):
    mask_ref, router_ref = refs[:2]
    gate_parts, up_parts, m_refs = refs[2:4], refs[4:6], refs[6:-11]
    act_ref, up_ref, hid_ref, probs_ref, m_out, w_gate, w_up, m_full, *sems = refs[-11:]
    gate_sems, up_sems, m_sems = sems
    me_z, me_t = idx[0], idx[2]
    step = pl.program_id(0)
    first = step == 0
    m_copies = [
        [
            pltpu.make_async_copy(
                m_refs[j].at[pl.ds(row, seq), :],
                m_full.at[pl.ds(i * seq, seq), pl.ds(k * quarter, quarter)],
                m_sems.at[i, k],
            )
            for k, (j, row) in enumerate(places[i])
        ]
        for i in range(nz)
    ]
    gate_copies = weight_copies(nz, slice_d, own_e, idx, gate_parts, w_gate, gate_sems, False)
    up_copies = weight_copies(nz, slice_d, own_e, idx, up_parts, w_up, up_sems, False)

    @pl.when(first)
    def _():
        start(m_copies[0] + gate_copies + up_copies)
        for copies in m_copies[1:]:
            start(copies)

    for i in range(nz):

        @pl.when(step == i)
        def _(i=i):
            finish(m_copies[i])

    rows = seq
    m_block = m_full[pl.ds(pl.multiple_of(step * seq, seq), seq), :]
    m_out[...] = m_block
    lane = lax.broadcasted_iota(jnp.int32, (rows, LANES), 1)
    logits = jnp.zeros((rows, LANES), f32)
    for k in range(n):
        logits += dot_nn(m_block[:, k * quarter : (k + 1) * quarter], router_ref[me_t ^ k])
    named = (lane >= FIRST) & (lane < FIRST + EXPERTS)
    logits = jnp.where(named, logits, -1e30)
    expd = jnp.where(named, jnp.exp(logits - jnp.max(logits, -1, keepdims=True)), 0.0)
    probs = expd / jnp.sum(expd, -1, keepdims=True)
    probs_ref[...] = probs
    gates = probs * mask_ref[...]

    @pl.when(first)
    def _():
        finish(gate_copies)

    for e in range(own_e):
        at = pl.ds(e * hid, hid)
        act_ref[:, at] = dot_nn(m_block, w_gate[:, at])

    @pl.when(first)
    def _():
        finish(up_copies)

    for e in range(own_e):
        at = pl.ds(e * hid, hid)
        up = dot_nn(m_block, w_up[:, at])
        up_ref[:, at] = up
        act = act_ref[:, at]
        gate = own_gate(gates, lane, me_z, own_e, e)
        hid_ref[:, at] = (gate * (act * jax.nn.sigmoid(act) * up)).astype(bf16)


def forward_call(idx, pieces, places, mask_all, router_q, gate_parts, up_parts, nz):
    n, quarter = router_q.shape[:2]
    tokens = mask_all.shape[0]
    seq = tokens // nz
    own_e, slice_d, hid = up_parts[0].shape[1:]
    wide = own_e * hid
    here = lambda i, idx: (i, 0)
    return pl.pallas_call(
        functools.partial(forward_kernel, nz, n, own_e, hid, slice_d, seq, quarter, places),
        grid_spec=pltpu.PrefetchScalarGridSpec(
            num_scalar_prefetch=1,
            grid=(nz,),
            in_specs=[
                pl.BlockSpec((seq, LANES), here),
                pl.BlockSpec((n, quarter, LANES), lambda i, idx: (0, 0, 0)),
            ]
            + [pl.BlockSpec(memory_space=pl.ANY)] * (4 + len(pieces)),
            out_specs=[
                pl.BlockSpec((seq, wide), here),
                pl.BlockSpec((seq, wide), here),
                pl.BlockSpec((seq, wide), here),
                pl.BlockSpec((seq, LANES), here),
                pl.BlockSpec((seq, n * quarter), here),
            ],
            scratch_shapes=[
                pltpu.VMEM((n * quarter, wide), bf16),
                pltpu.VMEM((n * quarter, wide), bf16),
                pltpu.VMEM((tokens, n * quarter), bf16),
                pltpu.SemaphoreType.DMA((2 * nz * own_e,)),
                pltpu.SemaphoreType.DMA((2 * nz * own_e,)),
                pltpu.SemaphoreType.DMA((nz, n)),
            ],
        ),
        out_shape=[
            jax.ShapeDtypeStruct((tokens, wide), f32),
            jax.ShapeDtypeStruct((tokens, wide), f32),
            jax.ShapeDtypeStruct((tokens, wide), bf16),
            jax.ShapeDtypeStruct((tokens, LANES), f32),
            jax.ShapeDtypeStruct((tokens, n * quarter), bf16),
        ],
        compiler_params=pltpu.CompilerParams(vmem_limit_bytes=56 * MIB),
        cost_estimate=pl.CostEstimate(
            flops=4 * tokens * n * quarter * wide, bytes_accessed=40 * MIB, transcendentals=0
        ),
    )(idx, mask_all, router_q, *gate_parts, *up_parts, *pieces)


def backward_kernel(nz, n, own_e, hid, slice_d, quarter, idx, *refs):
    g_ref, act_ref, up_ref, probs_ref, mask_ref = refs[:5]
    dx_ref, dg_ref, du_ref, w_gate, w_up, w_down, gate_sems, up_sems, down_sems = refs[11:]
    i = pl.program_id(0)
    me_z = idx[0]
    gate_copies = weight_copies(nz, slice_d, own_e, idx, refs[5:7], w_gate, gate_sems, False)
    up_copies = weight_copies(nz, slice_d, own_e, idx, refs[7:9], w_up, up_sems, False)
    down_copies = weight_copies(nz, slice_d, own_e, idx, refs[9:11], w_down, down_sems, True)

    @pl.when(i == 0)
    def _():
        start(down_copies + gate_copies + up_copies)
        finish(down_copies)

    rows = act_ref.shape[0]
    lane = lax.broadcasted_iota(jnp.int32, (rows, LANES), 1)
    gates = probs_ref[...] * mask_ref[...]
    dgate = jnp.zeros((rows, LANES), f32)
    g_block = jnp.concatenate([g_ref[q, 0] for q in range(n)], 1)
    for e in range(own_e):
        gate = own_gate(gates, lane, me_z, own_e, e)
        at = pl.ds(e * hid, hid)
        back = dot_nt(g_block, w_down[e])
        act = act_ref[:, at]
        up = up_ref[:, at]
        sigma = jax.nn.sigmoid(act)
        silu = act * sigma
        dgate = jnp.where(
            lane == me_z * own_e + e, jnp.sum(silu * up * back, -1, keepdims=True), dgate
        )
        back = gate * back
        dg_ref[:, at] = (back * up * sigma * (1.0 + act * (1.0 - sigma))).astype(bf16)
        du_ref[:, at] = (back * silu).astype(bf16)
    dgate = jnp.transpose(dgate)[:EXPERTS].astype(bf16)

    @pl.when(i == 0)
    def _():
        finish(gate_copies + up_copies)

    even, odd = order_of(n, 0), order_of(n, 1)
    for j in range(n):
        k = jnp.where(i % 2 == 0, even[j], odd[j])
        at = pl.ds(pl.multiple_of(k * quarter, quarter), quarter)
        total = dot_nt(dg_ref[...], w_gate[at, :]) + dot_nt(du_ref[...], w_up[at, :])
        dx_ref[0, j, pl.ds(0, rows), :] = total.astype(bf16)
        for h in range(rows // quarter):
            dx_ref[0, j, pl.ds(rows + h * EXPERTS, EXPERTS), :] = dgate[
                :, h * quarter : (h + 1) * quarter
            ]


def backward_call(idx, first, g_all, act, up, probs, mask_all, weights):
    n, nz, seq, quarter = g_all.shape
    own_e, slice_d, hid = weights[0].shape[1:]
    blocks = nz // 2
    wide = own_e * hid
    tall = seq + EXPERTS * (seq // quarter)
    some = lambda i, idx: (2 * i + first, 0)
    here = lambda i, idx: (i, 0)
    hbm = pl.BlockSpec(memory_space=pl.ANY)
    return pl.pallas_call(
        functools.partial(backward_kernel, nz, n, own_e, hid, slice_d, quarter),
        grid_spec=pltpu.PrefetchScalarGridSpec(
            num_scalar_prefetch=1,
            grid=(blocks,),
            in_specs=[
                pl.BlockSpec((n, 1, seq, quarter), lambda i, idx: (0, 2 * i + first, 0, 0)),
                pl.BlockSpec((seq, wide), some),
                pl.BlockSpec((seq, wide), some),
                pl.BlockSpec((seq, LANES), some),
                pl.BlockSpec((seq, LANES), some),
            ]
            + [hbm] * 6,
            out_specs=[
                pl.BlockSpec((1, n, tall, quarter), lambda i, idx: (i, 0, 0, 0)),
                pl.BlockSpec((seq, wide), here),
                pl.BlockSpec((seq, wide), here),
            ],
            scratch_shapes=[
                pltpu.VMEM((n * quarter, wide), bf16),
                pltpu.VMEM((n * quarter, wide), bf16),
                pltpu.VMEM((own_e, hid, n * quarter), bf16),
                pltpu.SemaphoreType.DMA((2 * nz * own_e,)),
                pltpu.SemaphoreType.DMA((2 * nz * own_e,)),
                pltpu.SemaphoreType.DMA((2 * nz,)),
            ],
        ),
        out_shape=[
            jax.ShapeDtypeStruct((blocks, n, tall, quarter), bf16),
            jax.ShapeDtypeStruct((blocks * seq, wide), bf16),
            jax.ShapeDtypeStruct((blocks * seq, wide), bf16),
        ],
        compiler_params=pltpu.CompilerParams(vmem_limit_bytes=56 * MIB),
        cost_estimate=pl.CostEstimate(
            flops=6 * blocks * seq * n * quarter * wide,
            bytes_accessed=40 * MIB,
            transcendentals=0,
        ),
    )(idx, g_all, act, up, probs, mask_all, *weights)


def output_kernel(nz, own_e, hid, slice_d, quarter, idx, hid_ref, near, far, y_ref, w_down, sems):
    i, j = pl.program_id(0), pl.program_id(1)

    @pl.when((i == 0) & (j == 0))
    def _():
        copies = weight_copies(nz, slice_d, own_e, idx, (near, far), w_down, sems, True)
        start(copies)
        finish(copies)

    at = pl.ds(pl.multiple_of(j * quarter, quarter), quarter)
    part = w_down[:, :, at].reshape(own_e * hid, quarter)
    y_ref[0, 0] = dot_nn(hid_ref[...], part).astype(bf16)


def output_call(idx, hidden, parts, n, nz):
    tokens, wide = hidden.shape
    seq = tokens // nz
    own_e, hid, slice_d = parts[0].shape[1:]
    quarter = 2 * slice_d
    return pl.pallas_call(
        functools.partial(output_kernel, nz, own_e, hid, slice_d, quarter),
        grid_spec=pltpu.PrefetchScalarGridSpec(
            num_scalar_prefetch=1,
            grid=(nz, n),
            in_specs=[pl.BlockSpec((seq, wide), lambda i, j, idx: (i, 0))]
            + [pl.BlockSpec(memory_space=pl.ANY)] * 2,
            out_specs=pl.BlockSpec(
                (1, 1, seq, quarter), lambda i, j, idx: (j ^ idx[2], i ^ idx[0], 0, 0)
            ),
            scratch_shapes=[
                pltpu.VMEM((own_e, hid, n * quarter), bf16),
                pltpu.SemaphoreType.DMA((2 * nz,)),
            ],
        ),
        out_shape=jax.ShapeDtypeStruct((n, nz, seq, quarter), bf16),
        compiler_params=pltpu.CompilerParams(vmem_limit_bytes=48 * MIB),
        cost_estimate=pl.CostEstimate(
            flops=2 * tokens * n * quarter * wide, bytes_accessed=16 * MIB, transcendentals=0
        ),
    )(idx, hidden, *parts)


def down_grad_kernel(nz, n, own_e, hid, seq, slice_d, idx, hid_ref, *refs):
    g_refs, (keep_ref, give_ref, g_out, g_full, sems) = refs[:-5], refs[-5:]
    step = pl.program_id(0)
    copies = []
    for k in range(n):
        copies.append([])
        for i in range(nz):
            j, row = place_of(n, nz * seq // 2, k, i * seq)
            copies[k].append(
                pltpu.make_async_copy(
                    g_refs[j].at[pl.ds(row, seq), :],
                    g_full.at[k, pl.ds(i * seq, seq), :],
                    sems.at[k, i],
                )
            )

    @pl.when(step == 0)
    def _():
        for some in copies:
            start(some)

    for k in range(n):

        @pl.when(step == k)
        def _(k=k):
            finish(copies[k])

    g_block = g_full[step]
    g_out[0] = g_block
    total = dot_tn(g_block, hid_ref[...])
    halves = (total[:slice_d], total[slice_d:])
    for e in range(own_e):
        parts = [jnp.transpose(half[:, e * hid : (e + 1) * hid]).astype(bf16) for half in halves]
        keep_ref[0, e] = jnp.where(idx[1] == 0, parts[0], parts[1])
        give_ref[0, e] = jnp.where(idx[1] == 0, parts[1], parts[0])


def down_grad_call(idx, pieces, hidden, own_e, nz, n):
    tokens, wide = hidden.shape
    quarter, seq = pieces[0].shape[1], tokens // nz
    hid, slice_d = wide // own_e, quarter // 2
    out = pl.BlockSpec((1, own_e, hid, slice_d), lambda k, idx: (k ^ idx[2] ^ idx[0], 0, 0, 0))
    return pl.pallas_call(
        functools.partial(down_grad_kernel, nz, n, own_e, hid, seq, slice_d),
        grid_spec=pltpu.PrefetchScalarGridSpec(
            num_scalar_prefetch=1,
            grid=(n,),
            in_specs=[pl.BlockSpec((tokens, wide), lambda k, idx: (0, 0))]
            + [pl.BlockSpec(memory_space=pl.ANY)] * len(pieces),
            out_specs=[out, out, pl.BlockSpec((1, tokens, quarter), lambda k, idx: (k, 0, 0))],
            scratch_shapes=[
                pltpu.VMEM((n, tokens, quarter), bf16),
                pltpu.SemaphoreType.DMA((n, nz)),
            ],
        ),
        out_shape=[jax.ShapeDtypeStruct((nz, own_e, hid, slice_d), bf16)] * 2
        + [jax.ShapeDtypeStruct((n, tokens, quarter), bf16)],
        compiler_params=pltpu.CompilerParams(vmem_limit_bytes=48 * MIB),
        cost_estimate=pl.CostEstimate(
            flops=2 * tokens * n * quarter * wide, bytes_accessed=24 * MIB, transcendentals=0
        ),
    )(idx, hidden, *pieces)


def up_grad_kernel(nz, own_e, hid, seq, slice_d, idx, m_ref, *refs):
    rights, (keep_ref, give_ref) = refs[:4], refs[4:]
    lefts = [
        jnp.concatenate([m_ref[pl.ds(blk * seq, seq), :] for blk in range(odd, nz, 2)], 0)
        for odd in (0, 1)
    ]
    for w in range(2):
        for e in range(own_e):
            at = pl.ds(e * hid, hid)
            total = dot_tn(lefts[0], rights[2 * w][:, at]) + dot_tn(
                lefts[1], rights[2 * w + 1][:, at]
            )
            parts = (total[:slice_d].astype(bf16), total[slice_d:].astype(bf16))
            keep_ref[0, w, e] = jnp.where(idx[1] == 0, parts[0], parts[1])
            give_ref[0, w, e] = jnp.where(idx[1] == 0, parts[1], parts[0])


def up_grad_call(idx, m_all, early, late, own_e, nz, n):
    tokens, quarter = m_all.shape[0], m_all.shape[1] // n
    seq = tokens // nz
    wide = early[0].shape[1]
    hid, slice_d = wide // own_e, quarter // 2
    full = pl.BlockSpec(early[0].shape, lambda k, idx: (0, 0))
    out = pl.BlockSpec(
        (1, 2, own_e, slice_d, hid), lambda k, idx: (k ^ idx[2] ^ idx[0], 0, 0, 0, 0)
    )
    return pl.pallas_call(
        functools.partial(up_grad_kernel, nz, own_e, hid, seq, slice_d),
        grid_spec=pltpu.PrefetchScalarGridSpec(
            num_scalar_prefetch=1,
            grid=(n,),
            in_specs=[pl.BlockSpec((tokens, quarter), lambda k, idx: (0, k))] + [full] * 4,
            out_specs=[out, out],
        ),
        out_shape=[jax.ShapeDtypeStruct((nz, 2, own_e, slice_d, hid), bf16)] * 2,
        compiler_params=pltpu.CompilerParams(vmem_limit_bytes=48 * MIB),
        cost_estimate=pl.CostEstimate(
            flops=4 * tokens * n * quarter * wide, bytes_accessed=24 * MIB, transcendentals=0
        ),
    )(idx, m_all, early[0], late[0], early[1], late[1])


def place_kernel(nz, idx, *refs):
    ups, downs, outs = refs[:nz], refs[nz : 2 * nz], refs[2 * nz :]
    for i in range(nz):

        @pl.when(pl.program_id(0) == i)
        def _(i=i):
            outs[0][...] = ups[i][0].astype(f32)
            outs[1][...] = ups[i][1].astype(f32)
            outs[2][...] = downs[i][...].astype(f32)


def place_call(idx, ups, downs):
    nz = len(ups)
    flat = list(ups) + list(downs)
    fixed = lambda rank: lambda k, idx: (0,) * rank
    shapes = [ups[0].shape[1:], ups[0].shape[1:], downs[0].shape]
    return pl.pallas_call(
        functools.partial(place_kernel, nz),
        grid_spec=pltpu.PrefetchScalarGridSpec(
            num_scalar_prefetch=1,
            grid=(nz,),
            in_specs=[pl.BlockSpec(part.shape, fixed(part.ndim)) for part in flat],
            out_specs=[
                pl.BlockSpec(shape, lambda k, idx: (k ^ idx[0], 0, 0)) for shape in shapes
            ],
        ),
        out_shape=[jax.ShapeDtypeStruct((EXPERTS,) + shape[1:], f32) for shape in shapes],
        compiler_params=pltpu.CompilerParams(vmem_limit_bytes=48 * MIB),
        cost_estimate=pl.CostEstimate(flops=0, bytes_accessed=20 * MIB, transcendentals=0),
    )(idx, *flat)


def shards(
    tokens,
    cotangent,
    routes,
    wq,
    wk,
    wv,
    wo,
    attn_gain,
    q_gain,
    k_gain,
    moe_gain,
    router,
    w_gate,
    w_up,
    w_down,
):
    nz = lax.axis_size("z")
    me_t = lax.axis_index("tensor")
    me_z = lax.axis_index("z")
    me_c = lax.axis_index("core")
    dp = ("z", "core")
    seq, width = tokens.shape
    quarter = width // lax.axis_size("tensor")
    local = wq.shape[1]
    local_heads = local // HEAD_DIM
    slice_d = wq.shape[0]
    own_e = EXPERTS // nz
    hid = w_gate.shape[2]

    idx = jnp.stack([me_z, me_c, me_t]).astype(jnp.int32)

    small = jnp.concatenate([attn_gain[:, None], moe_gain[:, None], router], 1)
    small = jnp.pad(small, ((0, 0), (0, LANES - small.shape[1])))
    packed = lax.all_gather(jnp.concatenate([wq, wk, wv, small], 1), dp, axis=0, tiled=True)
    mask = jnp.sum(
        (routes[:, :, None] == jnp.arange(EXPERTS)[None, None, :]).astype(bf16), 1
    )
    n = width // quarter
    packed, *mask_parts = fence(packed, *spread_z(mask.T))
    mask_all = jnp.stack(mask_parts).transpose(0, 2, 1)
    mask_all = jnp.pad(
        mask_all.reshape(nz * seq, EXPERTS).astype(f32),
        ((0, 0), (FIRST, LANES - EXPERTS - FIRST)),
    )
    wqkv_full = packed[:, : 3 * local]
    small_full = packed[:, 3 * local :]
    a_gain = small_full[:, 0].astype(f32)
    m_gain = small_full[:, 1].astype(f32)
    router_full = small_full[:, FIRST : FIRST + EXPERTS]
    wo_full = lax.all_gather(after(wo, packed), dp, axis=1, tiled=True)

    def fetch(weight, ks):
        pick = lambda k: lax.dynamic_slice_in_dim(weight, (me_z ^ k) * own_e, own_e, 0)
        return [swap(pick(k), "z", k) for k in ks]

    def both_cores(parts):
        parts = jnp.stack(parts)
        return [parts, swap(parts, "core", 1)]

    most, last = range(nz - 1), range(nz - 1, nz)
    cot_parts = spread_z(after(columns(cotangent, me_t, quarter), packed))

    xf = tokens.astype(f32)
    rate_x = lax.rsqrt(jnp.mean(xf * xf, -1, keepdims=True) + EPS)
    gain_q = q_gain.astype(f32)
    gain_k = k_gain.astype(f32)
    a_low = (xf * rate_x * a_gain).astype(bf16)
    qkv = jnp.dot(a_low, wqkv_full, preferred_element_type=f32)
    query, keyed, valued = qkv[:, :local], qkv[:, local : 2 * local], qkv[:, 2 * local :]
    sums = tensor_sum(jnp.stack([jnp.sum(query * query, -1), jnp.sum(keyed * keyed, -1)]))
    rate_q = lax.rsqrt(sums[0] / width + EPS)[:, None]
    rate_k = lax.rsqrt(sums[1] / width + EPS)[:, None]
    cosine, sine = rope_tables(seq, HEAD_DIM)
    heads = (seq, local_heads, HEAD_DIM)
    q_rot = rotate((query * rate_q * gain_q).reshape(heads), cosine, sine).astype(bf16)
    k_rot = rotate((keyed * rate_k * gain_k).reshape(heads), cosine, sine).astype(bf16)
    v_low = valued.reshape(heads).astype(bf16)
    scale = HEAD_DIM ** (-0.5)
    scores = scale * jnp.einsum("qhd,khd->hqk", q_rot, k_rot, preferred_element_type=f32)
    causal = jnp.arange(seq)[:, None] >= jnp.arange(seq)[None, :]
    scores = jnp.where(causal[None], scores, -1e30)
    peak = jnp.max(scores, -1, keepdims=True)
    expd = jnp.exp(scores - peak)
    weights = expd / jnp.sum(expd, -1, keepdims=True)
    weights_low = weights.astype(bf16)
    outputs = jnp.einsum("hqk,khd->qhd", weights_low, v_low, preferred_element_type=f32)
    joined = outputs.reshape(seq, local).astype(bf16)
    wo_full = after(wo_full, joined)
    attn = jnp.dot(joined, wo_full, preferred_element_type=f32).astype(bf16)
    attn, *cot_parts[:-1] = fence(attn, *cot_parts[:-1])
    gate_parts = fetch(after(w_gate, attn), most)

    x_own = columns(xf, me_t, quarter)
    blocks = columns_blocks(attn)
    got = [scatter_first(block, odd) for odd, block in enumerate(blocks)]
    resid = x_own + jnp.concatenate(
        [scatter_third(*scatter_second(b, g, odd)) for odd, (b, g) in enumerate(zip(blocks, got))],
        0,
    )
    rate_r = lax.rsqrt(tensor_sum(jnp.sum(resid * resid, -1)) / width + EPS)[:, None]
    gain_own = lax.dynamic_slice_in_dim(m_gain, me_t * quarter, quarter, 0)
    m_own = (resid * rate_r * gain_own).astype(bf16)

    held = fence(m_own, *gate_parts, *cot_parts)
    m_own, gate_parts, cot_parts = held[0], held[1:nz], held[nz:]
    cot_flat = jnp.concatenate(cot_parts, 0)
    cot_near = spread_tensor_near(cot_flat)
    held = fence(*spread_z(m_own), *cot_near)
    m_parts, cot_near = held[:nz], held[nz:]
    gate_parts += fetch(after(w_gate, m_parts[0]), last)
    up_parts = fetch(after(w_up, m_parts[0]), most)
    m_flat = jnp.concatenate(m_parts, 0)
    m_near = spread_tensor_near(m_flat)
    held = fence(gate_parts[-1], *up_parts, *m_near)
    gate_parts[-1], up_parts, m_near = held[0], held[1:nz], held[nz:]
    gate_parts = both_cores(gate_parts)
    up_parts += fetch(after(w_up, m_near[0]), last)
    held = fence(m_flat, *m_near, *spread_tensor_cross(m_near), up_parts[-1])
    up_parts[-1], pieces = held[-1], held[:-1]
    up_parts = both_cores(up_parts)
    down_parts = fetch(after(w_down, up_parts[0]), range(nz))
    cot_cross = spread_tensor_cross([after(x, pieces[-1]) for x in cot_near])
    places = [
        [place_of(n, nz * seq // 2, k, i * seq) for k in range(n)] for i in range(nz)
    ]
    router_q = small_full.reshape(-1, quarter, LANES)
    act, up, hidden, probs_all, m_all = forward_call(
        idx, pieces, places, mask_all, router_q, gate_parts, up_parts, nz
    )
    hidden, *cot_cross = fence(hidden, *cot_cross)
    down_keep, down_give, cot_all = down_grad_call(
        idx, [cot_flat, *cot_near, *cot_cross], hidden, own_e, nz, n
    )
    cot_all = cot_all.reshape(n, nz, seq, quarter)

    def to_owners(keep, got):
        summed = (keep.astype(f32) + got.astype(f32)).astype(bf16)
        return [swap(summed[k], "z", k) for k in range(nz)]

    down_give, *down_parts = fence(down_give, *down_parts)
    down_parts = both_cores(down_parts)
    down_got = swap(down_give, "core", 1)
    half_call = lambda first, probs: backward_call(
        idx, first, cot_all, act, up, probs, mask_all, gate_parts + up_parts + down_parts
    )
    odds, evens = range(1, nz, 2), range(0, nz, 2)
    late = half_call(1, after(probs_all, down_give))
    first = {k: scatter_first(late[0][k // 2], k // 2 % 2) for k in odds}
    down_own = to_owners(after(down_keep, late[1]), down_got)
    early = half_call(0, after(probs_all, late[1], down_own[0]))
    held = fence(*early, *down_own[:-1], *(first[k] for k in odds))
    early, down_own[:-1] = held[:3], held[3 : 2 + nz]
    got = dict(zip(odds, held[2 + nz :]))
    second = {k: scatter_second(late[0][k // 2], got[k], k // 2 % 2) for k in odds}
    first = {k: scatter_first(early[0][k // 2], k // 2 % 2) for k in evens}
    up_keep, up_give = up_grad_call(idx, m_all, early[1:3], late[1:3], own_e, nz, n)
    few = [second[k] for k in odds if second[k][1] is not None]
    held = fence(
        up_keep,
        up_give,
        down_own[-1],
        *(first[k] for k in evens),
        *(x[1] for x in few),
    )
    (up_keep, up_give, down_own[-1]), got = held[:3], dict(zip(evens, held[3:]))
    if few:
        second = {k: (second[k][0], x) for k, x in zip(odds, held[3 + nz // 2 :])}
    near = scatter_z_near({k: scatter_third(*second[k]) for k in odds})
    second = {k: scatter_second(early[0][k // 2], got[k], k // 2 % 2) for k in evens}
    up_got = swap(up_give, "core", 1)
    moe_part = output_call(idx, after(hidden, up_give), down_parts, n, nz)
    few = [second[k][1] for k in evens if second[k][1] is not None]
    near, moe_part, *few = fence(near, moe_part, *few)
    if few:
        second = {k: (second[k][0], x) for k, x in zip(evens, few)}
    dm_own = scatter_z_far({k: scatter_third(*second[k]) for k in evens}, near)
    dgate = jnp.concatenate(
        [dm_own[seq + h * EXPERTS :][:EXPERTS] for h in range(seq // quarter)], 1
    )
    dm_own, up_got = fence(dm_own[:seq], up_got)
    summed = (up_keep.astype(f32) + up_got.astype(f32)).astype(bf16)
    up_own = [swap(summed[k], "z", k) for k in range(nz - 1)] + [None]
    up_last = summed[nz - 1]
    moe_sum = lax.psum_scatter(moe_part, "tensor", scatter_dimension=0, tiled=False)

    dgate = dgate.T
    probs = probs_all[:seq, FIRST : FIRST + EXPERTS]
    dprobs = dgate * mask.astype(f32)
    dlogits = probs * (dprobs - jnp.sum(probs * dprobs, -1, keepdims=True))
    router_own = lax.dynamic_slice_in_dim(router_full, me_t * quarter, quarter, 0)
    router_part = jnp.dot(m_own.astype(f32).T, dlogits, precision=HIGH)
    dm_own = dm_own + jnp.dot(dlogits, router_own.astype(f32).T, precision=HIGH)

    normed = resid * rate_r
    moe_gain_part = jnp.sum(dm_own * normed, 0)
    pulled = dm_own * gain_own
    inner_r = tensor_sum(jnp.sum(pulled * normed, -1))[:, None] / width
    cot_own = columns(cotangent, me_t, quarter).astype(f32)
    dresid = cot_own + rate_r * (pulled - normed * inner_r)
    dresid_low = gather_tensor(dresid.astype(bf16))
    dresid_low, *up_own[:-1] = fence(dresid_low, *up_own[:-1])
    up_own[-1] = swap(after(up_last, dresid_low), "z", nz - 1)
    moe_sum = after(moe_sum, dresid_low)
    moe_parts = {
        k: lax.dynamic_index_in_dim(moe_sum, me_z ^ k, 0, keepdims=False) for k in range(nz)
    }
    moe_near = scatter_z_near({k: moe_parts[k] for k in range(1, nz, 2)})

    wo_grad = jnp.einsum("sa,sd->ad", joined, dresid_low, preferred_element_type=f32)
    dout = (
        jnp.einsum("sd,ad->sa", dresid_low, wo_full, preferred_element_type=f32)
        .astype(bf16)
        .reshape(heads)
    )
    dweights = jnp.einsum("qhd,khd->hqk", dout, v_low, preferred_element_type=f32)
    dv = jnp.einsum("hqk,qhd->khd", weights_low, dout, preferred_element_type=f32)
    inner = jnp.sum(weights * dweights, -1, keepdims=True)
    dscores = (weights * (dweights - inner)).astype(bf16)
    dscores, up_own[-1], moe_near = fence(dscores, up_own[-1], moe_near)
    wo_grad = after(wo_grad.astype(bf16), dscores)
    wo_own = lax.psum_scatter(wo_grad, dp, scatter_dimension=1, tiled=True)
    dq_rot = scale * jnp.einsum("hqk,khd->qhd", dscores, k_rot, preferred_element_type=f32)
    dk_rot = scale * jnp.einsum("hqk,qhd->khd", dscores, q_rot, preferred_element_type=f32)
    dq_norm = unrotate(dq_rot, cosine, sine).reshape(seq, local)
    dk_norm = unrotate(dk_rot, cosine, sine).reshape(seq, local)
    inners = tensor_sum(
        jnp.stack(
            [jnp.sum(dq_norm * gain_q * query, -1), jnp.sum(dk_norm * gain_k * keyed, -1)]
        )
    )
    dq_low = (rate_q * gain_q * dq_norm - query * rate_q**3 * inners[0][:, None] / width).astype(
        bf16
    )
    dk_low = (rate_k * gain_k * dk_norm - keyed * rate_k**3 * inners[1][:, None] / width).astype(
        bf16
    )
    dv_low = dv.reshape(seq, local).astype(bf16)
    q_gain_part = jnp.sum(dq_norm * query * rate_q, 0)
    k_gain_part = jnp.sum(dk_norm * keyed * rate_k, 0)
    dqkv = jnp.concatenate([dq_low, dk_low, dv_low], 1)
    smalls = jnp.concatenate(
        [q_gain_part[None], k_gain_part[None], moe_gain_part[None], router_part.T], 0
    )
    moe_own = scatter_z_far({k: moe_parts[k].astype(f32) for k in range(0, nz, 2)}, moe_near)
    dqkv, moe_own, smalls = fence(dqkv, moe_own, butterfly_sum(smalls, ("core", "z")))
    half = lax.dynamic_slice_in_dim(smalls[2:], me_c * slice_d, slice_d, 1)
    half = tensor_sum(jnp.where(me_t == me_z, half, 0.0))
    mixed = gather_tensor((resid + moe_own).astype(bf16))
    wqkv_grad = jnp.einsum("sd,sa->da", a_low, dqkv, preferred_element_type=f32).astype(bf16)
    da_part = jnp.einsum("sa,da->sd", dqkv, wqkv_full, preferred_element_type=f32)
    blocks = columns_blocks(da_part.astype(bf16))
    got = [scatter_first(b, odd) for odd, b in enumerate(blocks)]
    expert_grads = place_call(idx, up_own, down_own)
    da_own = jnp.concatenate(
        [scatter_third(*scatter_second(b, g, odd)) for odd, (b, g) in enumerate(zip(blocks, got))],
        0,
    )
    da_own, mixed = fence(da_own, mixed)
    norm_x = x_own * rate_x
    pulled_x = da_own * lax.dynamic_slice_in_dim(a_gain, me_t * quarter, quarter, 0)
    inner_x = tensor_sum(jnp.sum(pulled_x * norm_x, -1))[:, None] / width
    tokens_grad = gather_tensor(
        (dresid + rate_x * (pulled_x - norm_x * inner_x)).astype(bf16)
    )

    wqkv_grad, wo_own = fence(wqkv_grad, wo_own)
    wqkv_own = lax.psum_scatter(wqkv_grad, dp, scatter_dimension=0, tiled=True)
    tokens_grad, wqkv_own = fence(tokens_grad, wqkv_own)
    wqkv_own, wo_own = wqkv_own.astype(f32), wo_own.astype(f32)
    attn_gain_grad = jnp.sum(jnp.concatenate([wq, wk, wv], 1).astype(f32) * wqkv_own, -1)
    attn_gain_grad = [attn_gain_grad] + [swap(attn_gain_grad, "tensor", k) for k in range(1, n)]
    while len(attn_gain_grad) > 1:
        attn_gain_grad = [a + b for a, b in zip(attn_gain_grad[::2], attn_gain_grad[1::2])]
    attn_gain_grad = attn_gain_grad[0] / attn_gain.astype(f32)
    return (
        mixed,
        tokens_grad,
        wqkv_own[:, :local],
        wqkv_own[:, local : 2 * local],
        wqkv_own[:, 2 * local : 3 * local],
        wo_own,
        attn_gain_grad,
        smalls[0],
        smalls[1],
        half[0],
        half[1:].T,
        expert_grads[0],
        expert_grads[1],
        expert_grads[2],
    )


def solution(mesh):
    fine = Mesh(
        mesh.devices.reshape(mesh.shape["dp"] // 2, 2, mesh.shape["tensor"]),
        ("z", "core", "tensor"),
    )
    dp = ("z", "core")
    in_specs = (
        P(dp, None),
        P(dp, None),
        P(dp, None),
        P(dp, "tensor"),
        P(dp, "tensor"),
        P(dp, "tensor"),
        P("tensor", dp),
        P(dp),
        P("tensor"),
        P("tensor"),
        P(dp),
        P(dp, None),
        P(None, dp, "tensor"),
        P(None, dp, "tensor"),
        P(None, "tensor", dp),
    )
    out_specs = (
        P(dp, None),
        P(dp, None),
        P(dp, "tensor"),
        P(dp, "tensor"),
        P(dp, "tensor"),
        P("tensor", dp),
        P(dp),
        P("tensor"),
        P("tensor"),
        P(dp),
        P(dp, None),
        P(None, dp, "tensor"),
        P(None, dp, "tensor"),
        P(None, "tensor", dp),
    )
    return jax.shard_map(shards, mesh=fine, in_specs=in_specs, out_specs=out_specs, check_vma=False)
```

```python
import functools

import jax
import jax.numpy as jnp
from jax import lax
from jax.experimental import pallas as pl
from jax.experimental.pallas import tpu as pltpu
from jax.sharding import Mesh
from jax.sharding import PartitionSpec as P

HEAD_DIM = 128
EXPERTS = 16
LANES = 128
FIRST = 2

EPS = 1e-05
THETA = 10000.0
HIGH = lax.Precision.HIGHEST
f32 = jnp.float32
bf16 = jnp.bfloat16
MIB = 1 << 20


def after(value, *earlier):
    return lax.optimization_barrier((value, *earlier))[0]


def fence(*values):
    return list(lax.optimization_barrier(values))


def swap(value, axis, mask):
    if mask == 0:
        return value
    n = lax.axis_size(axis)
    return lax.ppermute(value, axis, [(i, i ^ mask) for i in range(n)])


def bits_of(axis):
    n = lax.axis_size(axis)
    return [1 << b for b in range(n.bit_length() - 1)]


def butterfly_sum(value, axes):
    for axis in axes:
        for bit in bits_of(axis):
            value = value + swap(value, axis, bit)
    return value


def tensor_sum(value):
    parts = [value] + [swap(value, "tensor", k) for k in range(1, lax.axis_size("tensor"))]
    while len(parts) > 1:
        parts = [a + b for a, b in zip(parts[::2], parts[1::2])]
    return parts[0]


def rope_tables(length, head_dim):
    half = head_dim // 2
    freq = THETA ** (-(jnp.arange(half).astype(f32) * 2.0 / head_dim))
    angle = jnp.arange(length).astype(f32)[:, None] * freq[None, :]
    cosine = jnp.concatenate([jnp.cos(angle), jnp.cos(angle)], -1)
    sine = jnp.concatenate([jnp.sin(angle), jnp.sin(angle)], -1)
    return (cosine, sine)


def rotate(value, cosine, sine):
    half = value.shape[-1] // 2
    turned = jnp.concatenate([-value[..., half:], value[..., :half]], -1)
    return value * cosine[:, None, :] + turned * sine[:, None, :]


def unrotate(grad, cosine, sine):
    half = grad.shape[-1] // 2
    scaled = grad * sine[:, None, :]
    back_turn = jnp.concatenate([scaled[..., half:], -scaled[..., :half]], -1)
    return grad * cosine[:, None, :] + back_turn


def columns(value, index, size):
    return lax.dynamic_slice_in_dim(value, index * size, size, 1)


def spread_z(value):
    parts = {0: value}
    for bit in reversed(bits_of("z")):
        parts.update({k ^ bit: swap(v, "z", bit) for k, v in parts.items()})
    return [parts[k] for k in range(len(parts))]


def spread_tensor_near(value):
    n = lax.axis_size("tensor")
    return [swap(value, "tensor", k) for k in ((1, 2) if n == 4 else range(1, n))]


def spread_tensor_cross(near):
    if lax.axis_size("tensor") != 4:
        return []
    half = near[0].shape[0] // 2
    return [swap(near[0][:half], "tensor", 2), swap(near[1][half:], "tensor", 1)]


def place_of(n, half, k, row):
    if n != 4 or k < 3:
        return (k, row)
    return (3, row) if row < half else (4, row - half)


def spread_tensor_far(value, near):
    if lax.axis_size("tensor") != 4:
        return jnp.stack([value, *near])
    half = value.shape[0] // 2
    cross = [swap(near[0][:half], "tensor", 2), swap(near[1][half:], "tensor", 1)]
    return jnp.stack([value, *near, jnp.concatenate(cross, 0)])


def spread_tensor(value):
    return spread_tensor_far(value, spread_tensor_near(value))


def gather_tensor(value):
    me, n = lax.axis_index("tensor"), lax.axis_size("tensor")
    rows, width = value.shape
    out = jnp.zeros((rows, n * width), value.dtype)
    parts = spread_tensor(value)
    for k in range(n):
        part = parts[k]
        out = lax.dynamic_update_slice(out, part, (0, (me ^ k) * width))
    return out


def order_of(n, odd):
    if n != 4:
        return tuple(range(n))
    return (0, 1, 2, 3) if odd else (0, 2, 1, 3)


def scatter_first(block, odd):
    n = block.shape[0]
    if n != 4:
        return jnp.stack([swap(block[k], "tensor", k) for k in range(1, n)])
    return swap(block[2:], "tensor", 2 if odd else 1)


def scatter_second(block, got, odd):
    got = got.astype(f32)
    mine = block[0].astype(f32)
    if block.shape[0] != 4:
        return mine + jnp.sum(got, 0), None
    other = (block[1].astype(f32) + got[1]).astype(bf16)
    return mine + got[0], swap(other, "tensor", 1 if odd else 2)


def scatter_third(mine, got):
    return mine if got is None else mine + got.astype(f32)


def scatter_z_near(parts):
    return swap(jnp.stack([parts[k].astype(bf16) for k in sorted(parts)]), "z", 1)


def scatter_z_far(parts, got):
    parts = {k: parts[k] + got[i].astype(f32) for i, k in enumerate(sorted(parts))}
    for bit in bits_of("z")[1:]:
        away = sorted(k for k in parts if k & bit)
        got = swap(jnp.stack([parts[k].astype(bf16) for k in away]), "z", bit)
        parts = {k ^ bit: parts[k ^ bit] + got[i].astype(f32) for i, k in enumerate(away)}
    return parts[0]


def columns_blocks(value):
    me, n = lax.axis_index("tensor"), lax.axis_size("tensor")
    rows, width = value.shape[0], value.shape[1] // n
    half = rows // 2
    return [
        jnp.stack(
            [
                columns(value[odd * half : (odd + 1) * half], me ^ k, width)
                for k in order_of(n, odd)
            ]
        )
        for odd in (0, 1)
    ]


def dot_nn(a, b):
    return lax.dot_general(a, b, (((1,), (0,)), ((), ())), preferred_element_type=f32)


def dot_nt(a, b):
    return lax.dot_general(a, b, (((1,), (1,)), ((), ())), preferred_element_type=f32)


def dot_tn(a, b):
    return lax.dot_general(a, b, (((0,), (0,)), ((), ())), preferred_element_type=f32)


def weight_copies(nz, slice_d, own_e, idx, parts, whole, sems, down):
    copies = []
    for c in range(2):
        for k in range(nz):
            half = pl.multiple_of((idx[1] ^ c) * slice_d, slice_d)
            at = pl.multiple_of((idx[0] ^ k ^ idx[2]) * 2 * slice_d, slice_d) + half
            if down:
                copies.append((parts[c].at[k], whole.at[:, :, pl.ds(at, slice_d)]))
            else:
                hid = whole.shape[1] // own_e
                for e in range(own_e):
                    target = whole.at[pl.ds(at, slice_d), pl.ds(e * hid, hid)]
                    copies.append((parts[c].at[k, e], target))
    return [pltpu.make_async_copy(*pair, sems.at[j]) for j, pair in enumerate(copies)]


def start(copies):
    for copy in copies:
        copy.start()


def finish(copies):
    for copy in copies:
        copy.wait()


def own_gate(gates, lane, me_z, own_e, e):
    return jnp.sum(jnp.where(lane == FIRST + me_z * own_e + e, gates, 0.0), -1, keepdims=True)


def forward_kernel(nz, n, own_e, hid, slice_d, seq, quarter, places, idx, *refs):
    mask_ref, router_ref = refs[:2]
    gate_parts, up_parts, m_refs = refs[2:4], refs[4:6], refs[6:-11]
    act_ref, up_ref, hid_ref, probs_ref, m_out, w_gate, w_up, m_full, *sems = refs[-11:]
    gate_sems, up_sems, m_sems = sems
    me_z, me_t = idx[0], idx[2]
    step = pl.program_id(0)
    first = step == 0
    m_copies = [
        [
            pltpu.make_async_copy(
                m_refs[j].at[pl.ds(row, seq), :],
                m_full.at[pl.ds(i * seq, seq), pl.ds(k * quarter, quarter)],
                m_sems.at[i, k],
            )
            for k, (j, row) in enumerate(places[i])
        ]
        for i in range(nz)
    ]
    gate_copies = weight_copies(nz, slice_d, own_e, idx, gate_parts, w_gate, gate_sems, False)
    up_copies = weight_copies(nz, slice_d, own_e, idx, up_parts, w_up, up_sems, False)

    @pl.when(first)
    def _():
        start(m_copies[0] + gate_copies + up_copies)
        for copies in m_copies[1:]:
            start(copies)

    for i in range(nz):

        @pl.when(step == i)
        def _(i=i):
            finish(m_copies[i])

    rows = seq
    m_block = m_full[pl.ds(pl.multiple_of(step * seq, seq), seq), :]
    m_out[...] = m_block
    lane = lax.broadcasted_iota(jnp.int32, (rows, LANES), 1)
    logits = jnp.zeros((rows, LANES), f32)
    for k in range(n):
        logits += dot_nn(m_block[:, k * quarter : (k + 1) * quarter], router_ref[me_t ^ k])
    named = (lane >= FIRST) & (lane < FIRST + EXPERTS)
    logits = jnp.where(named, logits, -1e30)
    expd = jnp.where(named, jnp.exp(logits - jnp.max(logits, -1, keepdims=True)), 0.0)
    probs = expd / jnp.sum(expd, -1, keepdims=True)
    probs_ref[...] = probs
    gates = probs * mask_ref[...]

    @pl.when(first)
    def _():
        finish(gate_copies)

    for e in range(own_e):
        at = pl.ds(e * hid, hid)
        act_ref[:, at] = dot_nn(m_block, w_gate[:, at])

    @pl.when(first)
    def _():
        finish(up_copies)

    for e in range(own_e):
        at = pl.ds(e * hid, hid)
        up = dot_nn(m_block, w_up[:, at])
        up_ref[:, at] = up
        act = act_ref[:, at]
        gate = own_gate(gates, lane, me_z, own_e, e)
        hid_ref[:, at] = (gate * (act * jax.nn.sigmoid(act) * up)).astype(bf16)


def forward_call(idx, pieces, places, mask_all, router_q, gate_parts, up_parts, nz):
    n, quarter = router_q.shape[:2]
    tokens = mask_all.shape[0]
    seq = tokens // nz
    own_e, slice_d, hid = up_parts[0].shape[1:]
    wide = own_e * hid
    here = lambda i, idx: (i, 0)
    return pl.pallas_call(
        functools.partial(forward_kernel, nz, n, own_e, hid, slice_d, seq, quarter, places),
        grid_spec=pltpu.PrefetchScalarGridSpec(
            num_scalar_prefetch=1,
            grid=(nz,),
            in_specs=[
                pl.BlockSpec((seq, LANES), here),
                pl.BlockSpec((n, quarter, LANES), lambda i, idx: (0, 0, 0)),
            ]
            + [pl.BlockSpec(memory_space=pl.ANY)] * (4 + len(pieces)),
            out_specs=[
                pl.BlockSpec((seq, wide), here),
                pl.BlockSpec((seq, wide), here),
                pl.BlockSpec((seq, wide), here),
                pl.BlockSpec((seq, LANES), here),
                pl.BlockSpec((seq, n * quarter), here),
            ],
            scratch_shapes=[
                pltpu.VMEM((n * quarter, wide), bf16),
                pltpu.VMEM((n * quarter, wide), bf16),
                pltpu.VMEM((tokens, n * quarter), bf16),
                pltpu.SemaphoreType.DMA((2 * nz * own_e,)),
                pltpu.SemaphoreType.DMA((2 * nz * own_e,)),
                pltpu.SemaphoreType.DMA((nz, n)),
            ],
        ),
        out_shape=[
            jax.ShapeDtypeStruct((tokens, wide), f32),
            jax.ShapeDtypeStruct((tokens, wide), f32),
            jax.ShapeDtypeStruct((tokens, wide), bf16),
            jax.ShapeDtypeStruct((tokens, LANES), f32),
            jax.ShapeDtypeStruct((tokens, n * quarter), bf16),
        ],
        compiler_params=pltpu.CompilerParams(vmem_limit_bytes=56 * MIB),
        cost_estimate=pl.CostEstimate(
            flops=4 * tokens * n * quarter * wide, bytes_accessed=40 * MIB, transcendentals=0
        ),
    )(idx, mask_all, router_q, *gate_parts, *up_parts, *pieces)


def backward_kernel(nz, n, own_e, hid, slice_d, quarter, idx, *refs):
    g_ref, act_ref, up_ref, probs_ref, mask_ref = refs[:5]
    dx_ref, dg_ref, du_ref, w_gate, w_up, w_down, gate_sems, up_sems, down_sems = refs[11:]
    i = pl.program_id(0)
    me_z = idx[0]
    gate_copies = weight_copies(nz, slice_d, own_e, idx, refs[5:7], w_gate, gate_sems, False)
    up_copies = weight_copies(nz, slice_d, own_e, idx, refs[7:9], w_up, up_sems, False)
    down_copies = weight_copies(nz, slice_d, own_e, idx, refs[9:11], w_down, down_sems, True)

    @pl.when(i == 0)
    def _():
        start(down_copies + gate_copies + up_copies)
        finish(down_copies)

    rows = act_ref.shape[0]
    lane = lax.broadcasted_iota(jnp.int32, (rows, LANES), 1)
    gates = probs_ref[...] * mask_ref[...]
    dgate = jnp.zeros((rows, LANES), f32)
    g_block = jnp.concatenate([g_ref[q, 0] for q in range(n)], 1)
    for e in range(own_e):
        gate = own_gate(gates, lane, me_z, own_e, e)
        at = pl.ds(e * hid, hid)
        back = dot_nt(g_block, w_down[e])
        act = act_ref[:, at]
        up = up_ref[:, at]
        sigma = jax.nn.sigmoid(act)
        silu = act * sigma
        dgate = jnp.where(
            lane == me_z * own_e + e, jnp.sum(silu * up * back, -1, keepdims=True), dgate
        )
        back = gate * back
        dg_ref[:, at] = (back * up * sigma * (1.0 + act * (1.0 - sigma))).astype(bf16)
        du_ref[:, at] = (back * silu).astype(bf16)
    dgate = jnp.transpose(dgate)[:EXPERTS].astype(bf16)

    @pl.when(i == 0)
    def _():
        finish(gate_copies + up_copies)

    even, odd = order_of(n, 0), order_of(n, 1)
    for j in range(n):
        k = jnp.where(i % 2 == 0, even[j], odd[j])
        at = pl.ds(pl.multiple_of(k * quarter, quarter), quarter)
        total = dot_nt(dg_ref[...], w_gate[at, :]) + dot_nt(du_ref[...], w_up[at, :])
        dx_ref[0, j, pl.ds(0, rows), :] = total.astype(bf16)
        for h in range(rows // quarter):
            dx_ref[0, j, pl.ds(rows + h * EXPERTS, EXPERTS), :] = dgate[
                :, h * quarter : (h + 1) * quarter
            ]


def backward_call(idx, first, g_all, act, up, probs, mask_all, weights):
    n, nz, seq, quarter = g_all.shape
    own_e, slice_d, hid = weights[0].shape[1:]
    blocks = nz // 2
    wide = own_e * hid
    tall = seq + EXPERTS * (seq // quarter)
    some = lambda i, idx: (2 * i + first, 0)
    here = lambda i, idx: (i, 0)
    hbm = pl.BlockSpec(memory_space=pl.ANY)
    return pl.pallas_call(
        functools.partial(backward_kernel, nz, n, own_e, hid, slice_d, quarter),
        grid_spec=pltpu.PrefetchScalarGridSpec(
            num_scalar_prefetch=1,
            grid=(blocks,),
            in_specs=[
                pl.BlockSpec((n, 1, seq, quarter), lambda i, idx: (0, 2 * i + first, 0, 0)),
                pl.BlockSpec((seq, wide), some),
                pl.BlockSpec((seq, wide), some),
                pl.BlockSpec((seq, LANES), some),
                pl.BlockSpec((seq, LANES), some),
            ]
            + [hbm] * 6,
            out_specs=[
                pl.BlockSpec((1, n, tall, quarter), lambda i, idx: (i, 0, 0, 0)),
                pl.BlockSpec((seq, wide), here),
                pl.BlockSpec((seq, wide), here),
            ],
            scratch_shapes=[
                pltpu.VMEM((n * quarter, wide), bf16),
                pltpu.VMEM((n * quarter, wide), bf16),
                pltpu.VMEM((own_e, hid, n * quarter), bf16),
                pltpu.SemaphoreType.DMA((2 * nz * own_e,)),
                pltpu.SemaphoreType.DMA((2 * nz * own_e,)),
                pltpu.SemaphoreType.DMA((2 * nz,)),
            ],
        ),
        out_shape=[
            jax.ShapeDtypeStruct((blocks, n, tall, quarter), bf16),
            jax.ShapeDtypeStruct((blocks * seq, wide), bf16),
            jax.ShapeDtypeStruct((blocks * seq, wide), bf16),
        ],
        compiler_params=pltpu.CompilerParams(vmem_limit_bytes=56 * MIB),
        cost_estimate=pl.CostEstimate(
            flops=6 * blocks * seq * n * quarter * wide,
            bytes_accessed=40 * MIB,
            transcendentals=0,
        ),
    )(idx, g_all, act, up, probs, mask_all, *weights)


def output_kernel(nz, own_e, hid, slice_d, quarter, idx, hid_ref, near, far, y_ref, w_down, sems):
    i, j = pl.program_id(0), pl.program_id(1)

    @pl.when((i == 0) & (j == 0))
    def _():
        copies = weight_copies(nz, slice_d, own_e, idx, (near, far), w_down, sems, True)
        start(copies)
        finish(copies)

    at = pl.ds(pl.multiple_of(j * quarter, quarter), quarter)
    part = w_down[:, :, at].reshape(own_e * hid, quarter)
    y_ref[0, 0] = dot_nn(hid_ref[...], part).astype(bf16)


def output_call(idx, hidden, parts, n, nz):
    tokens, wide = hidden.shape
    seq = tokens // nz
    own_e, hid, slice_d = parts[0].shape[1:]
    quarter = 2 * slice_d
    return pl.pallas_call(
        functools.partial(output_kernel, nz, own_e, hid, slice_d, quarter),
        grid_spec=pltpu.PrefetchScalarGridSpec(
            num_scalar_prefetch=1,
            grid=(nz, n),
            in_specs=[pl.BlockSpec((seq, wide), lambda i, j, idx: (i, 0))]
            + [pl.BlockSpec(memory_space=pl.ANY)] * 2,
            out_specs=pl.BlockSpec(
                (1, 1, seq, quarter), lambda i, j, idx: (j ^ idx[2], i ^ idx[0], 0, 0)
            ),
            scratch_shapes=[
                pltpu.VMEM((own_e, hid, n * quarter), bf16),
                pltpu.SemaphoreType.DMA((2 * nz,)),
            ],
        ),
        out_shape=jax.ShapeDtypeStruct((n, nz, seq, quarter), bf16),
        compiler_params=pltpu.CompilerParams(vmem_limit_bytes=48 * MIB),
        cost_estimate=pl.CostEstimate(
            flops=2 * tokens * n * quarter * wide, bytes_accessed=16 * MIB, transcendentals=0
        ),
    )(idx, hidden, *parts)


def down_grad_kernel(nz, n, own_e, hid, seq, slice_d, idx, hid_ref, *refs):
    g_refs, (keep_ref, give_ref, g_out, g_full, sems) = refs[:-5], refs[-5:]
    step = pl.program_id(0)
    copies = []
    for k in range(n):
        copies.append([])
        for i in range(nz):
            j, row = place_of(n, nz * seq // 2, k, i * seq)
            copies[k].append(
                pltpu.make_async_copy(
                    g_refs[j].at[pl.ds(row, seq), :],
                    g_full.at[k, pl.ds(i * seq, seq), :],
                    sems.at[k, i],
                )
            )

    @pl.when(step == 0)
    def _():
        for some in copies:
            start(some)

    for k in range(n):

        @pl.when(step == k)
        def _(k=k):
            finish(copies[k])

    g_block = g_full[step]
    g_out[0] = g_block
    total = dot_tn(g_block, hid_ref[...])
    halves = (total[:slice_d], total[slice_d:])
    for e in range(own_e):
        parts = [jnp.transpose(half[:, e * hid : (e + 1) * hid]).astype(bf16) for half in halves]
        keep_ref[0, e] = jnp.where(idx[1] == 0, parts[0], parts[1])
        give_ref[0, e] = jnp.where(idx[1] == 0, parts[1], parts[0])


def down_grad_call(idx, pieces, hidden, own_e, nz, n):
    tokens, wide = hidden.shape
    quarter, seq = pieces[0].shape[1], tokens // nz
    hid, slice_d = wide // own_e, quarter // 2
    out = pl.BlockSpec((1, own_e, hid, slice_d), lambda k, idx: (k ^ idx[2] ^ idx[0], 0, 0, 0))
    return pl.pallas_call(
        functools.partial(down_grad_kernel, nz, n, own_e, hid, seq, slice_d),
        grid_spec=pltpu.PrefetchScalarGridSpec(
            num_scalar_prefetch=1,
            grid=(n,),
            in_specs=[pl.BlockSpec((tokens, wide), lambda k, idx: (0, 0))]
            + [pl.BlockSpec(memory_space=pl.ANY)] * len(pieces),
            out_specs=[out, out, pl.BlockSpec((1, tokens, quarter), lambda k, idx: (k, 0, 0))],
            scratch_shapes=[
                pltpu.VMEM((n, tokens, quarter), bf16),
                pltpu.SemaphoreType.DMA((n, nz)),
            ],
        ),
        out_shape=[jax.ShapeDtypeStruct((nz, own_e, hid, slice_d), bf16)] * 2
        + [jax.ShapeDtypeStruct((n, tokens, quarter), bf16)],
        compiler_params=pltpu.CompilerParams(vmem_limit_bytes=48 * MIB),
        cost_estimate=pl.CostEstimate(
            flops=2 * tokens * n * quarter * wide, bytes_accessed=24 * MIB, transcendentals=0
        ),
    )(idx, hidden, *pieces)


def up_grad_kernel(nz, own_e, hid, seq, slice_d, idx, m_ref, *refs):
    rights, (keep_ref, give_ref) = refs[:4], refs[4:]
    lefts = [
        jnp.concatenate([m_ref[pl.ds(blk * seq, seq), :] for blk in range(odd, nz, 2)], 0)
        for odd in (0, 1)
    ]
    for w in range(2):
        for e in range(own_e):
            at = pl.ds(e * hid, hid)
            total = dot_tn(lefts[0], rights[2 * w][:, at]) + dot_tn(
                lefts[1], rights[2 * w + 1][:, at]
            )
            parts = (total[:slice_d].astype(bf16), total[slice_d:].astype(bf16))
            keep_ref[0, w, e] = jnp.where(idx[1] == 0, parts[0], parts[1])
            give_ref[0, w, e] = jnp.where(idx[1] == 0, parts[1], parts[0])


def up_grad_call(idx, m_all, early, late, own_e, nz, n):
    tokens, quarter = m_all.shape[0], m_all.shape[1] // n
    seq = tokens // nz
    wide = early[0].shape[1]
    hid, slice_d = wide // own_e, quarter // 2
    full = pl.BlockSpec(early[0].shape, lambda k, idx: (0, 0))
    out = pl.BlockSpec(
        (1, 2, own_e, slice_d, hid), lambda k, idx: (k ^ idx[2] ^ idx[0], 0, 0, 0, 0)
    )
    return pl.pallas_call(
        functools.partial(up_grad_kernel, nz, own_e, hid, seq, slice_d),
        grid_spec=pltpu.PrefetchScalarGridSpec(
            num_scalar_prefetch=1,
            grid=(n,),
            in_specs=[pl.BlockSpec((tokens, quarter), lambda k, idx: (0, k))] + [full] * 4,
            out_specs=[out, out],
        ),
        out_shape=[jax.ShapeDtypeStruct((nz, 2, own_e, slice_d, hid), bf16)] * 2,
        compiler_params=pltpu.CompilerParams(vmem_limit_bytes=48 * MIB),
        cost_estimate=pl.CostEstimate(
            flops=4 * tokens * n * quarter * wide, bytes_accessed=24 * MIB, transcendentals=0
        ),
    )(idx, m_all, early[0], late[0], early[1], late[1])


def place_kernel(nz, idx, *refs):
    ups, downs, outs = refs[:nz], refs[nz : 2 * nz], refs[2 * nz :]
    for i in range(nz):

        @pl.when(pl.program_id(0) == i)
        def _(i=i):
            outs[0][...] = ups[i][0].astype(f32)
            outs[1][...] = ups[i][1].astype(f32)
            outs[2][...] = downs[i][...].astype(f32)


def place_call(idx, ups, downs):
    nz = len(ups)
    flat = list(ups) + list(downs)
    fixed = lambda rank: lambda k, idx: (0,) * rank
    shapes = [ups[0].shape[1:], ups[0].shape[1:], downs[0].shape]
    return pl.pallas_call(
        functools.partial(place_kernel, nz),
        grid_spec=pltpu.PrefetchScalarGridSpec(
            num_scalar_prefetch=1,
            grid=(nz,),
            in_specs=[pl.BlockSpec(part.shape, fixed(part.ndim)) for part in flat],
            out_specs=[
                pl.BlockSpec(shape, lambda k, idx: (k ^ idx[0], 0, 0)) for shape in shapes
            ],
        ),
        out_shape=[jax.ShapeDtypeStruct((EXPERTS,) + shape[1:], f32) for shape in shapes],
        compiler_params=pltpu.CompilerParams(vmem_limit_bytes=48 * MIB),
        cost_estimate=pl.CostEstimate(flops=0, bytes_accessed=20 * MIB, transcendentals=0),
    )(idx, *flat)


def shards(
    tokens,
    cotangent,
    routes,
    wq,
    wk,
    wv,
    wo,
    attn_gain,
    q_gain,
    k_gain,
    moe_gain,
    router,
    w_gate,
    w_up,
    w_down,
):
    nz = lax.axis_size("z")
    me_t = lax.axis_index("tensor")
    me_z = lax.axis_index("z")
    me_c = lax.axis_index("core")
    dp = ("z", "core")
    seq, width = tokens.shape
    quarter = width // lax.axis_size("tensor")
    local = wq.shape[1]
    local_heads = local // HEAD_DIM
    slice_d = wq.shape[0]
    own_e = EXPERTS // nz
    hid = w_gate.shape[2]

    idx = jnp.stack([me_z, me_c, me_t]).astype(jnp.int32)

    small = jnp.concatenate([attn_gain[:, None], moe_gain[:, None], router], 1)
    small = jnp.pad(small, ((0, 0), (0, LANES - small.shape[1])))
    packed = lax.all_gather(jnp.concatenate([wq, wk, wv, small], 1), dp, axis=0, tiled=True)
    mask = jnp.sum(
        (routes[:, :, None] == jnp.arange(EXPERTS)[None, None, :]).astype(bf16), 1
    )
    n = width // quarter
    packed, *mask_parts = fence(packed, *spread_z(mask.T))
    mask_all = jnp.stack(mask_parts).transpose(0, 2, 1)
    mask_all = jnp.pad(
        mask_all.reshape(nz * seq, EXPERTS).astype(f32),
        ((0, 0), (FIRST, LANES - EXPERTS - FIRST)),
    )
    wqkv_full = packed[:, : 3 * local]
    small_full = packed[:, 3 * local :]
    a_gain = small_full[:, 0].astype(f32)
    m_gain = small_full[:, 1].astype(f32)
    router_full = small_full[:, FIRST : FIRST + EXPERTS]
    wo_full = lax.all_gather(after(wo, packed), dp, axis=1, tiled=True)

    def fetch(weight, ks):
        pick = lambda k: lax.dynamic_slice_in_dim(weight, (me_z ^ k) * own_e, own_e, 0)
        return [swap(pick(k), "z", k) for k in ks]

    def both_cores(parts):
        parts = jnp.stack(parts)
        return [parts, swap(parts, "core", 1)]

    most, last = range(nz - 1), range(nz - 1, nz)
    cot_parts = spread_z(after(columns(cotangent, me_t, quarter), packed))

    xf = tokens.astype(f32)
    rate_x = lax.rsqrt(jnp.mean(xf * xf, -1, keepdims=True) + EPS)
    gain_q = q_gain.astype(f32)
    gain_k = k_gain.astype(f32)
    a_low = (xf * rate_x * a_gain).astype(bf16)
    qkv = jnp.dot(a_low, wqkv_full, preferred_element_type=f32)
    query, keyed, valued = qkv[:, :local], qkv[:, local : 2 * local], qkv[:, 2 * local :]
    sums = tensor_sum(jnp.stack([jnp.sum(query * query, -1), jnp.sum(keyed * keyed, -1)]))
    rate_q = lax.rsqrt(sums[0] / width + EPS)[:, None]
    rate_k = lax.rsqrt(sums[1] / width + EPS)[:, None]
    cosine, sine = rope_tables(seq, HEAD_DIM)
    heads = (seq, local_heads, HEAD_DIM)
    q_rot = rotate((query * rate_q * gain_q).reshape(heads), cosine, sine).astype(bf16)
    k_rot = rotate((keyed * rate_k * gain_k).reshape(heads), cosine, sine).astype(bf16)
    v_low = valued.reshape(heads).astype(bf16)
    scale = HEAD_DIM ** (-0.5)
    scores = scale * jnp.einsum("qhd,khd->hqk", q_rot, k_rot, preferred_element_type=f32)
    causal = jnp.arange(seq)[:, None] >= jnp.arange(seq)[None, :]
    scores = jnp.where(causal[None], scores, -1e30)
    peak = jnp.max(scores, -1, keepdims=True)
    expd = jnp.exp(scores - peak)
    weights = expd / jnp.sum(expd, -1, keepdims=True)
    weights_low = weights.astype(bf16)
    outputs = jnp.einsum("hqk,khd->qhd", weights_low, v_low, preferred_element_type=f32)
    joined = outputs.reshape(seq, local).astype(bf16)
    wo_full = after(wo_full, joined)
    attn = jnp.dot(joined, wo_full, preferred_element_type=f32).astype(bf16)
    attn, *cot_parts[:-1] = fence(attn, *cot_parts[:-1])
    gate_parts = fetch(after(w_gate, attn), most)

    x_own = columns(xf, me_t, quarter)
    blocks = columns_blocks(attn)
    got = [scatter_first(block, odd) for odd, block in enumerate(blocks)]
    resid = x_own + jnp.concatenate(
        [scatter_third(*scatter_second(b, g, odd)) for odd, (b, g) in enumerate(zip(blocks, got))],
        0,
    )
    rate_r = lax.rsqrt(tensor_sum(jnp.sum(resid * resid, -1)) / width + EPS)[:, None]
    gain_own = lax.dynamic_slice_in_dim(m_gain, me_t * quarter, quarter, 0)
    m_own = (resid * rate_r * gain_own).astype(bf16)

    held = fence(m_own, *gate_parts, *cot_parts)
    m_own, gate_parts, cot_parts = held[0], held[1:nz], held[nz:]
    cot_flat = jnp.concatenate(cot_parts, 0)
    cot_near = spread_tensor_near(cot_flat)
    held = fence(*spread_z(m_own), *cot_near)
    m_parts, cot_near = held[:nz], held[nz:]
    gate_parts += fetch(after(w_gate, m_parts[0]), last)
    up_parts = fetch(after(w_up, m_parts[0]), most)
    m_flat = jnp.concatenate(m_parts, 0)
    m_near = spread_tensor_near(m_flat)
    held = fence(gate_parts[-1], *up_parts, *m_near)
    gate_parts[-1], up_parts, m_near = held[0], held[1:nz], held[nz:]
    gate_parts = both_cores(gate_parts)
    up_parts += fetch(after(w_up, m_near[0]), last)
    held = fence(m_flat, *m_near, *spread_tensor_cross(m_near), up_parts[-1])
    up_parts[-1], pieces = held[-1], held[:-1]
    up_parts = both_cores(up_parts)
    down_parts = fetch(after(w_down, up_parts[0]), range(nz))
    cot_cross = spread_tensor_cross([after(x, pieces[-1]) for x in cot_near])
    places = [
        [place_of(n, nz * seq // 2, k, i * seq) for k in range(n)] for i in range(nz)
    ]
    router_q = small_full.reshape(-1, quarter, LANES)
    act, up, hidden, probs_all, m_all = forward_call(
        idx, pieces, places, mask_all, router_q, gate_parts, up_parts, nz
    )
    hidden, *cot_cross = fence(hidden, *cot_cross)
    down_keep, down_give, cot_all = down_grad_call(
        idx, [cot_flat, *cot_near, *cot_cross], hidden, own_e, nz, n
    )
    cot_all = cot_all.reshape(n, nz, seq, quarter)

    def to_owners(keep, got):
        summed = (keep.astype(f32) + got.astype(f32)).astype(bf16)
        return [swap(summed[k], "z", k) for k in range(nz)]

    down_give, *down_parts = fence(down_give, *down_parts)
    down_parts = both_cores(down_parts)
    down_got = swap(down_give, "core", 1)
    half_call = lambda first, probs: backward_call(
        idx, first, cot_all, act, up, probs, mask_all, gate_parts + up_parts + down_parts
    )
    odds, evens = range(1, nz, 2), range(0, nz, 2)
    late = half_call(1, after(probs_all, down_give))
    first = {k: scatter_first(late[0][k // 2], k // 2 % 2) for k in odds}
    down_own = to_owners(after(down_keep, late[1]), down_got)
    early = half_call(0, after(probs_all, late[1], down_own[0]))
    held = fence(*early, *down_own[:-1], *(first[k] for k in odds))
    early, down_own[:-1] = held[:3], held[3 : 2 + nz]
    got = dict(zip(odds, held[2 + nz :]))
    second = {k: scatter_second(late[0][k // 2], got[k], k // 2 % 2) for k in odds}
    first = {k: scatter_first(early[0][k // 2], k // 2 % 2) for k in evens}
    up_keep, up_give = up_grad_call(idx, m_all, early[1:3], late[1:3], own_e, nz, n)
    few = [second[k] for k in odds if second[k][1] is not None]
    held = fence(
        up_keep,
        up_give,
        down_own[-1],
        *(first[k] for k in evens),
        *(x[1] for x in few),
    )
    (up_keep, up_give, down_own[-1]), got = held[:3], dict(zip(evens, held[3:]))
    if few:
        second = {k: (second[k][0], x) for k, x in zip(odds, held[3 + nz // 2 :])}
    near = scatter_z_near({k: scatter_third(*second[k]) for k in odds})
    second = {k: scatter_second(early[0][k // 2], got[k], k // 2 % 2) for k in evens}
    up_got = swap(up_give, "core", 1)
    moe_part = output_call(idx, after(hidden, up_give), down_parts, n, nz)
    few = [second[k][1] for k in evens if second[k][1] is not None]
    near, moe_part, *few = fence(near, moe_part, *few)
    if few:
        second = {k: (second[k][0], x) for k, x in zip(evens, few)}
    dm_own = scatter_z_far({k: scatter_third(*second[k]) for k in evens}, near)
    dgate = jnp.concatenate(
        [dm_own[seq + h * EXPERTS :][:EXPERTS] for h in range(seq // quarter)], 1
    )
    dm_own, up_got = fence(dm_own[:seq], up_got)
    summed = (up_keep.astype(f32) + up_got.astype(f32)).astype(bf16)
    up_own = [swap(summed[k], "z", k) for k in range(nz - 1)] + [None]
    up_last = summed[nz - 1]
    moe_sum = lax.psum_scatter(moe_part, "tensor", scatter_dimension=0, tiled=False)

    dgate = dgate.T
    probs = probs_all[:seq, FIRST : FIRST + EXPERTS]
    dprobs = dgate * mask.astype(f32)
    dlogits = probs * (dprobs - jnp.sum(probs * dprobs, -1, keepdims=True))
    router_own = lax.dynamic_slice_in_dim(router_full, me_t * quarter, quarter, 0)
    router_part = jnp.dot(m_own.astype(f32).T, dlogits, precision=HIGH)
    dm_own = dm_own + jnp.dot(dlogits, router_own.astype(f32).T, precision=HIGH)

    normed = resid * rate_r
    moe_gain_part = jnp.sum(dm_own * normed, 0)
    pulled = dm_own * gain_own
    inner_r = tensor_sum(jnp.sum(pulled * normed, -1))[:, None] / width
    cot_own = columns(cotangent, me_t, quarter).astype(f32)
    dresid = cot_own + rate_r * (pulled - normed * inner_r)
    dresid_low = gather_tensor(dresid.astype(bf16))
    dresid_low, *up_own[:-1] = fence(dresid_low, *up_own[:-1])
    up_own[-1] = swap(after(up_last, dresid_low), "z", nz - 1)
    moe_sum = after(moe_sum, dresid_low)
    moe_parts = {
        k: lax.dynamic_index_in_dim(moe_sum, me_z ^ k, 0, keepdims=False) for k in range(nz)
    }
    moe_near = scatter_z_near({k: moe_parts[k] for k in range(1, nz, 2)})

    wo_grad = jnp.einsum("sa,sd->ad", joined, dresid_low, preferred_element_type=f32)
    dout = (
        jnp.einsum("sd,ad->sa", dresid_low, wo_full, preferred_element_type=f32)
        .astype(bf16)
        .reshape(heads)
    )
    dweights = jnp.einsum("qhd,khd->hqk", dout, v_low, preferred_element_type=f32)
    dv = jnp.einsum("hqk,qhd->khd", weights_low, dout, preferred_element_type=f32)
    inner = jnp.sum(weights * dweights, -1, keepdims=True)
    dscores = (weights * (dweights - inner)).astype(bf16)
    dscores, up_own[-1], moe_near = fence(dscores, up_own[-1], moe_near)
    wo_grad = after(wo_grad.astype(bf16), dscores)
    wo_own = lax.psum_scatter(wo_grad, dp, scatter_dimension=1, tiled=True)
    dq_rot = scale * jnp.einsum("hqk,khd->qhd", dscores, k_rot, preferred_element_type=f32)
    dk_rot = scale * jnp.einsum("hqk,qhd->khd", dscores, q_rot, preferred_element_type=f32)
    dq_norm = unrotate(dq_rot, cosine, sine).reshape(seq, local)
    dk_norm = unrotate(dk_rot, cosine, sine).reshape(seq, local)
    inners = tensor_sum(
        jnp.stack(
            [jnp.sum(dq_norm * gain_q * query, -1), jnp.sum(dk_norm * gain_k * keyed, -1)]
        )
    )
    dq_low = (rate_q * gain_q * dq_norm - query * rate_q**3 * inners[0][:, None] / width).astype(
        bf16
    )
    dk_low = (rate_k * gain_k * dk_norm - keyed * rate_k**3 * inners[1][:, None] / width).astype(
        bf16
    )
    dv_low = dv.reshape(seq, local).astype(bf16)
    q_gain_part = jnp.sum(dq_norm * query * rate_q, 0)
    k_gain_part = jnp.sum(dk_norm * keyed * rate_k, 0)
    dqkv = jnp.concatenate([dq_low, dk_low, dv_low], 1)
    smalls = jnp.concatenate(
        [q_gain_part[None], k_gain_part[None], moe_gain_part[None], router_part.T], 0
    )
    moe_own = scatter_z_far({k: moe_parts[k].astype(f32) for k in range(0, nz, 2)}, moe_near)
    dqkv, moe_own, smalls = fence(dqkv, moe_own, butterfly_sum(smalls, ("core", "z")))
    half = lax.dynamic_slice_in_dim(smalls[2:], me_c * slice_d, slice_d, 1)
    half = tensor_sum(jnp.where(me_t == me_z, half, 0.0))
    mixed = gather_tensor((resid + moe_own).astype(bf16))
    wqkv_grad = jnp.einsum("sd,sa->da", a_low, dqkv, preferred_element_type=f32).astype(bf16)
    da_part = jnp.einsum("sa,da->sd", dqkv, wqkv_full, preferred_element_type=f32)
    blocks = columns_blocks(da_part.astype(bf16))
    got = [scatter_first(b, odd) for odd, b in enumerate(blocks)]
    expert_grads = place_call(idx, up_own, down_own)
    da_own = jnp.concatenate(
        [scatter_third(*scatter_second(b, g, odd)) for odd, (b, g) in enumerate(zip(blocks, got))],
        0,
    )
    da_own, mixed = fence(da_own, mixed)
    norm_x = x_own * rate_x
    pulled_x = da_own * lax.dynamic_slice_in_dim(a_gain, me_t * quarter, quarter, 0)
    inner_x = tensor_sum(jnp.sum(pulled_x * norm_x, -1))[:, None] / width
    tokens_grad = gather_tensor(
        (dresid + rate_x * (pulled_x - norm_x * inner_x)).astype(bf16)
    )

    wqkv_grad, wo_own = fence(wqkv_grad, wo_own)
    wqkv_own = lax.psum_scatter(wqkv_grad, dp, scatter_dimension=0, tiled=True)
    tokens_grad, wqkv_own = fence(tokens_grad, wqkv_own)
    wqkv_own, wo_own = wqkv_own.astype(f32), wo_own.astype(f32)
    attn_gain_grad = jnp.sum(jnp.concatenate([wq, wk, wv], 1).astype(f32) * wqkv_own, -1)
    attn_gain_grad = tensor_sum(attn_gain_grad) / attn_gain.astype(f32)
    return (
        mixed,
        tokens_grad,
        wqkv_own[:, :local],
        wqkv_own[:, local : 2 * local],
        wqkv_own[:, 2 * local : 3 * local],
        wo_own,
        attn_gain_grad,
        smalls[0],
        smalls[1],
        half[0],
        half[1:].T,
        expert_grads[0],
        expert_grads[1],
        expert_grads[2],
    )


def solution(mesh):
    fine = Mesh(
        mesh.devices.reshape(mesh.shape["dp"] // 2, 2, mesh.shape["tensor"]),
        ("z", "core", "tensor"),
    )
    dp = ("z", "core")
    in_specs = (
        P(dp, None),
        P(dp, None),
        P(dp, None),
        P(dp, "tensor"),
        P(dp, "tensor"),
        P(dp, "tensor"),
        P("tensor", dp),
        P(dp),
        P("tensor"),
        P("tensor"),
        P(dp),
        P(dp, None),
        P(None, dp, "tensor"),
        P(None, dp, "tensor"),
        P(None, "tensor", dp),
    )
    out_specs = (
        P(dp, None),
        P(dp, None),
        P(dp, "tensor"),
        P(dp, "tensor"),
        P(dp, "tensor"),
        P("tensor", dp),
        P(dp),
        P("tensor"),
        P("tensor"),
        P(dp),
        P(dp, None),
        P(None, dp, "tensor"),
        P(None, dp, "tensor"),
        P(None, "tensor", dp),
    )
    return jax.shard_map(shards, mesh=fine, in_specs=in_specs, out_specs=out_specs, check_vma=False)
```
